128 devices in a mesh: lev: 8 (over y_lo, x), tile: 16 (over z, y_hi, core).
Axes of the slice: x: 4, y: 4 (y_hi: 2, y_lo: 2; y = y_hi * 2 + y_lo), z: 4, core: 2. Of those that a mesh axis runs over, the one named last changes fastest.
Arguments:
- inputs: bfloat16 [8, 80, 512, 128], P('lev', None, 'tile'), may hold values from -6 to 6
- level_ids: int32 [8], replicated, may hold values from 0 to 12
- level_table: bfloat16 [13, 512], replicated, may hold values from -6 to 6
- w_embed: bfloat16 [80, 512], replicated, may hold values from -0.625 to 0.625
- queries: bfloat16 [3, 512], replicated, may hold values from -6 to 6
- w_kv: bfloat16 [512, 1024], replicated, may hold values from -0.25 to 0.25
- w_out: bfloat16 [512, 512], replicated, may hold values from -0.25 to 0.25
- gain: float32 [512], replicated, may hold values from 0.1 to 1.9
- w_qkv: bfloat16 [512, 1536], replicated, may hold values from -0.25 to 0.25
- w_proj: bfloat16 [512, 512], replicated, may hold values from -0.25 to 0.25
- d_latent: bfloat16 [512, 128, 3, 512], P('tile', 'lev'), may hold values from -6 to 6
Outputs:
- swin_out: bfloat16 [512, 128, 3, 512], P('tile', 'lev')
- grad_embed: float32 [80, 512], replicated
- grad_keyval: float32 [512, 1024], replicated
- grad_out: float32 [512, 512], replicated
The draws below stay inside these ranges and needn't reach their ends.
All inputs are finite; a program needn't handle non-finite values.
Results may differ from the reference program's by a relative error of at most 0.015.
Values may be sent and summed in bfloat16 or wider, within the bound.
A program may use at most 192 MiB of HBM per device.

```python
import math
import jax
import jax.numpy as jnp
from jax import lax

D = 512
F = 80
HD = 64
HEADS = 8
LATENT = 3
PLEVELS = 13
WIN = 8
LON_DEV = 32
LEVELS = 8
LAT = 128
LON = 512
N_TILE = 16


def touch_ends(drawn, rng, low, top_value):
    extent = drawn.shape
    place = [jax.random.randint(jax.random.fold_in(rng, axis), (), 0, extent[axis]) for axis in range(len(extent))]
    drawn = drawn.at[tuple(place)].set(low)
    longest = extent.index(max(extent))
    place[longest] = (place[longest] + 1) % extent[longest]
    return drawn.at[tuple(place)].set(top_value)


def block_levels(rng, dims, cuts, least, largest):
    level = 1.0
    for axis_at, blocks in cuts:
        draws = jax.random.uniform(jax.random.fold_in(jax.random.fold_in(rng, 6), axis_at), (blocks,), jnp.float32, least / len(cuts), largest / len(cuts))
        level = level * jnp.repeat(jnp.exp(draws), dims[axis_at] // blocks).reshape((-1,) + (1,) * (len(dims) - 1 - axis_at))
    return level


def gaussian(stream_key, dims, scale, bound, cuts=(), kind=jnp.bfloat16):
    drawn = scale * jax.random.normal(stream_key, dims, jnp.float32)
    if cuts:
        drawn = drawn * block_levels(stream_key, dims, cuts, -0.22, 0.18)
    return jnp.clip(drawn, -bound, bound).astype(kind)


def setup_inputs(seed: int = 0) -> dict:
    key_of = jax.random.split(jax.random.key(seed), 12)
    inputs = gaussian(key_of[0], (LEVELS, F, LON, LAT), 1.0, 6.0, ((0, 8), (2, 16)))
    level_ids = touch_ends(jax.random.randint(key_of[1], (LEVELS,), 0, PLEVELS), jax.random.fold_in(key_of[1], 1), 0, PLEVELS - 1).astype(jnp.int32)
    level_table = gaussian(key_of[2], (PLEVELS, D), 1.0, 6.0)
    w_embed = gaussian(key_of[3], (F, D), F ** -0.5, 0.625)
    queries = gaussian(key_of[4], (LATENT, D), 1.0, 6.0)
    w_kv = gaussian(key_of[5], (D, 2 * D), D ** -0.5, 0.25)
    w_out = gaussian(key_of[6], (D, D), D ** -0.5, 0.25)
    gain = jnp.clip(1.0 + 0.18 * jax.random.normal(key_of[7], (D,), jnp.float32), 0.1, 1.9)
    w_qkv = gaussian(key_of[8], (D, 3 * D), D ** -0.5, 0.25)
    w_proj = gaussian(key_of[9], (D, D), D ** -0.5, 0.25)
    d_latent = gaussian(key_of[10], (LON, LAT, LATENT, D), 1.0, 6.0, ((0, 16), (1, 8)))
    return dict(inputs=inputs, level_ids=level_ids, level_table=level_table, w_embed=w_embed, queries=queries, w_kv=w_kv, w_out=w_out, gain=gain, w_qkv=w_qkv, w_proj=w_proj, d_latent=d_latent)


def layer_norm(values, gain):
    mean = lax.optimization_barrier(jnp.mean(values, axis=-1, keepdims=True))
    centred = values - mean
    var = lax.optimization_barrier(jnp.mean(centred * centred, axis=-1, keepdims=True))
    return centred * lax.rsqrt(var + 1e-05) * gain

def window_attention(grid, row_mask, w_qkv):
    along, across, depth, width = grid.shape
    heads = width // HD
    tokens = grid.reshape(along // WIN, WIN, across // WIN, WIN, depth, width)
    tokens = tokens.transpose(0, 2, 1, 3, 4, 5).reshape(-1, WIN * WIN * depth, width)
    windows = tokens.shape[0]
    keep = jnp.broadcast_to(row_mask.reshape(1, across // WIN, 1, WIN, 1), (along // WIN, across // WIN, WIN, WIN, depth))
    keep = keep.reshape(windows, WIN * WIN * depth)
    qkv = jnp.dot(tokens.reshape(-1, width), w_qkv, preferred_element_type=jnp.float32).astype(jnp.bfloat16)
    qkv = qkv.reshape(windows, WIN * WIN * depth, 3, heads, HD).astype(jnp.float32)
    scores = jnp.einsum('wihe,wjhe->whij', qkv[:, :, 0], qkv[:, :, 1]) / math.sqrt(HD)
    expo = jnp.exp(scores) * keep[:, None, None, :]
    probs = (expo / lax.optimization_barrier(jnp.sum(expo, axis=-1, keepdims=True))).astype(jnp.bfloat16)
    attended = jnp.einsum('whij,wjhe->wihe', probs.astype(jnp.float32), qkv[:, :, 2]).astype(jnp.bfloat16)
    attended = attended.reshape(along // WIN, across // WIN, WIN, WIN, depth, width)
    return attended.transpose(0, 2, 1, 3, 4, 5).reshape(along, across, depth, width)

def reference(inputs, level_ids, level_table, w_embed, queries, w_kv, w_out, gain, w_qkv, w_proj, d_latent):
    levels = inputs.shape[0]
    blocks = inputs.reshape(levels, F, N_TILE, LON_DEV, LAT).transpose(2, 0, 1, 3, 4)
    d_blocks = d_latent.reshape(N_TILE, LON_DEV, LAT, LATENT, D)
    onehot = (level_ids[:, None] == jnp.arange(PLEVELS, dtype=jnp.int32)[None, :]).astype(jnp.float32)
    level_rows = jnp.dot(onehot, level_table.astype(jnp.float32), precision=lax.Precision.HIGHEST)
    query_heads = queries.reshape(LATENT, HEADS, HD).astype(jnp.float32)
    scale = 1.0 / math.sqrt(HD)

    def pool_block(carry, item):
        x_block, d_block = item
        count = LON_DEV * LAT
        emb = jnp.einsum('lfpa,fd->lpad', x_block.astype(jnp.float32), w_embed.astype(jnp.float32))
        emb = (emb + level_rows[:, None, None, :]).astype(jnp.bfloat16)
        emb_rows = emb.reshape(levels * count, D)
        kv = jnp.dot(emb_rows, w_kv, preferred_element_type=jnp.float32).astype(jnp.bfloat16)
        keys = kv[:, :D].reshape(levels, count, HEADS, HD).astype(jnp.float32)
        values = kv[:, D:].reshape(levels, count, HEADS, HD).astype(jnp.float32)
        scores = jnp.einsum('qhe,lmhe->mqhl', query_heads, keys) * scale
        expo = jnp.exp(scores)
        probs = (expo / lax.optimization_barrier(jnp.sum(expo, axis=-1, keepdims=True))).astype(jnp.bfloat16)
        probs_f = probs.astype(jnp.float32)
        pooled = jnp.einsum('mqhl,lmhe->mqhe', probs_f, values).astype(jnp.bfloat16).reshape(count * LATENT, D)
        latent = jnp.dot(pooled, w_out, preferred_element_type=jnp.float32).astype(jnp.bfloat16)
        d_rows = d_block.reshape(count * LATENT, D)
        dpool = jnp.dot(d_rows, w_out.T, preferred_element_type=jnp.float32).astype(jnp.bfloat16)
        dpool = dpool.reshape(count, LATENT, HEADS, HD).astype(jnp.float32)
        g_out = jnp.dot(pooled.T, d_rows, preferred_element_type=jnp.float32)
        dprob = jnp.einsum('mqhe,lmhe->mqhl', dpool, values)
        delta = lax.optimization_barrier(jnp.sum(probs_f * dprob, axis=-1, keepdims=True))
        dscore = (probs_f * (dprob - delta) * scale).astype(jnp.bfloat16).astype(jnp.float32)
        dkeys = jnp.einsum('mqhl,qhe->lmhe', dscore, query_heads).astype(jnp.bfloat16)
        dvalues = jnp.einsum('mqhl,mqhe->lmhe', probs_f, dpool).astype(jnp.bfloat16)
        dkv = jnp.concatenate([dkeys.reshape(levels * count, D), dvalues.reshape(levels * count, D)], axis=1)
        g_kv = jnp.dot(emb_rows.T, dkv, preferred_element_type=jnp.float32)
        demb = jnp.dot(dkv, w_kv.T, preferred_element_type=jnp.float32).astype(jnp.bfloat16)
        demb = demb.reshape(levels, LON_DEV, LAT, D)
        g_embed = jnp.einsum('lfpa,lpad->fd', x_block.astype(jnp.float32), demb.astype(jnp.float32))
        total = (carry[0] + g_embed, carry[1] + g_kv, carry[2] + g_out)
        return (total, latent.reshape(LON_DEV, LAT, LATENT, D))
    start = (jnp.zeros((F, D), jnp.float32), jnp.zeros((D, 2 * D), jnp.float32), jnp.zeros((D, D), jnp.float32))
    sums, latents = lax.scan(pool_block, start, (blocks, d_blocks))
    latent = latents.reshape(LON, LAT, LATENT, D)
    normed = layer_norm(latent.astype(jnp.float32), gain).astype(jnp.bfloat16)
    half = WIN // 2
    extended = jnp.pad(jnp.roll(normed, half, axis=0), ((0, 0), (half, half), (0, 0), (0, 0)))
    rows = jnp.arange(LAT + WIN, dtype=jnp.int32)
    row_mask = ((rows >= half) & (rows < LAT + half)).astype(jnp.float32)

    def one_column(index):
        column = lax.dynamic_slice_in_dim(extended, index * WIN, WIN, 0)
        return window_attention(column, row_mask, w_qkv)
    columns = lax.map(one_column, jnp.arange(LON // WIN, dtype=jnp.int32))
    attended = columns.reshape(LON, LAT + WIN, LATENT, D)[:, half:half + LAT]
    attended = jnp.roll(attended, -half, axis=0)
    projected = jnp.dot(attended.reshape(-1, D), w_proj, preferred_element_type=jnp.float32).reshape(LON, LAT, LATENT, D)
    swin_out = (latent.astype(jnp.float32) + projected).astype(jnp.bfloat16)
    factor = 1.0 / math.sqrt(LAT * LON)
    return (swin_out, sums[0] * factor, sums[1] * factor, sums[2] * factor)
```

```python
import functools
import math

import jax
import jax.numpy as jnp
import numpy as np
from jax import lax
from jax.experimental import pallas as pl
from jax.experimental.pallas import tpu as pltpu
from jax.sharding import PartitionSpec as P

HD = 64
HEADS = 8
WIN = 8
D = 512
F = 80
LEVELS = 8
LATENT = 3
KX = 128
MV = 544
CHUNK = 176
TERMS = 16 * CHUNK
BF = jnp.bfloat16
F32 = jnp.float32
VMEM_LIMIT = 56 * 1024 * 1024


def dot(a, b, ca=1, cb=0):
    return lax.dot_general(a, b, (((ca,), (cb,)), ((), ())), preferred_element_type=F32)


def split(value):
    high = value.astype(BF)
    return high, (value - high.astype(F32)).astype(BF)


def query_rows(queries):
    rows = jnp.concatenate([jnp.broadcast_to(queries[q : q + 1], (HEADS, D)) for q in range(LATENT)], axis=0)
    head = lax.broadcasted_iota(jnp.int32, (LATENT * HEADS, D), 0) % HEADS
    lane = lax.broadcasted_iota(jnp.int32, (LATENT * HEADS, D), 1) // HD
    return jnp.where(head == lane, rows, 0.0)


def weights_kernel(we_ref, queries_ref, wkv_ref, wout_ref, w2_ref, woutp_ref):
    row = lax.broadcasted_iota(jnp.int32, (D, D), 0)
    lane = lax.broadcasted_iota(jnp.int32, (D, D), 1)
    mix = jnp.where(lane == (row % HEADS) * HD + row // HEADS, 1.0, 0.0).astype(BF)
    we = we_ref[...]
    wv = dot(mix, wkv_ref[:, D:], 1, 1).astype(BF)
    woutp_ref[...] = dot(mix, wout_ref[...]).astype(BF)
    high, low = split(dot(wv, we, 1, 1))
    w2_ref[0:D, 0:KX] = high
    w2_ref[0:D, KX:] = low
    qm = query_rows(queries_ref[...].astype(F32)).astype(BF)
    shigh, slow = split(dot(qm, wkv_ref[:, :D], 1, 1) * (1.0 / math.sqrt(HD)))
    score = dot(shigh, we, 1, 1) + dot(slow, we, 1, 1)
    score = jnp.concatenate([score, jnp.zeros((MV - D - 24, KX), F32)], axis=0)
    high, low = split(score)
    w2_ref[D:MV, 0:KX] = high
    w2_ref[D:MV, KX:] = low


def level_rows(x, level):
    row = lax.broadcasted_iota(jnp.int32, (KX - F, 128), 0)
    ones = jnp.where(row == level, 1.0, 0.0).astype(BF)
    return jnp.concatenate([x, ones], axis=0)


def forward_levels(read, w2_ref, vals_ref):
    scores = []
    pairs = []
    for pair in range(LEVELS // 2):
        pixels = jnp.concatenate([level_rows(read(2 * pair), 2 * pair), level_rows(read(2 * pair + 1), 2 * pair + 1)], axis=1)
        pairs.append(pixels)
        out = dot(w2_ref[...], jnp.concatenate([pixels, pixels], axis=0))
        vals_ref[2 * pair] = out[:D, :128]
        vals_ref[2 * pair + 1] = out[:D, 128:]
        scores.append(out[D : D + 24, :128])
        scores.append(out[D : D + 24, 128:])
    expo = [jnp.exp(s) for s in scores]
    total = expo[0]
    for e in expo[1:]:
        total = total + e
    inverse = 1.0 / total
    return pairs, [(e * inverse).astype(BF).astype(F32) for e in expo]


def pool_kernel(x_ref, d_ref, w2_ref, woutp_ref, latent_ref, terms_ref, vals_ref, dpool_ref, pooled_ref, dv_ref, tacc_ref, gacc_ref):
    step = pl.program_id(0)
    pairs, probs = forward_levels(lambda l: x_ref[l], w2_ref, vals_ref)
    d_rows = jnp.concatenate([d_ref[:, q].reshape(128, D) for q in range(LATENT)], axis=0)
    dpool_ref[...] = dot(woutp_ref[...], d_rows, 1, 1)
    parts = [[probs[l][q * HEADS : (q + 1) * HEADS] for q in range(LATENT)] for l in range(LEVELS)]

    def mix_loop(i, carry):
        base = pl.multiple_of(i * 16, 16)
        pooled = [[], [], []]
        dvals = [[] for _ in range(LEVELS)]
        for e in range(2):
            rows = pl.ds(base + 8 * e, 8)
            dq = [dpool_ref[rows, q * 128 : (q + 1) * 128] for q in range(LATENT)]
            acc = [None] * LATENT
            for l in range(LEVELS):
                v = vals_ref[l, rows, :]
                for q in range(LATENT):
                    term = parts[l][q] * v
                    acc[q] = term if acc[q] is None else acc[q] + term
                dvals[l].append(parts[l][0] * dq[0] + parts[l][1] * dq[1] + parts[l][2] * dq[2])
            for q in range(LATENT):
                pooled[q].append(acc[q])
        for q in range(LATENT):
            pooled_ref[pl.ds(base, 16), q * 128 : (q + 1) * 128] = jnp.concatenate(pooled[q], axis=0).astype(BF)
        for l in range(LEVELS):
            lanes = slice((l % 2) * 128, (l % 2) * 128 + 128)
            dv_ref[l // 2, pl.ds(base, 16), lanes] = jnp.concatenate(dvals[l], axis=0).astype(BF)
        return carry

    lax.fori_loop(0, D // 16, mix_loop, 0)

    def dprob_loop(i, carry):
        acc = list(carry)
        for e in range(2):
            rows = pl.ds(pl.multiple_of(i * 16 + 8 * e, 8), 8)
            dq = [dpool_ref[rows, q * 128 : (q + 1) * 128] for q in range(LATENT)]
            for l in range(LEVELS):
                v = vals_ref[l, rows, :]
                for q in range(LATENT):
                    acc[l * LATENT + q] = acc[l * LATENT + q] + dq[q] * v
        return tuple(acc)

    zero = jnp.zeros((HEADS, 128), F32)
    dprob = lax.fori_loop(0, D // 16, dprob_loop, (zero,) * (LEVELS * LATENT))
    scale = 1.0 / math.sqrt(HD)
    delta = []
    for q in range(LATENT):
        total = parts[0][q] * dprob[q]
        for l in range(1, LEVELS):
            total = total + parts[l][q] * dprob[l * LATENT + q]
        delta.append(total)
    for l in range(LEVELS):
        ds = [parts[l][q] * (dprob[l * LATENT + q] - delta[q]) * scale for q in range(LATENT)]
        lanes = slice((l % 2) * 128, (l % 2) * 128 + 128)
        dv_ref[l // 2, D:MV, lanes] = jnp.concatenate(ds + [zero], axis=0).astype(BF)

    @pl.when(step == 0)
    def _():
        tacc_ref[...] = jnp.zeros_like(tacc_ref)
        gacc_ref[...] = jnp.zeros_like(gacc_ref)

    terms = dot(dv_ref[0], pairs[0], 1, 1)
    for pair in range(1, LEVELS // 2):
        terms = terms + dot(dv_ref[pair], pairs[pair], 1, 1)
    tacc_ref[...] += terms
    pooled = pooled_ref[...]
    gterm = dot(pooled, d_rows)
    for j in range(4):
        gacc_ref[j * D : (j + 1) * D, :] += gterm[:, j * 128 : (j + 1) * 128]
    latent = dot(pooled, woutp_ref[...], 0, 0).astype(BF)
    for q in range(LATENT):
        latent_ref[:, q] = latent[q * 128 : (q + 1) * 128].reshape(8, 16, D)

    @pl.when(step == pl.num_programs(0) - 1)
    def _():
        for h in range(HEADS):
            for j in range(4):
                terms_ref[j * D + h * HD : j * D + (h + 1) * HD, :] = gacc_ref[pl.ds(j * D + h, HD, stride=HEADS), :].astype(BF)
            terms_ref[4 * D + h * HD : 4 * D + (h + 1) * HD, :] = tacc_ref[pl.ds(h, HD, stride=HEADS), :].astype(BF)
        terms_ref[5 * D : 5 * D + MV - D, :] = tacc_ref[D:MV, :].astype(BF)
        terms_ref[5 * D + MV - D :, :] = jnp.zeros((TERMS - 5 * D - MV + D, KX), BF)


def normalise(values, gain):
    mean = jnp.mean(values, axis=-1, keepdims=True)
    centred = values - mean
    var = jnp.mean(centred * centred, axis=-1, keepdims=True)
    return (centred * lax.rsqrt(var + 1e-05) * gain).astype(BF)


def window_index(column, wa):
    return column * 3 + wa


def permutation(rows, dim):
    dst = lax.broadcasted_iota(jnp.int32, (rows, rows), dim)
    src = lax.broadcasted_iota(jnp.int32, (rows, rows), 1 - dim)
    a = dst
    b = dst - 96
    c = dst - 288
    low = (a // 4) * 16 + a % 4
    mid = (b // 8) * 16 + 4 + b % 8
    high = (c // 4) * 16 + 12 + c % 4
    want = jnp.where(dst < 96, low, jnp.where(dst < 288, mid, high))
    return jnp.where(src == want, 1.0, 0.0).astype(BF)


def window_kernel(edge_ref, xh_ref, latent_ref, w2_ref, woutp_ref, gain_ref, wqkv_ref, wproj_ref, out_ref, vals_ref, pooled_ref, q_ref, kv_ref, att_ref):
    gain = gain_ref[...]

    def halo(group, carry):
        lane0 = pl.multiple_of(group * 128, 128)
        _, probs = forward_levels(lambda l: xh_ref[l, :, pl.ds(lane0, 128)], w2_ref, vals_ref)
        parts = [[probs[l][q * HEADS : (q + 1) * HEADS] for q in range(LATENT)] for l in range(LEVELS)]

        def mix_loop(i, inner):
            base = pl.multiple_of(i * 16, 16)
            pooled = [[], [], []]
            for e in range(2):
                rows = pl.ds(base + 8 * e, 8)
                acc = [None] * LATENT
                for l in range(LEVELS):
                    v = vals_ref[l, rows, :]
                    for q in range(LATENT):
                        term = parts[l][q] * v
                        acc[q] = term if acc[q] is None else acc[q] + term
                for q in range(LATENT):
                    pooled[q].append(acc[q])
            for q in range(LATENT):
                pooled_ref[pl.ds(base, 16), q * 128 : (q + 1) * 128] = jnp.concatenate(pooled[q], axis=0).astype(BF)
            return inner

        lax.fori_loop(0, D // 16, mix_loop, 0)
        latent = dot(pooled_ref[...], woutp_ref[...], 0, 0).astype(BF).astype(F32)
        normed = normalise(latent, gain)
        kv = dot(normed, wqkv_ref[:, D:]).astype(BF)

        @pl.when(group < 2)
        def _():
            first = group * 3
            for q in range(LATENT):
                kv_ref[first, 48 + 48 * q : 96 + 48 * q, :] = kv[q * 128 : q * 128 + 48]
                kv_ref[first + 1, 96 + 32 * q : 128 + 32 * q, :] = kv[q * 128 + 48 : q * 128 + 80]
                kv_ref[first + 2, 48 + 48 * q : 96 + 48 * q, :] = kv[q * 128 + 80 : q * 128 + 128]

        @pl.when(group >= 2)
        def _():
            first = 6 + (group - 2) * 6
            for half in range(2):
                for q in range(LATENT):
                    row = q * 128 + half * 64
                    kv_ref[first + 3 * half, 96 + 32 * q : 128 + 32 * q, :] = kv[row : row + 32]
                    kv_ref[first + 3 * half + 2, 96 + 32 * q : 128 + 32 * q, :] = kv[row + 32 : row + 64]
        return carry

    lax.fori_loop(0, 4, halo, 0)

    def project(rows, column):
        normed = normalise(rows.astype(F32), gain)
        normed = dot(permutation(384, 0), normed).astype(BF)
        q_ref[column] = (dot(normed, wqkv_ref[:, :D]).astype(BF).astype(F32) * (1.0 / math.sqrt(HD))).astype(BF)
        return dot(normed, wqkv_ref[:, D:]).astype(BF)

    rows = jnp.concatenate([latent_ref[28:32].reshape(192, D), latent_ref[0:4].reshape(192, D)], axis=0)
    kv = project(rows, 0)
    for side in range(2):
        first = 3 * (1 - side)
        kv_ref[first, 0:48, :] = kv[48 * side : 48 * side + 48]
        kv_ref[first + 1, 0:96, :] = kv[96 + 96 * side : 192 + 96 * side]
        kv_ref[first + 2, 0:48, :] = kv[288 + 48 * side : 336 + 48 * side]

    def own(column, carry):
        rows = latent_ref[pl.ds(8 * column - 4, 8)].reshape(384, D)
        kv = project(rows, column)
        first = 3 + 3 * column
        kv_ref[first, 0:96, :] = kv[0:96]
        kv_ref[first + 1, 0:192, :] = kv[96:288]
        kv_ref[first + 2, 0:96, :] = kv[288:384]
        return carry

    lax.fori_loop(1, 4, own, 0)

    key = lax.broadcasted_iota(jnp.int32, (1, 192), 1)
    odd_lane = lax.broadcasted_iota(jnp.int32, (1, 128), 1) >= HD

    def attend(column, window, row0, count, valid):
        for pair in range(HEADS // 2):
            lanes = slice(pair * 128, pair * 128 + 128)
            q = q_ref[column, row0 : row0 + count, lanes]
            nil = jnp.zeros_like(q)
            q2 = jnp.concatenate([jnp.where(odd_lane, nil, q), jnp.where(odd_lane, q, nil)], axis=0)
            expo = jnp.exp(dot(q2, kv_ref[window, :, lanes], 1, 1))
            if valid is not None:
                expo = jnp.where(valid, expo, 0.0)
            probs = (expo * (1.0 / jnp.sum(expo, axis=-1, keepdims=True))).astype(BF)
            both = dot(probs, kv_ref[window, :, D + pair * 128 : D + pair * 128 + 128])
            att_ref[row0 : row0 + count, lanes] = jnp.where(odd_lane, both[count:], both[:count]).astype(BF)

    inside = (edge_ref[0] == 0, edge_ref[1] == 0)
    plain = [(key < 96) | ok for ok in inside]
    corner = [(key < 48) | (key % 48 < 16) | ok for ok in inside]

    def finish(rows):
        natural = dot(permutation(384, 1), att_ref[...]).astype(BF)
        return (rows.astype(F32) + dot(natural, wproj_ref[...])).astype(BF)

    for side in range(2):
        first = 3 * (1 - side)
        attend(0, first, 48 * side, 48, corner[0])
        attend(0, first + 1, 96 + 96 * side, 96, None)
        attend(0, first + 2, 288 + 48 * side, 48, corner[1])
    done = finish(rows)
    out_ref[28:32] = done[:192].reshape(4, 3, 16, D)
    out_ref[0:4] = done[192:].reshape(4, 3, 16, D)

    def column_loop(column, carry):
        first = 3 + 3 * column
        attend(column, first, 0, 96, plain[0])
        attend(column, first + 1, 96, 192, None)
        attend(column, first + 2, 288, 96, plain[1])
        rows = latent_ref[pl.ds(8 * column - 4, 8)].reshape(384, D)
        out_ref[pl.ds(8 * column - 4, 8)] = finish(rows).reshape(8, 3, 16, D)
        return carry

    lax.fori_loop(1, 4, column_loop, 0)


def place(lev, tile):
    return {"lev": lev, "tile": tile}


def sum_kernel(terms_ref, total_ref, part_ref, band_ref, full_ref, send_sem, recv_sem):
    lev, tile = lax.axis_index("lev"), lax.axis_index("tile")
    bands, tiles = lax.axis_size("lev"), lax.axis_size("tile")
    barrier = pltpu.get_barrier_semaphore()
    for off in range(1, tiles):
        pl.semaphore_signal(barrier, inc=1, device_id=place(lev, lax.rem(tile + off, tiles)), device_id_type=pl.DeviceIdType.MESH)
    for off in range(1, bands):
        pl.semaphore_signal(barrier, inc=1, device_id=place(lax.rem(lev + off, bands), tile), device_id_type=pl.DeviceIdType.MESH)
    pl.semaphore_wait(barrier, tiles + bands - 2)

    def copy(src, dst, slot, device):
        return pltpu.make_async_remote_copy(src_ref=src, dst_ref=dst, send_sem=send_sem.at[slot], recv_sem=recv_sem.at[slot], device_id=device, device_id_type=pl.DeviceIdType.MESH)

    first = []
    for off in range(1, tiles):
        peer = lax.rem(tile + off, tiles)
        first.append(copy(terms_ref.at[peer], part_ref.at[off], off - 1, place(lev, peer)))
    for c in first:
        c.start()
    total = terms_ref[tile].astype(F32)
    for off, c in enumerate(first):
        c.wait_recv()
        total = total + part_ref[off + 1].astype(F32)
    band_ref[lev] = total.astype(BF)
    second = []
    for off in range(1, bands):
        second.append(copy(band_ref.at[lev], band_ref.at[lev], 14 + off, place(lax.rem(lev + off, bands), tile)))
    for c in second:
        c.start()
    for c in second:
        c.wait_recv()
    total = band_ref[0].astype(F32)
    for b in range(1, bands):
        total = total + band_ref[b].astype(F32)
    full_ref[tile] = total.astype(BF)
    third = []
    for off in range(1, tiles):
        third.append(copy(full_ref.at[tile], full_ref.at[tile], 21 + off, place(lev, lax.rem(tile + off, tiles))))
    for c in third:
        c.start()
    for c in third:
        c.wait_recv()
    total_ref[...] = full_ref[...]
    for c in first + second + third:
        c.wait_send()


def grads_kernel(total_ref, we_ref, queries_ref, wkv_ref, gembed_ref, gkv_ref, gout_ref, factor):
    qm = query_rows(queries_ref[...].astype(F32)).astype(BF)
    for j in range(4):
        gout_ref[:, j * 128 : (j + 1) * 128] = total_ref[j * D : (j + 1) * D, :].astype(F32) * factor
    values = total_ref[4 * D : 5 * D, :]
    keys = dot(qm, total_ref[5 * D : 5 * D + 32, :][:24], 0, 0)
    khigh, klow = split(keys)
    we = we_ref[...]
    gkv_ref[:, :D] = (dot(we, khigh, 0, 1) + dot(we, klow, 0, 1)) * factor
    gkv_ref[:, D:] = dot(we, values, 0, 1) * factor
    wk, wv = wkv_ref[:, :D], wkv_ref[:, D:]
    grad = dot(khigh, wk, 0, 1) + dot(klow, wk, 0, 1) + dot(values, wv, 0, 1)
    gembed_ref[...] = grad[:F] * factor


def whole(shape, dtype):
    return jax.ShapeDtypeStruct(shape, dtype)


def params(**kw):
    return pltpu.CompilerParams(vmem_limit_bytes=VMEM_LIMIT, **kw)


def halo_positions(ext):
    bands = ext.reshape(F, 40, 17, 8)
    low, mid, high = (bands[:, :, wa : wa + 15 : 2] for wa in range(3))

    def flat(block):
        return block.transpose(2, 0, 1, 3).reshape(LEVELS, F, -1)

    pieces = []
    for far, near in ((slice(0, 4), slice(4, 8)), (slice(36, 40), slice(32, 36))):
        pieces += [flat(low[:, far, :, 4:]), flat(low[:, far, :, :4]), flat(low[:, near, :, :4])]
        pieces += [flat(mid[:, far])]
        pieces += [flat(high[:, far, :, :4]), flat(high[:, far, :, 4:]), flat(high[:, near, :, 4:])]
    for c in (1, 2, 3):
        pieces += [flat(low[:, 8 * c : 8 * c + 8, :, :4]), flat(high[:, 8 * c : 8 * c + 8, :, 4:])]
    pieces.append(jnp.zeros((LEVELS, F, 64), ext.dtype))
    return jnp.concatenate(pieces, axis=2)


def per_device(inputs, level_ids, level_table, w_embed, queries, w_kv, w_out, gain, w_qkv, w_proj, d_latent):
    band = lax.axis_index("lev")
    bands = lax.axis_size("lev")
    tiles = lax.axis_size("tile")
    lon_rows, lat_rows = d_latent.shape[:2]
    x = inputs[0]
    ring = [(i, (i + 1) % tiles) for i in range(tiles)]
    back = [(target, source) for source, target in ring]
    west = lax.ppermute(x[:, 28:32], "tile", ring)
    east = lax.ppermute(x[:, 0:4], "tile", back)
    own = x.reshape(F, 32, 8, 16).transpose(2, 0, 1, 3).reshape(LEVELS, F, 512)
    own = lax.all_to_all(own, "lev", split_axis=0, concat_axis=0, tiled=True)
    ext = jnp.pad(jnp.concatenate([west, x, east], axis=1), ((0, 0), (0, 0), (4, 4)))
    far = lax.all_to_all(halo_positions(ext), "lev", split_axis=0, concat_axis=0, tiled=True)

    onehot = (level_ids[:, None] == jnp.arange(level_table.shape[0], dtype=jnp.int32)[None, :]).astype(BF)
    rows = jnp.dot(onehot, level_table, preferred_element_type=F32).astype(BF)
    we = jnp.concatenate([w_embed, rows, jnp.zeros((KX - F - LEVELS, D), BF)], axis=0)
    w2, woutp = pl.pallas_call(
        weights_kernel,
        out_shape=(whole((MV, 2 * KX), BF), whole((D, D), BF)),
        compiler_params=params(),
        name="weights",
    )(we, queries, w_kv, w_out)

    d_nat = d_latent.transpose(0, 2, 1, 3)
    block = pl.BlockSpec((8, LATENT, 16, D), lambda g: (g, 0, 0, 0))

    def fixed(shape):
        return pl.BlockSpec(shape, lambda g: (0,) * len(shape))

    latent, terms = pl.pallas_call(
        pool_kernel,
        grid=(4,),
        in_specs=[
            pl.BlockSpec((LEVELS, F, 128), lambda g: (0, 0, g)),
            block,
            fixed((MV, 2 * KX)),
            fixed((D, D)),
        ],
        out_specs=[block, fixed((TERMS, KX))],
        out_shape=(whole(d_nat.shape, BF), whole((TERMS, KX), BF)),
        scratch_shapes=[
            pltpu.VMEM((LEVELS, D, 128), F32),
            pltpu.VMEM((D, 384), F32),
            pltpu.VMEM((D, 384), BF),
            pltpu.VMEM((LEVELS // 2, MV, 256), BF),
            pltpu.VMEM((MV, KX), F32),
            pltpu.VMEM((4 * D, 128), F32),
        ],
        compiler_params=params(dimension_semantics=("arbitrary",)),
        name="pool",
    )(own, d_nat, w2, woutp)

    factor = 1.0 / math.sqrt(lon_rows * lat_rows * bands * tiles)
    total = pl.pallas_call(
        sum_kernel,
        in_specs=[pl.BlockSpec(memory_space=pltpu.VMEM)],
        out_specs=pl.BlockSpec(memory_space=pltpu.VMEM),
        out_shape=whole((16, CHUNK, KX), BF),
        scratch_shapes=[
            pltpu.VMEM((16, CHUNK, KX), BF),
            pltpu.VMEM((8, CHUNK, KX), BF),
            pltpu.VMEM((16, CHUNK, KX), BF),
            pltpu.SemaphoreType.DMA((37,)),
            pltpu.SemaphoreType.DMA((37,)),
        ],
        compiler_params=params(collective_id=1, has_side_effects=True),
        name="sums",
    )(terms.reshape(16, CHUNK, KX))

    edge = jnp.stack([band == 0, band == bands - 1]).astype(jnp.int32)
    vmem = pl.BlockSpec(memory_space=pltpu.VMEM)
    out = pl.pallas_call(
        window_kernel,
        in_specs=[pl.BlockSpec(memory_space=pltpu.SMEM)] + [vmem] * 7,
        out_specs=vmem,
        out_shape=whole(d_nat.shape, BF),
        scratch_shapes=[
            pltpu.VMEM((LEVELS, D, 128), F32),
            pltpu.VMEM((D, 384), BF),
            pltpu.VMEM((4, 384, D), BF),
            pltpu.VMEM((18, 192, 2 * D), BF),
            pltpu.VMEM((384, D), BF),
        ],
        compiler_params=params(),
        name="windows",
    )(edge, far, latent, w2, woutp, gain.reshape(1, D), w_qkv, w_proj)

    gembed, gkv, gout = pl.pallas_call(
        functools.partial(grads_kernel, factor=factor),
        out_shape=(whole((F, D), F32), whole((D, 2 * D), F32), whole((D, D), F32)),
        compiler_params=params(),
        name="grads",
    )(total.reshape(TERMS, KX), we, queries, w_kv)
    return (out.transpose(0, 2, 1, 3), gembed, gkv, gout)


def solution(mesh):
    placed = (P("lev", None, "tile", None),) + (P(),) * 9 + (P("tile", "lev", None, None),)
    return jax.shard_map(
        per_device,
        mesh=mesh,
        in_specs=placed,
        out_specs=(P("tile", "lev", None, None), P(), P(), P()),
        check_vma=False,
    )
```

```python
import functools
import math

import jax
import jax.numpy as jnp
import numpy as np
from jax import lax
from jax.experimental import pallas as pl
from jax.experimental.pallas import tpu as pltpu
from jax.sharding import PartitionSpec as P

HD = 64
HEADS = 8
WIN = 8
D = 512
F = 80
LEVELS = 8
LATENT = 3
KX = 128
MV = 544
CHUNK = 176
TERMS = 16 * CHUNK
BF = jnp.bfloat16
F32 = jnp.float32
VMEM_LIMIT = 56 * 1024 * 1024


def dot(a, b, ca=1, cb=0):
    return lax.dot_general(a, b, (((ca,), (cb,)), ((), ())), preferred_element_type=F32)


def split(value):
    high = value.astype(BF)
    return high, (value - high.astype(F32)).astype(BF)


def query_rows(queries):
    rows = jnp.concatenate([jnp.broadcast_to(queries[q : q + 1], (HEADS, D)) for q in range(LATENT)], axis=0)
    head = lax.broadcasted_iota(jnp.int32, (LATENT * HEADS, D), 0) % HEADS
    lane = lax.broadcasted_iota(jnp.int32, (LATENT * HEADS, D), 1) // HD
    return jnp.where(head == lane, rows, 0.0)


def weights_kernel(we_ref, queries_ref, wkv_ref, wout_ref, w2_ref, woutp_ref):
    row = lax.broadcasted_iota(jnp.int32, (D, D), 0)
    lane = lax.broadcasted_iota(jnp.int32, (D, D), 1)
    mix = jnp.where(lane == (row % HEADS) * HD + row // HEADS, 1.0, 0.0).astype(BF)
    we = we_ref[...]
    wv = dot(mix, wkv_ref[:, D:], 1, 1).astype(BF)
    woutp_ref[...] = dot(mix, wout_ref[...]).astype(BF)
    high, low = split(dot(wv, we, 1, 1))
    w2_ref[0:D, 0:KX] = high
    w2_ref[0:D, KX:] = low
    qm = query_rows(queries_ref[...].astype(F32)).astype(BF)
    shigh, slow = split(dot(qm, wkv_ref[:, :D], 1, 1) * (1.0 / math.sqrt(HD)))
    score = dot(shigh, we, 1, 1) + dot(slow, we, 1, 1)
    score = jnp.concatenate([score, jnp.zeros((MV - D - 24, KX), F32)], axis=0)
    high, low = split(score)
    w2_ref[D:MV, 0:KX] = high
    w2_ref[D:MV, KX:] = low


def level_rows(x, level):
    row = lax.broadcasted_iota(jnp.int32, (KX - F, 128), 0)
    ones = jnp.where(row == level, 1.0, 0.0).astype(BF)
    return jnp.concatenate([x, ones], axis=0)


def forward_levels(read, w2_ref, vals_ref):
    scores = []
    pairs = []
    for pair in range(LEVELS // 2):
        pixels = jnp.concatenate([level_rows(read(2 * pair), 2 * pair), level_rows(read(2 * pair + 1), 2 * pair + 1)], axis=1)
        pairs.append(pixels)
        out = dot(w2_ref[...], jnp.concatenate([pixels, pixels], axis=0))
        vals_ref[2 * pair] = out[:D, :128]
        vals_ref[2 * pair + 1] = out[:D, 128:]
        scores.append(out[D : D + 24, :128])
        scores.append(out[D : D + 24, 128:])
    expo = [jnp.exp(s) for s in scores]
    total = expo[0]
    for e in expo[1:]:
        total = total + e
    inverse = 1.0 / total
    return pairs, [(e * inverse).astype(BF).astype(F32) for e in expo]


def pool_kernel(x_ref, d_ref, w2_ref, woutp_ref, latent_ref, terms_ref, vals_ref, dpool_ref, pooled_ref, dv_ref, tacc_ref, gacc_ref):
    step = pl.program_id(0)
    pairs, probs = forward_levels(lambda l: x_ref[l], w2_ref, vals_ref)
    d_rows = jnp.concatenate([d_ref[:, q].reshape(128, D) for q in range(LATENT)], axis=0)
    dpool_ref[...] = dot(woutp_ref[...], d_rows, 1, 1)
    parts = [[probs[l][q * HEADS : (q + 1) * HEADS] for q in range(LATENT)] for l in range(LEVELS)]

    def mix_loop(i, carry):
        base = pl.multiple_of(i * 16, 16)
        pooled = [[], [], []]
        dvals = [[] for _ in range(LEVELS)]
        for e in range(2):
            rows = pl.ds(base + 8 * e, 8)
            dq = [dpool_ref[rows, q * 128 : (q + 1) * 128] for q in range(LATENT)]
            acc = [None] * LATENT
            for l in range(LEVELS):
                v = vals_ref[l, rows, :]
                for q in range(LATENT):
                    term = parts[l][q] * v
                    acc[q] = term if acc[q] is None else acc[q] + term
                dvals[l].append(parts[l][0] * dq[0] + parts[l][1] * dq[1] + parts[l][2] * dq[2])
            for q in range(LATENT):
                pooled[q].append(acc[q])
        for q in range(LATENT):
            pooled_ref[pl.ds(base, 16), q * 128 : (q + 1) * 128] = jnp.concatenate(pooled[q], axis=0).astype(BF)
        for l in range(LEVELS):
            lanes = slice((l % 2) * 128, (l % 2) * 128 + 128)
            dv_ref[l // 2, pl.ds(base, 16), lanes] = jnp.concatenate(dvals[l], axis=0).astype(BF)
        return carry

    lax.fori_loop(0, D // 16, mix_loop, 0)

    def dprob_loop(i, carry):
        acc = list(carry)
        for e in range(2):
            rows = pl.ds(pl.multiple_of(i * 16 + 8 * e, 8), 8)
            dq = [dpool_ref[rows, q * 128 : (q + 1) * 128] for q in range(LATENT)]
            for l in range(LEVELS):
                v = vals_ref[l, rows, :]
                for q in range(LATENT):
                    acc[l * LATENT + q] = acc[l * LATENT + q] + dq[q] * v
        return tuple(acc)

    zero = jnp.zeros((HEADS, 128), F32)
    dprob = lax.fori_loop(0, D // 16, dprob_loop, (zero,) * (LEVELS * LATENT))
    scale = 1.0 / math.sqrt(HD)
    delta = []
    for q in range(LATENT):
        total = parts[0][q] * dprob[q]
        for l in range(1, LEVELS):
            total = total + parts[l][q] * dprob[l * LATENT + q]
        delta.append(total)
    for l in range(LEVELS):
        ds = [parts[l][q] * (dprob[l * LATENT + q] - delta[q]) * scale for q in range(LATENT)]
        lanes = slice((l % 2) * 128, (l % 2) * 128 + 128)
        dv_ref[l // 2, D:MV, lanes] = jnp.concatenate(ds + [zero], axis=0).astype(BF)

    @pl.when(step == 0)
    def _():
        tacc_ref[...] = jnp.zeros_like(tacc_ref)
        gacc_ref[...] = jnp.zeros_like(gacc_ref)

    terms = dot(dv_ref[0], pairs[0], 1, 1)
    for pair in range(1, LEVELS // 2):
        terms = terms + dot(dv_ref[pair], pairs[pair], 1, 1)
    tacc_ref[...] += terms
    pooled = pooled_ref[...]
    gterm = dot(pooled, d_rows)
    for j in range(4):
        gacc_ref[j * D : (j + 1) * D, :] += gterm[:, j * 128 : (j + 1) * 128]
    latent = dot(pooled, woutp_ref[...], 0, 0).astype(BF)
    for q in range(LATENT):
        latent_ref[:, q] = latent[q * 128 : (q + 1) * 128].reshape(8, 16, D)

    @pl.when(step == pl.num_programs(0) - 1)
    def _():
        for h in range(HEADS):
            for j in range(4):
                terms_ref[j * D + h * HD : j * D + (h + 1) * HD, :] = gacc_ref[pl.ds(j * D + h, HD, stride=HEADS), :].astype(BF)
            terms_ref[4 * D + h * HD : 4 * D + (h + 1) * HD, :] = tacc_ref[pl.ds(h, HD, stride=HEADS), :].astype(BF)
        terms_ref[5 * D : 5 * D + MV - D, :] = tacc_ref[D:MV, :].astype(BF)
        terms_ref[5 * D + MV - D :, :] = jnp.zeros((TERMS - 5 * D - MV + D, KX), BF)


def normalise(values, gain):
    mean = jnp.mean(values, axis=-1, keepdims=True)
    centred = values - mean
    var = jnp.mean(centred * centred, axis=-1, keepdims=True)
    return (centred * lax.rsqrt(var + 1e-05) * gain).astype(BF)


def window_index(column, wa):
    return column * 3 + wa


def permutation(rows, dim):
    dst = lax.broadcasted_iota(jnp.int32, (rows, rows), dim)
    src = lax.broadcasted_iota(jnp.int32, (rows, rows), 1 - dim)
    a = dst
    b = dst - 96
    c = dst - 288
    low = (a // 4) * 16 + a % 4
    mid = (b // 8) * 16 + 4 + b % 8
    high = (c // 4) * 16 + 12 + c % 4
    want = jnp.where(dst < 96, low, jnp.where(dst < 288, mid, high))
    return jnp.where(src == want, 1.0, 0.0).astype(BF)


def place(lev, tile):
    return {"lev": lev, "tile": tile}


def sum_stages(terms_ref, part_ref, band_ref, full_ref, send_sem, recv_sem):
    lev, tile = lax.axis_index("lev"), lax.axis_index("tile")
    bands, tiles = lax.axis_size("lev"), lax.axis_size("tile")

    def copy(src, dst, slot, device):
        return pltpu.make_async_remote_copy(src_ref=src, dst_ref=dst, send_sem=send_sem.at[slot], recv_sem=recv_sem.at[slot], device_id=device, device_id_type=pl.DeviceIdType.MESH)

    tile_peers = [place(lev, lax.rem(tile + off, tiles)) for off in range(1, tiles)]
    lev_peers = [place(lax.rem(lev + off, bands), tile) for off in range(1, bands)]
    first = [copy(terms_ref.at[peer["tile"]], part_ref.at[i], i, peer) for i, peer in enumerate(tile_peers)]
    second = [copy(band_ref.at[lev], band_ref.at[lev], 15 + i, peer) for i, peer in enumerate(lev_peers)]
    third = [copy(full_ref.at[tile], full_ref.at[tile], 22 + i, peer) for i, peer in enumerate(tile_peers)]

    def greet():
        barrier = pltpu.get_barrier_semaphore()
        for peer in tile_peers + lev_peers:
            pl.semaphore_signal(barrier, inc=1, device_id=peer, device_id_type=pl.DeviceIdType.MESH)
        pl.semaphore_wait(barrier, tiles + bands - 2)
        for c in first:
            c.start()

    def over_lev():
        total = terms_ref[tile].astype(F32)
        for i, c in enumerate(first):
            c.wait_recv()
            total = total + part_ref[i].astype(F32)
        band_ref[lev] = total.astype(BF)
        for c in second:
            c.start()

    def gather():
        for c in second:
            c.wait_recv()
        total = band_ref[0].astype(F32)
        for b in range(1, bands):
            total = total + band_ref[b].astype(F32)
        full_ref[tile] = total.astype(BF)
        for c in third:
            c.start()

    def close(total_ref):
        for c in third:
            c.wait_recv()
        total_ref[...] = full_ref[...]
        for c in first + second + third:
            c.wait_send()

    return greet, over_lev, gather, close


def window_kernel(terms_ref, edge_ref, xh_ref, latent_ref, w2_ref, woutp_ref, gain_ref, wqkv_ref, att_ref, total_ref, vals_ref, pooled_ref, q_ref, kv_ref, part_ref, band_ref, full_ref, send_sem, recv_sem):
    gain = gain_ref[...]
    greet, over_lev, gather, close = sum_stages(terms_ref, part_ref, band_ref, full_ref, send_sem, recv_sem)
    greet()

    def halo(group, carry):
        lane0 = pl.multiple_of(group * 128, 128)
        _, probs = forward_levels(lambda l: xh_ref[l, :, pl.ds(lane0, 128)], w2_ref, vals_ref)
        parts = [[probs[l][q * HEADS : (q + 1) * HEADS] for q in range(LATENT)] for l in range(LEVELS)]

        def mix_loop(i, inner):
            base = pl.multiple_of(i * 16, 16)
            pooled = [[], [], []]
            for e in range(2):
                rows = pl.ds(base + 8 * e, 8)
                acc = [None] * LATENT
                for l in range(LEVELS):
                    v = vals_ref[l, rows, :]
                    for q in range(LATENT):
                        term = parts[l][q] * v
                        acc[q] = term if acc[q] is None else acc[q] + term
                for q in range(LATENT):
                    pooled[q].append(acc[q])
            for q in range(LATENT):
                pooled_ref[pl.ds(base, 16), q * 128 : (q + 1) * 128] = jnp.concatenate(pooled[q], axis=0).astype(BF)
            return inner

        lax.fori_loop(0, D // 16, mix_loop, 0)
        latent = dot(pooled_ref[...], woutp_ref[...], 0, 0).astype(BF).astype(F32)
        normed = normalise(latent, gain)
        kv = dot(normed, wqkv_ref[:, D:]).astype(BF)

        @pl.when(group < 2)
        def _():
            first = group * 3
            for q in range(LATENT):
                kv_ref[first, 48 + 48 * q : 96 + 48 * q, :] = kv[q * 128 : q * 128 + 48]
                kv_ref[first + 1, 96 + 32 * q : 128 + 32 * q, :] = kv[q * 128 + 48 : q * 128 + 80]
                kv_ref[first + 2, 48 + 48 * q : 96 + 48 * q, :] = kv[q * 128 + 80 : q * 128 + 128]

        @pl.when(group >= 2)
        def _():
            first = 6 + (group - 2) * 6
            for half in range(2):
                for q in range(LATENT):
                    row = q * 128 + half * 64
                    kv_ref[first + 3 * half, 96 + 32 * q : 128 + 32 * q, :] = kv[row : row + 32]
                    kv_ref[first + 3 * half + 2, 96 + 32 * q : 128 + 32 * q, :] = kv[row + 32 : row + 64]
        return carry

    lax.fori_loop(0, 4, halo, 0)

    def project(rows, column):
        normed = normalise(rows.astype(F32), gain)
        normed = dot(permutation(384, 0), normed).astype(BF)
        q_ref[column] = (dot(normed, wqkv_ref[:, :D]).astype(BF).astype(F32) * (1.0 / math.sqrt(HD))).astype(BF)
        return dot(normed, wqkv_ref[:, D:]).astype(BF)

    rows = jnp.concatenate([latent_ref[28:32].reshape(192, D), latent_ref[0:4].reshape(192, D)], axis=0)
    kv = project(rows, 0)
    for side in range(2):
        first = 3 * (1 - side)
        kv_ref[first, 0:48, :] = kv[48 * side : 48 * side + 48]
        kv_ref[first + 1, 0:96, :] = kv[96 + 96 * side : 192 + 96 * side]
        kv_ref[first + 2, 0:48, :] = kv[288 + 48 * side : 336 + 48 * side]

    def own(column, carry):
        rows = latent_ref[pl.ds(8 * column - 4, 8)].reshape(384, D)
        kv = project(rows, column)
        first = 3 + 3 * column
        kv_ref[first, 0:96, :] = kv[0:96]
        kv_ref[first + 1, 0:192, :] = kv[96:288]
        kv_ref[first + 2, 0:96, :] = kv[288:384]
        return carry

    lax.fori_loop(1, 4, own, 0)
    over_lev()

    key = lax.broadcasted_iota(jnp.int32, (1, 192), 1)
    odd_lane = lax.broadcasted_iota(jnp.int32, (1, 128), 1) >= HD

    def attend(column, window, row0, count, valid):
        for pair in range(HEADS // 2):
            lanes = slice(pair * 128, pair * 128 + 128)
            q = q_ref[column, row0 : row0 + count, lanes]
            nil = jnp.zeros_like(q)
            q2 = jnp.concatenate([jnp.where(odd_lane, nil, q), jnp.where(odd_lane, q, nil)], axis=0)
            expo = jnp.exp(dot(q2, kv_ref[window, :, lanes], 1, 1))
            if valid is not None:
                expo = jnp.where(valid, expo, 0.0)
            probs = (expo * (1.0 / jnp.sum(expo, axis=-1, keepdims=True))).astype(BF)
            both = dot(probs, kv_ref[window, :, D + pair * 128 : D + pair * 128 + 128])
            att_ref[column, row0 : row0 + count, lanes] = jnp.where(odd_lane, both[count:], both[:count]).astype(BF)

    inside = (edge_ref[0] == 0, edge_ref[1] == 0)
    plain = [(key < 96) | ok for ok in inside]
    corner = [(key < 48) | (key % 48 < 16) | ok for ok in inside]

    for side in range(2):
        first = 3 * (1 - side)
        attend(0, first, 48 * side, 48, corner[0])
        attend(0, first + 1, 96 + 96 * side, 96, None)
        attend(0, first + 2, 288 + 48 * side, 48, corner[1])
    gather()

    def column_loop(column, carry):
        first = 3 + 3 * column
        attend(column, first, 0, 96, plain[0])
        attend(column, first + 1, 96, 192, None)
        attend(column, first + 2, 288, 96, plain[1])
        return carry

    lax.fori_loop(1, 4, column_loop, 0)
    close(total_ref)


def finish_kernel(att_ref, latent_ref, wproj_ref, total_ref, we_ref, queries_ref, wkv_ref, out_ref, gembed_ref, gkv_ref, gout_ref, factor):
    back = permutation(384, 1)

    def finish(column, rows):
        natural = dot(back, att_ref[column]).astype(BF)
        return (rows.astype(F32) + dot(natural, wproj_ref[...])).astype(BF)

    rows = jnp.concatenate([latent_ref[28:32].reshape(192, D), latent_ref[0:4].reshape(192, D)], axis=0)
    done = finish(0, rows)
    out_ref[28:32] = done[:192].reshape(4, 3, 16, D)
    out_ref[0:4] = done[192:].reshape(4, 3, 16, D)

    def column_loop(column, carry):
        rows = latent_ref[pl.ds(8 * column - 4, 8)].reshape(384, D)
        out_ref[pl.ds(8 * column - 4, 8)] = finish(column, rows).reshape(8, 3, 16, D)
        return carry

    lax.fori_loop(1, 4, column_loop, 0)
    grads(total_ref, we_ref, queries_ref, wkv_ref, gembed_ref, gkv_ref, gout_ref, factor)


def grads(total_ref, we_ref, queries_ref, wkv_ref, gembed_ref, gkv_ref, gout_ref, factor):
    qm = query_rows(queries_ref[...].astype(F32)).astype(BF)
    for j in range(4):
        gout_ref[:, j * 128 : (j + 1) * 128] = total_ref[j * D : (j + 1) * D, :].astype(F32) * factor
    values = total_ref[4 * D : 5 * D, :]
    keys = dot(qm, total_ref[5 * D : 5 * D + 32, :][:24], 0, 0)
    khigh, klow = split(keys)
    we = we_ref[...]
    gkv_ref[:, :D] = (dot(we, khigh, 0, 1) + dot(we, klow, 0, 1)) * factor
    gkv_ref[:, D:] = dot(we, values, 0, 1) * factor
    wk, wv = wkv_ref[:, :D], wkv_ref[:, D:]
    grad = dot(khigh, wk, 0, 1) + dot(klow, wk, 0, 1) + dot(values, wv, 0, 1)
    gembed_ref[...] = grad[:F] * factor


def whole(shape, dtype):
    return jax.ShapeDtypeStruct(shape, dtype)


def params(**kw):
    return pltpu.CompilerParams(vmem_limit_bytes=VMEM_LIMIT, **kw)


def halo_positions(ext):
    bands = ext.reshape(F, 40, 17, 8)
    low, mid, high = (bands[:, :, wa : wa + 15 : 2] for wa in range(3))

    def flat(block):
        return block.transpose(2, 0, 1, 3).reshape(LEVELS, F, -1)

    pieces = []
    for far, near in ((slice(0, 4), slice(4, 8)), (slice(36, 40), slice(32, 36))):
        pieces += [flat(low[:, far, :, 4:]), flat(low[:, far, :, :4]), flat(low[:, near, :, :4])]
        pieces += [flat(mid[:, far])]
        pieces += [flat(high[:, far, :, :4]), flat(high[:, far, :, 4:]), flat(high[:, near, :, 4:])]
    for c in (1, 2, 3):
        pieces += [flat(low[:, 8 * c : 8 * c + 8, :, :4]), flat(high[:, 8 * c : 8 * c + 8, :, 4:])]
    pieces.append(jnp.zeros((LEVELS, F, 64), ext.dtype))
    return jnp.concatenate(pieces, axis=2)


def per_device(inputs, level_ids, level_table, w_embed, queries, w_kv, w_out, gain, w_qkv, w_proj, d_latent):
    band = lax.axis_index("lev")
    bands = lax.axis_size("lev")
    tiles = lax.axis_size("tile")
    lon_rows, lat_rows = d_latent.shape[:2]
    x = inputs[0]
    ring = [(i, (i + 1) % tiles) for i in range(tiles)]
    back = [(target, source) for source, target in ring]
    west = lax.ppermute(x[:, 28:32], "tile", ring)
    east = lax.ppermute(x[:, 0:4], "tile", back)
    own = x.reshape(F, 32, 8, 16).transpose(2, 0, 1, 3).reshape(LEVELS, F, 512)
    own = lax.all_to_all(own, "lev", split_axis=0, concat_axis=0, tiled=True)
    ext = jnp.pad(jnp.concatenate([west, x, east], axis=1), ((0, 0), (0, 0), (4, 4)))
    far = lax.all_to_all(halo_positions(ext), "lev", split_axis=0, concat_axis=0, tiled=True)

    onehot = (level_ids[:, None] == jnp.arange(level_table.shape[0], dtype=jnp.int32)[None, :]).astype(BF)
    rows = jnp.dot(onehot, level_table, preferred_element_type=F32).astype(BF)
    we = jnp.concatenate([w_embed, rows, jnp.zeros((KX - F - LEVELS, D), BF)], axis=0)
    w2, woutp = pl.pallas_call(
        weights_kernel,
        out_shape=(whole((MV, 2 * KX), BF), whole((D, D), BF)),
        compiler_params=params(),
        name="weights",
    )(we, queries, w_kv, w_out)

    d_nat = d_latent.transpose(0, 2, 1, 3)
    block = pl.BlockSpec((8, LATENT, 16, D), lambda g: (g, 0, 0, 0))

    def fixed(shape):
        return pl.BlockSpec(shape, lambda g: (0,) * len(shape))

    latent, terms = pl.pallas_call(
        pool_kernel,
        grid=(4,),
        in_specs=[
            pl.BlockSpec((LEVELS, F, 128), lambda g: (0, 0, g)),
            block,
            fixed((MV, 2 * KX)),
            fixed((D, D)),
        ],
        out_specs=[block, fixed((TERMS, KX))],
        out_shape=(whole(d_nat.shape, BF), whole((TERMS, KX), BF)),
        scratch_shapes=[
            pltpu.VMEM((LEVELS, D, 128), F32),
            pltpu.VMEM((D, 384), F32),
            pltpu.VMEM((D, 384), BF),
            pltpu.VMEM((LEVELS // 2, MV, 256), BF),
            pltpu.VMEM((MV, KX), F32),
            pltpu.VMEM((4 * D, 128), F32),
        ],
        compiler_params=params(dimension_semantics=("arbitrary",)),
        name="pool",
    )(own, d_nat, w2, woutp)

    factor = 1.0 / math.sqrt(lon_rows * lat_rows * bands * tiles)
    edge = jnp.stack([band == 0, band == bands - 1]).astype(jnp.int32)
    vmem = pl.BlockSpec(memory_space=pltpu.VMEM)
    att, total = pl.pallas_call(
        window_kernel,
        in_specs=[vmem, pl.BlockSpec(memory_space=pltpu.SMEM)] + [vmem] * 6,
        out_specs=(vmem, vmem),
        out_shape=(whole((4, 384, D), BF), whole((16, CHUNK, KX), BF)),
        scratch_shapes=[
            pltpu.VMEM((LEVELS, D, 128), F32),
            pltpu.VMEM((D, 384), BF),
            pltpu.VMEM((4, 384, D), BF),
            pltpu.VMEM((18, 192, 2 * D), BF),
            pltpu.VMEM((15, CHUNK, KX), BF),
            pltpu.VMEM((8, CHUNK, KX), BF),
            pltpu.VMEM((16, CHUNK, KX), BF),
            pltpu.SemaphoreType.DMA((37,)),
            pltpu.SemaphoreType.DMA((37,)),
        ],
        compiler_params=params(collective_id=1, has_side_effects=True),
        name="windows",
    )(terms.reshape(16, CHUNK, KX), edge, far, latent, w2, woutp, gain.reshape(1, D), w_qkv)

    out, gembed, gkv, gout = pl.pallas_call(
        functools.partial(finish_kernel, factor=factor),
        out_shape=(whole(d_nat.shape, BF), whole((F, D), F32), whole((D, 2 * D), F32), whole((D, D), F32)),
        compiler_params=params(),
        name="finish",
    )(att, latent, w_proj, total.reshape(TERMS, KX), we, queries, w_kv)
    return (out.transpose(0, 2, 1, 3), gembed, gkv, gout)


def solution(mesh):
    placed = (P("lev", None, "tile", None),) + (P(),) * 9 + (P("tile", "lev", None, None),)
    return jax.shard_map(
        per_device,
        mesh=mesh,
        in_specs=placed,
        out_specs=(P("tile", "lev", None, None), P(), P(), P()),
        check_vma=False,
    )
```

```python
import functools
import math

import jax
import jax.numpy as jnp
import numpy as np
from jax import lax
from jax.experimental import pallas as pl
from jax.experimental.pallas import tpu as pltpu
from jax.sharding import PartitionSpec as P

HD = 64
HEADS = 8
WIN = 8
D = 512
F = 80
LEVELS = 8
LATENT = 3
KX = 128
MV = 544
CHUNK = 176
TERMS = 16 * CHUNK
BF = jnp.bfloat16
F32 = jnp.float32
VMEM_LIMIT = 56 * 1024 * 1024


def dot(a, b, ca=1, cb=0):
    return lax.dot_general(a, b, (((ca,), (cb,)), ((), ())), preferred_element_type=F32)


def split(value):
    high = value.astype(BF)
    return high, (value - high.astype(F32)).astype(BF)


def place(lev, tile):
    return {"lev": lev, "tile": tile}


def remote(src, dst, send, recv, device):
    return pltpu.make_async_remote_copy(src_ref=src, dst_ref=dst, send_sem=send, recv_sem=recv, device_id=device, device_id_type=pl.DeviceIdType.MESH)


def query_rows(queries):
    rows = jnp.concatenate([jnp.broadcast_to(queries[q : q + 1], (HEADS, D)) for q in range(LATENT)], axis=0)
    head = lax.broadcasted_iota(jnp.int32, (LATENT * HEADS, D), 0) % HEADS
    lane = lax.broadcasted_iota(jnp.int32, (LATENT * HEADS, D), 1) // HD
    return jnp.where(head == lane, rows, 0.0)


def fold_weights(we_ref, queries_ref, wkv_ref, wout_ref, w2_ref, woutp_ref):
    row = lax.broadcasted_iota(jnp.int32, (D, D), 0)
    lane = lax.broadcasted_iota(jnp.int32, (D, D), 1)
    mix = jnp.where(lane == (row % HEADS) * HD + row // HEADS, 1.0, 0.0).astype(BF)
    we = we_ref[...]
    wv = dot(mix, wkv_ref[:, D:], 1, 1).astype(BF)
    woutp_ref[...] = dot(mix, wout_ref[...]).astype(BF)
    high, low = split(dot(wv, we, 1, 1))
    w2_ref[0:D, 0:KX] = high
    w2_ref[0:D, KX:] = low
    qm = query_rows(queries_ref[...].astype(F32)).astype(BF)
    shigh, slow = split(dot(qm, wkv_ref[:, :D], 1, 1) * (1.0 / math.sqrt(HD)))
    score = dot(shigh, we, 1, 1) + dot(slow, we, 1, 1)
    score = jnp.concatenate([score, jnp.zeros((MV - D - 24, KX), F32)], axis=0)
    high, low = split(score)
    w2_ref[D:MV, 0:KX] = high
    w2_ref[D:MV, KX:] = low


def level_rows(x, level):
    row = lax.broadcasted_iota(jnp.int32, (KX - F, 128), 0)
    ones = jnp.where(row == level, 1.0, 0.0).astype(BF)
    return jnp.concatenate([x, ones], axis=0)


def forward_levels(read, w2_ref, vals_ref):
    scores = []
    pairs = []
    for pair in range(LEVELS // 2):
        pixels = jnp.concatenate([level_rows(read(2 * pair), 2 * pair), level_rows(read(2 * pair + 1), 2 * pair + 1)], axis=1)
        pairs.append(pixels)
        out = dot(w2_ref[...], jnp.concatenate([pixels, pixels], axis=0))
        vals_ref[2 * pair] = out[:D, :128]
        vals_ref[2 * pair + 1] = out[:D, 128:]
        scores.append(out[D : D + 24, :128])
        scores.append(out[D : D + 24, 128:])
    expo = [jnp.exp(s) for s in scores]
    total = expo[0]
    for e in expo[1:]:
        total = total + e
    inverse = 1.0 / total
    return pairs, [(e * inverse).astype(BF).astype(F32) for e in expo]


def select(rows, lanes, want):
    row = lax.broadcasted_iota(jnp.int32, (rows, lanes), 0)
    return jnp.where(row == want, 1.0, 0.0).astype(BF)


def lane_ids(lanes, start=0):
    return lax.broadcasted_iota(jnp.int32, (1, lanes), 1) + start


def inside_row(lon, lat):
    return jnp.where((lat >= 0) & (lat < 128), lon * 128 + lat, -1)


def exchange_stages(x_ref, pixels_ref, xa_ref, xb_ref, own_ref, near_ref, side_ref, mine_ref, rim_ref, send_sem, recv_sem):
    lev, tile = lax.axis_index("lev"), lax.axis_index("tile")
    bands, tiles = lax.axis_size("lev"), lax.axis_size("tile")
    next_tile, last_tile = lax.rem(tile + 1, tiles), lax.rem(tile + tiles - 1, tiles)
    levs = [lax.rem(lev + off, bands) for off in range(bands)]

    def copy(src, dst, slot, device):
        return remote(src, dst, send_sem.at[slot], recv_sem.at[slot], device)

    own, near, east, west = [], [], [], []
    for off in range(1, bands):
        own.append(copy(own_ref.at[levs[off]], mine_ref.at[lev], off - 1, place(levs[off], tile)))
        near.append(copy(near_ref.at[levs[off]], rim_ref.at[lev, :, 256:512], off + 6, place(levs[off], tile)))
    for off in range(bands):
        east.append(copy(side_ref.at[0, levs[off]], rim_ref.at[lev, :, 0:128], 14 + off, place(levs[off], next_tile)))
        west.append(copy(side_ref.at[1, levs[off]], rim_ref.at[lev, :, 128:256], 22 + off, place(levs[off], last_tile)))

    def greet():
        barrier = pltpu.get_barrier_semaphore()
        for off in range(1, bands):
            pl.semaphore_signal(barrier, inc=1, device_id=place(levs[off], tile), device_id_type=pl.DeviceIdType.MESH)
        for off in range(bands):
            for side in (next_tile, last_tile):
                pl.semaphore_signal(barrier, inc=1, device_id=place(levs[off], side), device_id_type=pl.DeviceIdType.MESH)

    def send_own():
        pixels_ref[...] = x_ref[...].reshape(F * 32, 128).astype(F32)
        for lon in range(32):
            plane = pixels_ref[pl.ds(lon, F, stride=32), :].astype(BF)
            xa_ref[(lon // 8) * F : (lon // 8 + 1) * F, (lon % 8) * 128 : (lon % 8 + 1) * 128] = plane
            moved = (lon + 4) % 32
            xb_ref[(moved // 8) * F : (moved // 8 + 1) * F, (moved % 8) * 128 : (moved % 8 + 1) * 128] = plane
        rows = xa_ref[...]
        for two in range(bands // 2):
            j = lane_ids(256)
            want = ((j % 128) // 16) * 128 + 16 * (2 * two + j // 128) + j % 16
            out = dot(rows, select(1024, 256, want)).astype(BF)
            for c in range(4):
                for half in range(2):
                    own_ref[2 * two + half, :, c * 128 : (c + 1) * 128] = out[c * F : (c + 1) * F, half * 128 : (half + 1) * 128]
        pl.semaphore_wait(pltpu.get_barrier_semaphore(), 3 * bands - 1)
        for c in own:
            c.start()
        mine_ref[lev] = own_ref[lev]

    def send_rim():
        rows = xb_ref[...]
        for four in range(2):
            j = lane_ids(256)
            band = 4 * four + j // 64
            lat = 16 * band + j % 4 + jnp.where(j % 64 < 32, -4, 16)
            out = dot(rows, select(1024, 256, inside_row((j % 32) // 4, lat))).astype(BF)
            for b in range(4):
                lanes = slice(64 * b, 64 * b + 64)
                for c in range(2):
                    pair = [out[k * F : (k + 1) * F, lanes] for k in (2 * c, 2 * c + 1)]
                    near_ref[4 * four + b, :, c * 128 : (c + 1) * 128] = jnp.concatenate(pair, axis=1)
        for c in near:
            c.start()
        rows = jnp.concatenate([xb_ref[0:F, 0:512], xb_ref[0:F, 512:1024]], axis=0)
        for two in range(bands // 2):
            j = lane_ids(256)
            k = j % 128
            thin = k % 16
            wide = k - 32
            lat = jnp.where(k < 16, 4 + thin % 4, jnp.where(k < 32, thin % 4, jnp.where(k < 64, 8 + wide % 8, jnp.where(k < 80, 16 + thin % 4, 20 + thin % 4))))
            lon = jnp.where((k >= 32) & (k < 64), wide // 8, thin // 4)
            lat = jnp.where(k < 96, 16 * (2 * two + j // 128) - 4 + lat, -1)
            out = dot(rows, select(512, 256, inside_row(lon, lat))).astype(BF)
            for side in range(2):
                for half in range(2):
                    side_ref[side, 2 * two + half] = out[side * F : (side + 1) * F, half * 128 : (half + 1) * 128]
        for c in east + west:
            c.start()
        rim_ref[lev, :, 256:512] = near_ref[lev]

    def take_own():
        for c in own:
            c.wait_recv()

    def take_rim():
        for c in near + east + west:
            c.wait_recv()
        for c in own + near + east + west:
            c.wait_send()

    return greet, send_own, send_rim, take_own, take_rim


def pool_kernel(x_ref, d_ref, we_ref, queries_ref, wkv_ref, wout_ref, latent_ref, terms_ref, w2_ref, woutp_ref, far_ref, vals_ref, dpool_ref, pooled_ref, dv_ref, tacc_ref, gacc_ref, pixels_ref, xa_ref, xb_ref, own_ref, near_ref, side_ref, mine_ref, rim_ref, send_sem, recv_sem):
    greet, send_own, send_rim, take_own, take_rim = exchange_stages(x_ref, pixels_ref, xa_ref, xb_ref, own_ref, near_ref, side_ref, mine_ref, rim_ref, send_sem, recv_sem)
    greet()
    send_own()
    send_rim()
    fold_weights(we_ref, queries_ref, wkv_ref, wout_ref, w2_ref, woutp_ref)
    tacc_ref[...] = jnp.zeros_like(tacc_ref)
    gacc_ref[...] = jnp.zeros_like(gacc_ref)
    take_own()

    def group_loop(group, carry):
        pool_group(group, mine_ref, d_ref, w2_ref, woutp_ref, latent_ref, vals_ref, dpool_ref, pooled_ref, dv_ref, tacc_ref, gacc_ref)
        return carry

    lax.fori_loop(0, 4, group_loop, 0)
    for h in range(HEADS):
        for j in range(4):
            terms_ref[j * D + h * HD : j * D + (h + 1) * HD, :] = gacc_ref[pl.ds(j * D + h, HD, stride=HEADS), :].astype(BF)
        terms_ref[4 * D + h * HD : 4 * D + (h + 1) * HD, :] = tacc_ref[pl.ds(h, HD, stride=HEADS), :].astype(BF)
    terms_ref[5 * D : 5 * D + MV - D, :] = tacc_ref[D:MV, :].astype(BF)
    terms_ref[5 * D + MV - D :, :] = jnp.zeros((TERMS - 5 * D - MV + D, KX), BF)
    take_rim()
    far_ref[...] = rim_ref[...]


def pool_group(group, x_ref, d_ref, w2_ref, woutp_ref, latent_ref, vals_ref, dpool_ref, pooled_ref, dv_ref, tacc_ref, gacc_ref):
    lane0 = pl.multiple_of(group * 128, 128)
    pairs, probs = forward_levels(lambda l: x_ref[l, :, pl.ds(lane0, 128)], w2_ref, vals_ref)
    d_rows = jnp.concatenate([d_ref[pl.ds(8 * group, 8), q].reshape(128, D) for q in range(LATENT)], axis=0)
    dpool_ref[...] = dot(woutp_ref[...], d_rows, 1, 1)
    parts = [[probs[l][q * HEADS : (q + 1) * HEADS] for q in range(LATENT)] for l in range(LEVELS)]

    def mix_loop(i, carry):
        base = pl.multiple_of(i * 16, 16)
        pooled = [[], [], []]
        dvals = [[] for _ in range(LEVELS)]
        for e in range(2):
            rows = pl.ds(base + 8 * e, 8)
            dq = [dpool_ref[rows, q * 128 : (q + 1) * 128] for q in range(LATENT)]
            acc = [None] * LATENT
            for l in range(LEVELS):
                v = vals_ref[l, rows, :]
                for q in range(LATENT):
                    term = parts[l][q] * v
                    acc[q] = term if acc[q] is None else acc[q] + term
                dvals[l].append(parts[l][0] * dq[0] + parts[l][1] * dq[1] + parts[l][2] * dq[2])
            for q in range(LATENT):
                pooled[q].append(acc[q])
        for q in range(LATENT):
            pooled_ref[pl.ds(base, 16), q * 128 : (q + 1) * 128] = jnp.concatenate(pooled[q], axis=0).astype(BF)
        for l in range(LEVELS):
            lanes = slice((l % 2) * 128, (l % 2) * 128 + 128)
            dv_ref[l // 2, pl.ds(base, 16), lanes] = jnp.concatenate(dvals[l], axis=0).astype(BF)
        return carry

    lax.fori_loop(0, D // 16, mix_loop, 0)

    def dprob_loop(i, carry):
        acc = list(carry)
        for e in range(2):
            rows = pl.ds(pl.multiple_of(i * 16 + 8 * e, 8), 8)
            dq = [dpool_ref[rows, q * 128 : (q + 1) * 128] for q in range(LATENT)]
            for l in range(LEVELS):
                v = vals_ref[l, rows, :]
                for q in range(LATENT):
                    acc[l * LATENT + q] = acc[l * LATENT + q] + dq[q] * v
        return tuple(acc)

    zero = jnp.zeros((HEADS, 128), F32)
    dprob = lax.fori_loop(0, D // 16, dprob_loop, (zero,) * (LEVELS * LATENT))
    scale = 1.0 / math.sqrt(HD)
    delta = []
    for q in range(LATENT):
        total = parts[0][q] * dprob[q]
        for l in range(1, LEVELS):
            total = total + parts[l][q] * dprob[l * LATENT + q]
        delta.append(total)
    for l in range(LEVELS):
        ds = [parts[l][q] * (dprob[l * LATENT + q] - delta[q]) * scale for q in range(LATENT)]
        lanes = slice((l % 2) * 128, (l % 2) * 128 + 128)
        dv_ref[l // 2, D:MV, lanes] = jnp.concatenate(ds + [zero], axis=0).astype(BF)

    terms = dot(dv_ref[0], pairs[0], 1, 1)
    for pair in range(1, LEVELS // 2):
        terms = terms + dot(dv_ref[pair], pairs[pair], 1, 1)
    tacc_ref[...] += terms
    pooled = pooled_ref[...]
    gterm = dot(pooled, d_rows)
    for j in range(4):
        gacc_ref[j * D : (j + 1) * D, :] += gterm[:, j * 128 : (j + 1) * 128]
    latent = dot(pooled, woutp_ref[...], 0, 0).astype(BF)
    for q in range(LATENT):
        latent_ref[pl.ds(8 * group, 8), q] = latent[q * 128 : (q + 1) * 128].reshape(8, 16, D)


def normalise(values, gain):
    mean = jnp.mean(values, axis=-1, keepdims=True)
    centred = values - mean
    var = jnp.mean(centred * centred, axis=-1, keepdims=True)
    return (centred * lax.rsqrt(var + 1e-05) * gain).astype(BF)


def window_index(column, wa):
    return column * 3 + wa


def permutation(rows, dim):
    dst = lax.broadcasted_iota(jnp.int32, (rows, rows), dim)
    src = lax.broadcasted_iota(jnp.int32, (rows, rows), 1 - dim)
    a = dst
    b = dst - 96
    c = dst - 288
    low = (a // 4) * 16 + a % 4
    mid = (b // 8) * 16 + 4 + b % 8
    high = (c // 4) * 16 + 12 + c % 4
    want = jnp.where(dst < 96, low, jnp.where(dst < 288, mid, high))
    return jnp.where(src == want, 1.0, 0.0).astype(BF)


def sum_stages(terms_ref, part_ref, band_ref, full_ref, send_sem, recv_sem):
    lev, tile = lax.axis_index("lev"), lax.axis_index("tile")
    bands, tiles = lax.axis_size("lev"), lax.axis_size("tile")

    def copy(src, dst, slot, device):
        return remote(src, dst, send_sem.at[slot], recv_sem.at[slot], device)

    tile_peers = [place(lev, lax.rem(tile + off, tiles)) for off in range(1, tiles)]
    lev_peers = [place(lax.rem(lev + off, bands), tile) for off in range(1, bands)]
    first = [copy(terms_ref.at[peer["tile"]], part_ref.at[i], i, peer) for i, peer in enumerate(tile_peers)]
    second = [copy(band_ref.at[lev], band_ref.at[lev], 15 + i, peer) for i, peer in enumerate(lev_peers)]
    third = [copy(full_ref.at[tile], full_ref.at[tile], 22 + i, peer) for i, peer in enumerate(tile_peers)]

    def greet():
        barrier = pltpu.get_barrier_semaphore()
        for peer in tile_peers + lev_peers:
            pl.semaphore_signal(barrier, inc=1, device_id=peer, device_id_type=pl.DeviceIdType.MESH)
        pl.semaphore_wait(barrier, tiles + bands - 2)
        for c in first:
            c.start()

    def over_lev():
        total = terms_ref[tile].astype(F32)
        for i, c in enumerate(first):
            c.wait_recv()
            total = total + part_ref[i].astype(F32)
        band_ref[lev] = total.astype(BF)
        for c in second:
            c.start()

    def gather():
        for c in second:
            c.wait_recv()
        total = band_ref[0].astype(F32)
        for b in range(1, bands):
            total = total + band_ref[b].astype(F32)
        full_ref[tile] = total.astype(BF)
        for c in third:
            c.start()

    def close(total_ref):
        for c in third:
            c.wait_recv()
        total_ref[...] = full_ref[...]
        for c in first + second + third:
            c.wait_send()

    return greet, over_lev, gather, close


def window_kernel(terms_ref, edge_ref, xh_ref, latent_ref, w2_ref, woutp_ref, gain_ref, wqkv_ref, att_ref, total_ref, vals_ref, pooled_ref, q_ref, kv_ref, part_ref, band_ref, full_ref, send_sem, recv_sem):
    gain = gain_ref[...]
    greet, over_lev, gather, close = sum_stages(terms_ref, part_ref, band_ref, full_ref, send_sem, recv_sem)
    greet()

    def halo(group, carry):
        lane0 = pl.multiple_of(group * 128, 128)
        _, probs = forward_levels(lambda l: xh_ref[l, :, pl.ds(lane0, 128)], w2_ref, vals_ref)
        parts = [[probs[l][q * HEADS : (q + 1) * HEADS] for q in range(LATENT)] for l in range(LEVELS)]

        def mix_loop(i, inner):
            base = pl.multiple_of(i * 16, 16)
            pooled = [[], [], []]
            for e in range(2):
                rows = pl.ds(base + 8 * e, 8)
                acc = [None] * LATENT
                for l in range(LEVELS):
                    v = vals_ref[l, rows, :]
                    for q in range(LATENT):
                        term = parts[l][q] * v
                        acc[q] = term if acc[q] is None else acc[q] + term
                for q in range(LATENT):
                    pooled[q].append(acc[q])
            for q in range(LATENT):
                pooled_ref[pl.ds(base, 16), q * 128 : (q + 1) * 128] = jnp.concatenate(pooled[q], axis=0).astype(BF)
            return inner

        lax.fori_loop(0, D // 16, mix_loop, 0)
        latent = dot(pooled_ref[...], woutp_ref[...], 0, 0).astype(BF).astype(F32)
        normed = normalise(latent, gain)
        kv = dot(normed, wqkv_ref[:, D:]).astype(BF)

        @pl.when(group < 2)
        def _():
            first = group * 3
            for q in range(LATENT):
                row = q * 128
                kv_ref[first, 48 + 32 * q : 80 + 32 * q, :] = kv[row : row + 32]
                kv_ref[first + 1, 96 + 32 * q : 128 + 32 * q, :] = kv[row + 32 : row + 64]
                kv_ref[first + 2, 48 + 32 * q : 80 + 32 * q, :] = kv[row + 64 : row + 96]

        @pl.when(group == 2)
        def _():
            for q in range(LATENT):
                row = q * 128
                near = slice(144 + 16 * q, 160 + 16 * q)
                kv_ref[3, near, :] = kv[row : row + 16]
                kv_ref[0, near, :] = kv[row + 16 : row + 32]
                kv_ref[5, near, :] = kv[row + 32 : row + 48]
                kv_ref[2, near, :] = kv[row + 48 : row + 64]

        def column_rim(half, column):
            for q in range(LATENT):
                row = q * 128 + half * 64
                near = slice(96 + 32 * q, 128 + 32 * q)
                kv_ref[3 + 3 * column, near, :] = kv[row : row + 32]
                kv_ref[5 + 3 * column, near, :] = kv[row + 32 : row + 64]

        @pl.when(group == 2)
        def _():
            column_rim(1, 1)

        @pl.when(group == 3)
        def _():
            column_rim(0, 2)
            column_rim(1, 3)
        return carry

    lax.fori_loop(0, 4, halo, 0)

    def project(rows, column):
        normed = normalise(rows.astype(F32), gain)
        normed = dot(permutation(384, 0), normed).astype(BF)
        q_ref[column] = (dot(normed, wqkv_ref[:, :D]).astype(BF).astype(F32) * (1.0 / math.sqrt(HD))).astype(BF)
        return dot(normed, wqkv_ref[:, D:]).astype(BF)

    rows = jnp.concatenate([latent_ref[28:32].reshape(192, D), latent_ref[0:4].reshape(192, D)], axis=0)
    kv = project(rows, 0)
    for side in range(2):
        first = 3 * (1 - side)
        kv_ref[first, 0:48, :] = kv[48 * side : 48 * side + 48]
        kv_ref[first + 1, 0:96, :] = kv[96 + 96 * side : 192 + 96 * side]
        kv_ref[first + 2, 0:48, :] = kv[288 + 48 * side : 336 + 48 * side]

    def own(column, carry):
        rows = latent_ref[pl.ds(8 * column - 4, 8)].reshape(384, D)
        kv = project(rows, column)
        first = 3 + 3 * column
        kv_ref[first, 0:96, :] = kv[0:96]
        kv_ref[first + 1, 0:192, :] = kv[96:288]
        kv_ref[first + 2, 0:96, :] = kv[288:384]
        return carry

    lax.fori_loop(1, 4, own, 0)
    over_lev()

    key = lax.broadcasted_iota(jnp.int32, (1, 192), 1)
    odd_lane = lax.broadcasted_iota(jnp.int32, (1, 128), 1) >= HD

    def attend(column, window, row0, count, valid):
        for pair in range(HEADS // 2):
            lanes = slice(pair * 128, pair * 128 + 128)
            q = q_ref[column, row0 : row0 + count, lanes]
            nil = jnp.zeros_like(q)
            q2 = jnp.concatenate([jnp.where(odd_lane, nil, q), jnp.where(odd_lane, q, nil)], axis=0)
            expo = jnp.exp(dot(q2, kv_ref[window, :, lanes], 1, 1))
            if valid is not None:
                expo = jnp.where(valid, expo, 0.0)
            probs = (expo * (1.0 / jnp.sum(expo, axis=-1, keepdims=True))).astype(BF)
            both = dot(probs, kv_ref[window, :, D + pair * 128 : D + pair * 128 + 128])
            att_ref[column, row0 : row0 + count, lanes] = jnp.where(odd_lane, both[count:], both[:count]).astype(BF)

    inside = (edge_ref[0] == 0, edge_ref[1] == 0)
    plain = [(key < 96) | ok for ok in inside]
    corner = [(key < 48) | ((key < 144) & ((key + 16) % 32 < 16)) | ok for ok in inside]

    for side in range(2):
        first = 3 * (1 - side)
        attend(0, first, 48 * side, 48, corner[0])
        attend(0, first + 1, 96 + 96 * side, 96, None)
        attend(0, first + 2, 288 + 48 * side, 48, corner[1])
    gather()

    def column_loop(column, carry):
        first = 3 + 3 * column
        attend(column, first, 0, 96, plain[0])
        attend(column, first + 1, 96, 192, None)
        attend(column, first + 2, 288, 96, plain[1])
        return carry

    lax.fori_loop(1, 4, column_loop, 0)
    close(total_ref)


def finish_kernel(att_ref, latent_ref, wproj_ref, total_ref, we_ref, queries_ref, wkv_ref, out_ref, gembed_ref, gkv_ref, gout_ref, factor):
    back = permutation(384, 1)

    def finish(column, rows):
        natural = dot(back, att_ref[column]).astype(BF)
        return (rows.astype(F32) + dot(natural, wproj_ref[...])).astype(BF)

    rows = jnp.concatenate([latent_ref[28:32].reshape(192, D), latent_ref[0:4].reshape(192, D)], axis=0)
    done = finish(0, rows)
    out_ref[28:32] = done[:192].reshape(4, 3, 16, D)
    out_ref[0:4] = done[192:].reshape(4, 3, 16, D)

    def column_loop(column, carry):
        rows = latent_ref[pl.ds(8 * column - 4, 8)].reshape(384, D)
        out_ref[pl.ds(8 * column - 4, 8)] = finish(column, rows).reshape(8, 3, 16, D)
        return carry

    lax.fori_loop(1, 4, column_loop, 0)
    grads(total_ref, we_ref, queries_ref, wkv_ref, gembed_ref, gkv_ref, gout_ref, factor)


def grads(total_ref, we_ref, queries_ref, wkv_ref, gembed_ref, gkv_ref, gout_ref, factor):
    qm = query_rows(queries_ref[...].astype(F32)).astype(BF)
    for j in range(4):
        gout_ref[:, j * 128 : (j + 1) * 128] = total_ref[j * D : (j + 1) * D, :].astype(F32) * factor
    values = total_ref[4 * D : 5 * D, :]
    keys = dot(qm, total_ref[5 * D : 5 * D + 32, :][:24], 0, 0)
    khigh, klow = split(keys)
    we = we_ref[...]
    gkv_ref[:, :D] = (dot(we, khigh, 0, 1) + dot(we, klow, 0, 1)) * factor
    gkv_ref[:, D:] = dot(we, values, 0, 1) * factor
    wk, wv = wkv_ref[:, :D], wkv_ref[:, D:]
    grad = dot(khigh, wk, 0, 1) + dot(klow, wk, 0, 1) + dot(values, wv, 0, 1)
    gembed_ref[...] = grad[:F] * factor


def whole(shape, dtype):
    return jax.ShapeDtypeStruct(shape, dtype)


def params(**kw):
    return pltpu.CompilerParams(vmem_limit_bytes=VMEM_LIMIT, **kw)


def per_device(inputs, level_ids, level_table, w_embed, queries, w_kv, w_out, gain, w_qkv, w_proj, d_latent):
    band = lax.axis_index("lev")
    bands = lax.axis_size("lev")
    tiles = lax.axis_size("tile")
    lon_rows, lat_rows = d_latent.shape[:2]
    onehot = (level_ids[:, None] == jnp.arange(level_table.shape[0], dtype=jnp.int32)[None, :]).astype(BF)
    rows = jnp.dot(onehot, level_table, preferred_element_type=F32).astype(BF)
    we = jnp.concatenate([w_embed, rows, jnp.zeros((KX - F - LEVELS, D), BF)], axis=0)
    vmem = pl.BlockSpec(memory_space=pltpu.VMEM)
    d_nat = d_latent.transpose(0, 2, 1, 3)
    latent, terms, w2, woutp, far = pl.pallas_call(
        pool_kernel,
        in_specs=[vmem] * 6,
        out_specs=(vmem,) * 5,
        out_shape=(whole(d_nat.shape, BF), whole((TERMS, KX), BF), whole((MV, 2 * KX), BF), whole((D, D), BF), whole((LEVELS, F, 512), BF)),
        scratch_shapes=[
            pltpu.VMEM((LEVELS, D, 128), F32),
            pltpu.VMEM((D, 384), F32),
            pltpu.VMEM((D, 384), BF),
            pltpu.VMEM((LEVELS // 2, MV, 256), BF),
            pltpu.VMEM((MV, KX), F32),
            pltpu.VMEM((4 * D, 128), F32),
            pltpu.VMEM((F * 32, 128), F32),
            pltpu.VMEM((4 * F, 1024), BF),
            pltpu.VMEM((4 * F, 1024), BF),
            pltpu.VMEM((LEVELS, F, 512), BF),
            pltpu.VMEM((LEVELS, F, 256), BF),
            pltpu.VMEM((2, LEVELS, F, 128), BF),
            pltpu.VMEM((LEVELS, F, 512), BF),
            pltpu.VMEM((LEVELS, F, 512), BF),
            pltpu.SemaphoreType.DMA((30,)),
            pltpu.SemaphoreType.DMA((30,)),
        ],
        compiler_params=params(collective_id=2, has_side_effects=True),
        name="pool",
    )(inputs[0], d_nat, we, queries, w_kv, w_out)

    factor = 1.0 / math.sqrt(lon_rows * lat_rows * bands * tiles)
    edge = jnp.stack([band == 0, band == bands - 1]).astype(jnp.int32)
    att, total = pl.pallas_call(
        window_kernel,
        in_specs=[vmem, pl.BlockSpec(memory_space=pltpu.SMEM)] + [vmem] * 6,
        out_specs=(vmem, vmem),
        out_shape=(whole((4, 384, D), BF), whole((16, CHUNK, KX), BF)),
        scratch_shapes=[
            pltpu.VMEM((LEVELS, D, 128), F32),
            pltpu.VMEM((D, 384), BF),
            pltpu.VMEM((4, 384, D), BF),
            pltpu.VMEM((18, 192, 2 * D), BF),
            pltpu.VMEM((15, CHUNK, KX), BF),
            pltpu.VMEM((8, CHUNK, KX), BF),
            pltpu.VMEM((16, CHUNK, KX), BF),
            pltpu.SemaphoreType.DMA((37,)),
            pltpu.SemaphoreType.DMA((37,)),
        ],
        compiler_params=params(collective_id=1, has_side_effects=True),
        name="windows",
    )(terms.reshape(16, CHUNK, KX), edge, far, latent, w2, woutp, gain.reshape(1, D), w_qkv)

    out, gembed, gkv, gout = pl.pallas_call(
        functools.partial(finish_kernel, factor=factor),
        out_shape=(whole(d_nat.shape, BF), whole((F, D), F32), whole((D, 2 * D), F32), whole((D, D), F32)),
        compiler_params=params(),
        name="finish",
    )(att, latent, w_proj, total.reshape(TERMS, KX), we, queries, w_kv)
    return (out.transpose(0, 2, 1, 3), gembed, gkv, gout)


def solution(mesh):
    placed = (P("lev", None, "tile", None),) + (P(),) * 9 + (P("tile", "lev", None, None),)
    return jax.shard_map(
        per_device,
        mesh=mesh,
        in_specs=placed,
        out_specs=(P("tile", "lev", None, None), P(), P(), P()),
        check_vma=False,
    )
```

```python
import functools
import math

import jax
import jax.numpy as jnp
import numpy as np
from jax import lax
from jax.experimental import pallas as pl
from jax.experimental.pallas import tpu as pltpu
from jax.sharding import PartitionSpec as P

HD = 64
HEADS = 8
WIN = 8
D = 512
F = 80
LEVELS = 8
LATENT = 3
KX = 128
MV = 544
CHUNK = 176
TERMS = 16 * CHUNK
BF = jnp.bfloat16
F32 = jnp.float32
VMEM_LIMIT = 56 * 1024 * 1024


def dot(a, b, ca=1, cb=0):
    return lax.dot_general(a, b, (((ca,), (cb,)), ((), ())), preferred_element_type=F32)


def split(value):
    high = value.astype(BF)
    return high, (value - high.astype(F32)).astype(BF)


def place(lev, tile):
    return {"lev": lev, "tile": tile}


def remote(src, dst, send, recv, device):
    return pltpu.make_async_remote_copy(src_ref=src, dst_ref=dst, send_sem=send, recv_sem=recv, device_id=device, device_id_type=pl.DeviceIdType.MESH)


def query_rows(queries):
    rows = jnp.concatenate([jnp.broadcast_to(queries[q : q + 1], (HEADS, D)) for q in range(LATENT)], axis=0)
    head = lax.broadcasted_iota(jnp.int32, (LATENT * HEADS, D), 0) % HEADS
    lane = lax.broadcasted_iota(jnp.int32, (LATENT * HEADS, D), 1) // HD
    return jnp.where(head == lane, rows, 0.0)


def fold_weights(ids_ref, table_ref, embed_ref, queries_ref, wkv_ref, wout_ref, w2_ref, woutp_ref, we_ref):
    slab = lax.broadcasted_iota(jnp.int32, (16, 1), 0)
    wanted = jnp.full((16, 1), -1, jnp.int32)
    for l in range(LEVELS):
        wanted = jnp.where(slab == l, ids_ref[l], wanted)
    onehot = jnp.where(lax.broadcasted_iota(jnp.int32, (16, 16), 1) == wanted, 1.0, 0.0).astype(BF)
    we_ref[0:F, :] = embed_ref[...]
    we_ref[F : F + 16, :] = dot(onehot, table_ref[...]).astype(BF)
    we_ref[F + 16 :, :] = jnp.zeros((KX - F - 16, D), BF)
    row = lax.broadcasted_iota(jnp.int32, (D, D), 0)
    lane = lax.broadcasted_iota(jnp.int32, (D, D), 1)
    mix = jnp.where(lane == (row % HEADS) * HD + row // HEADS, 1.0, 0.0).astype(BF)
    we = we_ref[...]
    wv = dot(mix, wkv_ref[:, D:], 1, 1).astype(BF)
    woutp_ref[...] = dot(mix, wout_ref[...]).astype(BF)
    high, low = split(dot(wv, we, 1, 1))
    w2_ref[0:D, 0:KX] = high
    w2_ref[0:D, KX:] = low
    qm = query_rows(queries_ref[...].astype(F32)).astype(BF)
    shigh, slow = split(dot(qm, wkv_ref[:, :D], 1, 1) * (1.0 / math.sqrt(HD)))
    score = dot(shigh, we, 1, 1) + dot(slow, we, 1, 1)
    score = jnp.concatenate([score, jnp.zeros((MV - D - 24, KX), F32)], axis=0)
    high, low = split(score)
    w2_ref[D:MV, 0:KX] = high
    w2_ref[D:MV, KX:] = low


def level_rows(x, level):
    row = lax.broadcasted_iota(jnp.int32, (KX - F, 128), 0)
    ones = jnp.where(row == level, 1.0, 0.0).astype(BF)
    return jnp.concatenate([x, ones], axis=0)


def forward_levels(read, w2_ref, vals_ref):
    scores = []
    pairs = []
    for pair in range(LEVELS // 2):
        pixels = jnp.concatenate([level_rows(read(2 * pair), 2 * pair), level_rows(read(2 * pair + 1), 2 * pair + 1)], axis=1)
        pairs.append(pixels)
        out = dot(w2_ref[...], jnp.concatenate([pixels, pixels], axis=0))
        vals_ref[2 * pair] = out[:D, :128]
        vals_ref[2 * pair + 1] = out[:D, 128:]
        scores.append(out[D : D + 24, :128])
        scores.append(out[D : D + 24, 128:])
    expo = [jnp.exp(s) for s in scores]
    total = expo[0]
    for e in expo[1:]:
        total = total + e
    inverse = 1.0 / total
    return pairs, [(e * inverse).astype(BF).astype(F32) for e in expo]


def select(rows, lanes, want):
    row = lax.broadcasted_iota(jnp.int32, (rows, lanes), 0)
    return jnp.where(row == want, 1.0, 0.0).astype(BF)


def lane_ids(lanes, start=0):
    return lax.broadcasted_iota(jnp.int32, (1, lanes), 1) + start


def inside_row(lon, lat):
    return jnp.where((lat >= 0) & (lat < 128), lon * 128 + lat, -1)


def exchange_stages(x_ref, pixels_ref, xa_ref, xb_ref, own_ref, near_ref, side_ref, mine_ref, rim_ref, send_sem, recv_sem):
    lev, tile = lax.axis_index("lev"), lax.axis_index("tile")
    bands, tiles = lax.axis_size("lev"), lax.axis_size("tile")
    next_tile, last_tile = lax.rem(tile + 1, tiles), lax.rem(tile + tiles - 1, tiles)
    levs = [lax.rem(lev + off, bands) for off in range(bands)]

    def copy(src, dst, slot, device):
        return remote(src, dst, send_sem.at[slot], recv_sem.at[slot], device)

    own, near, east, west = [], [], [], []
    for off in range(1, bands):
        own.append(copy(own_ref.at[levs[off]], mine_ref.at[lev], off - 1, place(levs[off], tile)))
        near.append(copy(near_ref.at[levs[off]], rim_ref.at[lev, :, 256:512], off + 6, place(levs[off], tile)))
    for off in range(bands):
        east.append(copy(side_ref.at[0, levs[off]], rim_ref.at[lev, :, 0:128], 14 + off, place(levs[off], next_tile)))
        west.append(copy(side_ref.at[1, levs[off]], rim_ref.at[lev, :, 128:256], 22 + off, place(levs[off], last_tile)))

    def greet():
        barrier = pltpu.get_barrier_semaphore()
        for off in range(1, bands):
            pl.semaphore_signal(barrier, inc=1, device_id=place(levs[off], tile), device_id_type=pl.DeviceIdType.MESH)
        for off in range(bands):
            for side in (next_tile, last_tile):
                pl.semaphore_signal(barrier, inc=1, device_id=place(levs[off], side), device_id_type=pl.DeviceIdType.MESH)

    def send_own():
        pixels_ref[...] = x_ref[...].reshape(F * 32, 128).astype(F32)
        for lon in range(32):
            plane = pixels_ref[pl.ds(lon, F, stride=32), :].astype(BF)
            xa_ref[(lon // 8) * F : (lon // 8 + 1) * F, (lon % 8) * 128 : (lon % 8 + 1) * 128] = plane
            moved = (lon + 4) % 32
            xb_ref[(moved // 8) * F : (moved // 8 + 1) * F, (moved % 8) * 128 : (moved % 8 + 1) * 128] = plane
        rows = xa_ref[...]
        for two in range(bands // 2):
            j = lane_ids(256)
            want = ((j % 128) // 16) * 128 + 16 * (2 * two + j // 128) + j % 16
            out = dot(rows, select(1024, 256, want)).astype(BF)
            for c in range(4):
                for half in range(2):
                    own_ref[2 * two + half, :, c * 128 : (c + 1) * 128] = out[c * F : (c + 1) * F, half * 128 : (half + 1) * 128]
        pl.semaphore_wait(pltpu.get_barrier_semaphore(), 3 * bands - 1)
        for c in own:
            c.start()
        mine_ref[lev] = own_ref[lev]

    def sort_rim():
        rows = xb_ref[...]
        for four in range(2):
            j = lane_ids(256)
            band = 4 * four + j // 64
            lat = 16 * band + j % 4 + jnp.where(j % 64 < 32, -4, 16)
            out = dot(rows, select(1024, 256, inside_row((j % 32) // 4, lat))).astype(BF)
            for b in range(4):
                lanes = slice(64 * b, 64 * b + 64)
                for c in range(2):
                    pair = [out[k * F : (k + 1) * F, lanes] for k in (2 * c, 2 * c + 1)]
                    near_ref[4 * four + b, :, c * 128 : (c + 1) * 128] = jnp.concatenate(pair, axis=1)
        rows = jnp.concatenate([xb_ref[0:F, 0:512], xb_ref[0:F, 512:1024]], axis=0)
        for two in range(bands // 2):
            j = lane_ids(256)
            k = j % 128
            thin = k % 16
            wide = k - 32
            lat = jnp.where(k < 16, 4 + thin % 4, jnp.where(k < 32, thin % 4, jnp.where(k < 64, 8 + wide % 8, jnp.where(k < 80, 16 + thin % 4, 20 + thin % 4))))
            lon = jnp.where((k >= 32) & (k < 64), wide // 8, thin // 4)
            lat = jnp.where(k < 96, 16 * (2 * two + j // 128) - 4 + lat, -1)
            out = dot(rows, select(512, 256, inside_row(lon, lat))).astype(BF)
            for side in range(2):
                for half in range(2):
                    side_ref[side, 2 * two + half] = out[side * F : (side + 1) * F, half * 128 : (half + 1) * 128]
        rim_ref[lev, :, 256:512] = near_ref[lev]

    def take_own():
        for c in own:
            c.wait_recv()
        for c in near + east + west:
            c.start()

    def take_rim():
        for c in near + east + west:
            c.wait_recv()
        for c in own + near + east + west:
            c.wait_send()

    return greet, send_own, sort_rim, take_own, take_rim


def pool_kernel(ids_ref, x_ref, d_ref, table_ref, embed_ref, queries_ref, wkv_ref, wout_ref, latent_ref, terms_ref, w2_ref, woutp_ref, far_ref, we_ref, vals_ref, dpool_ref, pooled_ref, dv_ref, tacc_ref, gacc_ref, pixels_ref, xa_ref, xb_ref, own_ref, near_ref, side_ref, mine_ref, rim_ref, send_sem, recv_sem):
    greet, send_own, sort_rim, take_own, take_rim = exchange_stages(x_ref, pixels_ref, xa_ref, xb_ref, own_ref, near_ref, side_ref, mine_ref, rim_ref, send_sem, recv_sem)
    greet()
    send_own()
    sort_rim()
    fold_weights(ids_ref, table_ref, embed_ref, queries_ref, wkv_ref, wout_ref, w2_ref, woutp_ref, we_ref)
    tacc_ref[...] = jnp.zeros_like(tacc_ref)
    gacc_ref[...] = jnp.zeros_like(gacc_ref)
    take_own()

    def group_loop(group, carry):
        pool_group(group, mine_ref, d_ref, w2_ref, woutp_ref, latent_ref, vals_ref, dpool_ref, pooled_ref, dv_ref, tacc_ref, gacc_ref)
        return carry

    lax.fori_loop(0, 4, group_loop, 0)
    for h in range(HEADS):
        for j in range(4):
            terms_ref[j * D + h * HD : j * D + (h + 1) * HD, :] = gacc_ref[pl.ds(j * D + h, HD, stride=HEADS), :].astype(BF)
        terms_ref[4 * D + h * HD : 4 * D + (h + 1) * HD, :] = tacc_ref[pl.ds(h, HD, stride=HEADS), :].astype(BF)
    terms_ref[5 * D : 5 * D + MV - D, :] = tacc_ref[D:MV, :].astype(BF)
    terms_ref[5 * D + MV - D :, :] = jnp.zeros((TERMS - 5 * D - MV + D, KX), BF)
    take_rim()
    far_ref[...] = rim_ref[...]


def pool_group(group, x_ref, d_ref, w2_ref, woutp_ref, latent_ref, vals_ref, dpool_ref, pooled_ref, dv_ref, tacc_ref, gacc_ref):
    lane0 = pl.multiple_of(group * 128, 128)
    pairs, probs = forward_levels(lambda l: x_ref[l, :, pl.ds(lane0, 128)], w2_ref, vals_ref)
    d_rows = jnp.concatenate([d_ref[pl.ds(8 * group, 8), q].reshape(128, D) for q in range(LATENT)], axis=0)
    dpool_ref[...] = dot(woutp_ref[...], d_rows, 1, 1)
    parts = [[probs[l][q * HEADS : (q + 1) * HEADS] for q in range(LATENT)] for l in range(LEVELS)]

    def mix_loop(i, carry):
        base = pl.multiple_of(i * 16, 16)
        pooled = [[], [], []]
        dvals = [[] for _ in range(LEVELS)]
        for e in range(2):
            rows = pl.ds(base + 8 * e, 8)
            dq = [dpool_ref[rows, q * 128 : (q + 1) * 128] for q in range(LATENT)]
            acc = [None] * LATENT
            for l in range(LEVELS):
                v = vals_ref[l, rows, :]
                for q in range(LATENT):
                    term = parts[l][q] * v
                    acc[q] = term if acc[q] is None else acc[q] + term
                dvals[l].append(parts[l][0] * dq[0] + parts[l][1] * dq[1] + parts[l][2] * dq[2])
            for q in range(LATENT):
                pooled[q].append(acc[q])
        for q in range(LATENT):
            pooled_ref[pl.ds(base, 16), q * 128 : (q + 1) * 128] = jnp.concatenate(pooled[q], axis=0).astype(BF)
        for l in range(LEVELS):
            lanes = slice((l % 2) * 128, (l % 2) * 128 + 128)
            dv_ref[l // 2, pl.ds(base, 16), lanes] = jnp.concatenate(dvals[l], axis=0).astype(BF)
        return carry

    lax.fori_loop(0, D // 16, mix_loop, 0)

    def dprob_loop(i, carry):
        acc = list(carry)
        for e in range(2):
            rows = pl.ds(pl.multiple_of(i * 16 + 8 * e, 8), 8)
            dq = [dpool_ref[rows, q * 128 : (q + 1) * 128] for q in range(LATENT)]
            for l in range(LEVELS):
                v = vals_ref[l, rows, :]
                for q in range(LATENT):
                    acc[l * LATENT + q] = acc[l * LATENT + q] + dq[q] * v
        return tuple(acc)

    zero = jnp.zeros((HEADS, 128), F32)
    dprob = lax.fori_loop(0, D // 16, dprob_loop, (zero,) * (LEVELS * LATENT))
    scale = 1.0 / math.sqrt(HD)
    delta = []
    for q in range(LATENT):
        total = parts[0][q] * dprob[q]
        for l in range(1, LEVELS):
            total = total + parts[l][q] * dprob[l * LATENT + q]
        delta.append(total)
    for l in range(LEVELS):
        ds = [parts[l][q] * (dprob[l * LATENT + q] - delta[q]) * scale for q in range(LATENT)]
        lanes = slice((l % 2) * 128, (l % 2) * 128 + 128)
        dv_ref[l // 2, D:MV, lanes] = jnp.concatenate(ds + [zero], axis=0).astype(BF)

    terms = dot(dv_ref[0], pairs[0], 1, 1)
    for pair in range(1, LEVELS // 2):
        terms = terms + dot(dv_ref[pair], pairs[pair], 1, 1)
    tacc_ref[...] += terms
    pooled = pooled_ref[...]
    gterm = dot(pooled, d_rows)
    for j in range(4):
        gacc_ref[j * D : (j + 1) * D, :] += gterm[:, j * 128 : (j + 1) * 128]
    latent = dot(pooled, woutp_ref[...], 0, 0).astype(BF)
    for q in range(LATENT):
        latent_ref[pl.ds(8 * group, 8), q] = latent[q * 128 : (q + 1) * 128].reshape(8, 16, D)


def normalise(values, gain):
    mean = jnp.mean(values, axis=-1, keepdims=True)
    centred = values - mean
    var = jnp.mean(centred * centred, axis=-1, keepdims=True)
    return (centred * lax.rsqrt(var + 1e-05) * gain).astype(BF)


def window_index(column, wa):
    return column * 3 + wa


def permutation(rows, dim):
    dst = lax.broadcasted_iota(jnp.int32, (rows, rows), dim)
    src = lax.broadcasted_iota(jnp.int32, (rows, rows), 1 - dim)
    a = dst
    b = dst - 96
    c = dst - 288
    low = (a // 4) * 16 + a % 4
    mid = (b // 8) * 16 + 4 + b % 8
    high = (c // 4) * 16 + 12 + c % 4
    want = jnp.where(dst < 96, low, jnp.where(dst < 288, mid, high))
    return jnp.where(src == want, 1.0, 0.0).astype(BF)


def sum_stages(terms_ref, halves_ref, pair_ref, part_ref, band_ref, full_ref, send_sem, recv_sem):
    lev, tile = lax.axis_index("lev"), lax.axis_index("tile")
    bands, tiles = lax.axis_size("lev"), lax.axis_size("tile")
    groups = tiles // 2
    group, core = tile // 2, lax.rem(tile, 2)

    def copy(src, dst, slot, device):
        return remote(src, dst, send_sem.at[slot], recv_sem.at[slot], device)

    other = place(lev, 2 * group + 1 - core)
    lev_peers = [place(lax.rem(lev + off, bands), tile) for off in range(1, bands)]
    group_ids = [lax.rem(group + off, groups) for off in range(1, groups)]
    group_peers = [place(lev, 2 * g + core) for g in group_ids]
    swap = copy(terms_ref.at[1 - core], halves_ref, 0, other)
    first = [copy(pair_ref.at[g], part_ref.at[i], 1 + i, group_peers[i]) for i, g in enumerate(group_ids)]
    second = [copy(band_ref.at[lev], band_ref.at[lev], 8 + i, peer) for i, peer in enumerate(lev_peers)]
    third = [copy(full_ref.at[core, group], full_ref.at[core, group], 15 + i, peer) for i, peer in enumerate(group_peers)]
    back = copy(full_ref.at[core], full_ref.at[core], 22, other)

    def greet():
        barrier = pltpu.get_barrier_semaphore()
        for peer in group_peers + lev_peers + [other]:
            pl.semaphore_signal(barrier, inc=1, device_id=peer, device_id_type=pl.DeviceIdType.MESH)
        pl.semaphore_wait(barrier, groups + bands - 1)
        swap.start()

    def over_group():
        swap.wait_recv()
        pair_ref[...] = (terms_ref[core].astype(F32) + halves_ref[...].astype(F32)).astype(BF)
        for c in first:
            c.start()

    def over_lev():
        total = pair_ref[group].astype(F32)
        for i, c in enumerate(first):
            c.wait_recv()
            total = total + part_ref[i].astype(F32)
        band_ref[lev] = total.astype(BF)
        for c in second:
            c.start()

    def gather():
        for c in second:
            c.wait_recv()
        total = band_ref[0].astype(F32)
        for b in range(1, bands):
            total = total + band_ref[b].astype(F32)
        full_ref[core, group] = total.astype(BF)
        for c in third:
            c.start()

    def swap_back():
        for c in third:
            c.wait_recv()
        back.start()

    def close(total_ref):
        back.wait_recv()
        total_ref[...] = full_ref[...]
        for c in [swap] + first + second + third + [back]:
            c.wait_send()

    return greet, over_group, over_lev, gather, swap_back, close


def window_kernel(terms_ref, xh_ref, latent_ref, w2_ref, woutp_ref, gain_ref, wqkv_ref, wproj_ref, out_ref, total_ref, vals_ref, pooled_ref, q_ref, kv_ref, att_ref, halves_ref, pair_ref, part_ref, band_ref, full_ref, send_sem, recv_sem):
    gain = gain_ref[...]
    greet, over_group, over_lev, gather, swap_back, close = sum_stages(terms_ref, halves_ref, pair_ref, part_ref, band_ref, full_ref, send_sem, recv_sem)
    greet()

    def halo(group, carry):
        lane0 = pl.multiple_of(group * 128, 128)
        _, probs = forward_levels(lambda l: xh_ref[l, :, pl.ds(lane0, 128)], w2_ref, vals_ref)
        parts = [[probs[l][q * HEADS : (q + 1) * HEADS] for q in range(LATENT)] for l in range(LEVELS)]

        def mix_loop(i, inner):
            base = pl.multiple_of(i * 16, 16)
            pooled = [[], [], []]
            for e in range(2):
                rows = pl.ds(base + 8 * e, 8)
                acc = [None] * LATENT
                for l in range(LEVELS):
                    v = vals_ref[l, rows, :]
                    for q in range(LATENT):
                        term = parts[l][q] * v
                        acc[q] = term if acc[q] is None else acc[q] + term
                for q in range(LATENT):
                    pooled[q].append(acc[q])
            for q in range(LATENT):
                pooled_ref[pl.ds(base, 16), q * 128 : (q + 1) * 128] = jnp.concatenate(pooled[q], axis=0).astype(BF)
            return inner

        lax.fori_loop(0, D // 16, mix_loop, 0)
        latent = dot(pooled_ref[...], woutp_ref[...], 0, 0).astype(BF).astype(F32)
        normed = normalise(latent, gain)
        kv = dot(normed, wqkv_ref[:, D:]).astype(BF)

        @pl.when(group < 2)
        def _():
            first = group * 3
            for q in range(LATENT):
                row = q * 128
                kv_ref[first, 48 + 32 * q : 80 + 32 * q, :] = kv[row : row + 32]
                kv_ref[first + 1, 96 + 32 * q : 128 + 32 * q, :] = kv[row + 32 : row + 64]
                kv_ref[first + 2, 48 + 32 * q : 80 + 32 * q, :] = kv[row + 64 : row + 96]

        @pl.when(group == 2)
        def _():
            for q in range(LATENT):
                row = q * 128
                near = slice(144 + 16 * q, 160 + 16 * q)
                kv_ref[3, near, :] = kv[row : row + 16]
                kv_ref[0, near, :] = kv[row + 16 : row + 32]
                kv_ref[5, near, :] = kv[row + 32 : row + 48]
                kv_ref[2, near, :] = kv[row + 48 : row + 64]

        def column_rim(half, column):
            for q in range(LATENT):
                row = q * 128 + half * 64
                near = slice(96 + 32 * q, 128 + 32 * q)
                kv_ref[3 + 3 * column, near, :] = kv[row : row + 32]
                kv_ref[5 + 3 * column, near, :] = kv[row + 32 : row + 64]

        @pl.when(group == 2)
        def _():
            column_rim(1, 1)

        @pl.when(group == 3)
        def _():
            column_rim(0, 2)
            column_rim(1, 3)

        @pl.when(group == 0)
        def _():
            over_group()
        return carry

    lax.fori_loop(0, 4, halo, 0)
    over_lev()

    def project(rows, column):
        normed = normalise(rows.astype(F32), gain)
        normed = dot(permutation(384, 0), normed).astype(BF)
        q_ref[column] = (dot(normed, wqkv_ref[:, :D]).astype(BF).astype(F32) * (1.0 / math.sqrt(HD))).astype(BF)
        return dot(normed, wqkv_ref[:, D:]).astype(BF)

    rows = jnp.concatenate([latent_ref[28:32].reshape(192, D), latent_ref[0:4].reshape(192, D)], axis=0)
    kv = project(rows, 0)
    for side in range(2):
        first = 3 * (1 - side)
        kv_ref[first, 0:48, :] = kv[48 * side : 48 * side + 48]
        kv_ref[first + 1, 0:96, :] = kv[96 + 96 * side : 192 + 96 * side]
        kv_ref[first + 2, 0:48, :] = kv[288 + 48 * side : 336 + 48 * side]

    def own(column, carry):
        rows = latent_ref[pl.ds(8 * column - 4, 8)].reshape(384, D)
        kv = project(rows, column)
        first = 3 + 3 * column
        kv_ref[first, 0:96, :] = kv[0:96]
        kv_ref[first + 1, 0:192, :] = kv[96:288]
        kv_ref[first + 2, 0:96, :] = kv[288:384]
        return carry

    lax.fori_loop(1, 4, own, 0)
    gather()

    key = lax.broadcasted_iota(jnp.int32, (1, 192), 1)
    odd_lane = lax.broadcasted_iota(jnp.int32, (1, 128), 1) >= HD

    def attend(column, window, row0, count, valid):
        for pair in range(HEADS // 2):
            lanes = slice(pair * 128, pair * 128 + 128)
            q = q_ref[column, row0 : row0 + count, lanes]
            nil = jnp.zeros_like(q)
            q2 = jnp.concatenate([jnp.where(odd_lane, nil, q), jnp.where(odd_lane, q, nil)], axis=0)
            expo = jnp.exp(dot(q2, kv_ref[window, :, lanes], 1, 1))
            if valid is not None:
                expo = jnp.where(valid, expo, 0.0)
            probs = (expo * (1.0 / jnp.sum(expo, axis=-1, keepdims=True))).astype(BF)
            both = dot(probs, kv_ref[window, :, D + pair * 128 : D + pair * 128 + 128])
            att_ref[row0 : row0 + count, lanes] = jnp.where(odd_lane, both[count:], both[:count]).astype(BF)

    lev = lax.axis_index("lev")
    inside = (lev > 0, lev < lax.axis_size("lev") - 1)
    plain = [(key < 96) | ok for ok in inside]
    corner = [(key < 48) | ((key < 144) & ((key + 16) % 32 < 16)) | ok for ok in inside]

    for side in range(2):
        first = 3 * (1 - side)
        attend(0, first, 48 * side, 48, corner[0])
        attend(0, first + 1, 96 + 96 * side, 96, None)
        attend(0, first + 2, 288 + 48 * side, 48, corner[1])
    back = permutation(384, 1)

    def finish(rows):
        natural = dot(back, att_ref[...]).astype(BF)
        return (rows.astype(F32) + dot(natural, wproj_ref[...])).astype(BF)

    done = finish(rows)
    out_ref[28:32] = done[:192].reshape(4, 3, 16, D)
    out_ref[0:4] = done[192:].reshape(4, 3, 16, D)

    def column_loop(column, carry):
        first = 3 + 3 * column
        attend(column, first, 0, 96, plain[0])
        attend(column, first + 1, 96, 192, None)
        attend(column, first + 2, 288, 96, plain[1])
        rows = latent_ref[pl.ds(8 * column - 4, 8)].reshape(384, D)
        out_ref[pl.ds(8 * column - 4, 8)] = finish(rows).reshape(8, 3, 16, D)

        @pl.when(column == 2)
        def _():
            swap_back()

        return carry

    lax.fori_loop(1, 4, column_loop, 0)
    close(total_ref)


def finish_kernel(done_ref, total_ref, we_ref, queries_ref, wkv_ref, out_ref, gembed_ref, gkv_ref, gout_ref, sem, factor):
    copy = pltpu.make_async_copy(done_ref, out_ref, sem)
    copy.start()
    grads(total_ref, we_ref, queries_ref, wkv_ref, gembed_ref, gkv_ref, gout_ref, factor)
    copy.wait()


def grads(total_ref, we_ref, queries_ref, wkv_ref, gembed_ref, gkv_ref, gout_ref, factor):
    qm = query_rows(queries_ref[...].astype(F32)).astype(BF)
    for j in range(4):
        gout_ref[:, j * 128 : (j + 1) * 128] = total_ref[j * D : (j + 1) * D, :].astype(F32) * factor
    values = total_ref[4 * D : 5 * D, :]
    keys = dot(qm, total_ref[5 * D : 5 * D + 32, :][:24], 0, 0)
    khigh, klow = split(keys)
    we = we_ref[...]
    gkv_ref[:, :D] = (dot(we, khigh, 0, 1) + dot(we, klow, 0, 1)) * factor
    gkv_ref[:, D:] = dot(we, values, 0, 1) * factor
    wk, wv = wkv_ref[:, :D], wkv_ref[:, D:]
    grad = dot(khigh, wk, 0, 1) + dot(klow, wk, 0, 1) + dot(values, wv, 0, 1)
    gembed_ref[...] = grad[:F] * factor


def whole(shape, dtype):
    return jax.ShapeDtypeStruct(shape, dtype)


def params(**kw):
    return pltpu.CompilerParams(vmem_limit_bytes=VMEM_LIMIT, **kw)


def per_device(inputs, level_ids, level_table, w_embed, queries, w_kv, w_out, gain, w_qkv, w_proj, d_latent):
    bands = lax.axis_size("lev")
    tiles = lax.axis_size("tile")
    lon_rows, lat_rows = d_latent.shape[:2]
    table = jnp.pad(level_table, ((0, 16 - level_table.shape[0]), (0, 0)))
    vmem = pl.BlockSpec(memory_space=pltpu.VMEM)
    d_nat = d_latent.transpose(0, 2, 1, 3)
    latent, terms, w2, woutp, far, we = pl.pallas_call(
        pool_kernel,
        in_specs=[pl.BlockSpec(memory_space=pltpu.SMEM)] + [vmem] * 7,
        out_specs=(vmem,) * 6,
        out_shape=(whole(d_nat.shape, BF), whole((TERMS, KX), BF), whole((MV, 2 * KX), BF), whole((D, D), BF), whole((LEVELS, F, 512), BF), whole((KX, D), BF)),
        scratch_shapes=[
            pltpu.VMEM((LEVELS, D, 128), F32),
            pltpu.VMEM((D, 384), F32),
            pltpu.VMEM((D, 384), BF),
            pltpu.VMEM((LEVELS // 2, MV, 256), BF),
            pltpu.VMEM((MV, KX), F32),
            pltpu.VMEM((4 * D, 128), F32),
            pltpu.VMEM((F * 32, 128), F32),
            pltpu.VMEM((4 * F, 1024), BF),
            pltpu.VMEM((4 * F, 1024), BF),
            pltpu.VMEM((LEVELS, F, 512), BF),
            pltpu.VMEM((LEVELS, F, 256), BF),
            pltpu.VMEM((2, LEVELS, F, 128), BF),
            pltpu.VMEM((LEVELS, F, 512), BF),
            pltpu.VMEM((LEVELS, F, 512), BF),
            pltpu.SemaphoreType.DMA((30,)),
            pltpu.SemaphoreType.DMA((30,)),
        ],
        compiler_params=params(collective_id=2, has_side_effects=True),
        name="pool",
    )(level_ids, inputs[0], d_nat, table, w_embed, queries, w_kv, w_out)

    factor = 1.0 / math.sqrt(lon_rows * lat_rows * bands * tiles)
    done, total = pl.pallas_call(
        window_kernel,
        in_specs=[vmem] * 8,
        out_specs=(vmem, vmem),
        out_shape=(whole(d_nat.shape, BF), whole((2, 8, CHUNK, KX), BF)),
        scratch_shapes=[
            pltpu.VMEM((LEVELS, D, 128), F32),
            pltpu.VMEM((D, 384), BF),
            pltpu.VMEM((4, 384, D), BF),
            pltpu.VMEM((15, 192, 2 * D), BF),
            pltpu.VMEM((384, D), BF),
            pltpu.VMEM((8, CHUNK, KX), BF),
            pltpu.VMEM((8, CHUNK, KX), BF),
            pltpu.VMEM((7, CHUNK, KX), BF),
            pltpu.VMEM((8, CHUNK, KX), BF),
            pltpu.VMEM((2, 8, CHUNK, KX), BF),
            pltpu.SemaphoreType.DMA((23,)),
            pltpu.SemaphoreType.DMA((23,)),
        ],
        compiler_params=params(collective_id=1, has_side_effects=True),
        name="windows",
    )(terms.reshape(2, 8, CHUNK, KX), far, latent, w2, woutp, gain.reshape(1, D), w_qkv, w_proj)

    anywhere = pl.BlockSpec(memory_space=pl.ANY)
    out, gembed, gkv, gout = pl.pallas_call(
        functools.partial(finish_kernel, factor=factor),
        in_specs=[anywhere] + [vmem] * 4,
        out_specs=(anywhere, vmem, vmem, vmem),
        out_shape=(whole(d_nat.shape, BF), whole((F, D), F32), whole((D, 2 * D), F32), whole((D, D), F32)),
        scratch_shapes=[pltpu.SemaphoreType.DMA],
        compiler_params=params(),
        name="finish",
    )(done, total.reshape(TERMS, KX), we, queries, w_kv)
    return (out.transpose(0, 2, 1, 3), gembed, gkv, gout)


def solution(mesh):
    placed = (P("lev", None, "tile", None),) + (P(),) * 9 + (P("tile", "lev", None, None),)
    return jax.shard_map(
        per_device,
        mesh=mesh,
        in_specs=placed,
        out_specs=(P("tile", "lev", None, None), P(), P(), P()),
        check_vma=False,
    )
```

```python
import functools
import math

import jax
import jax.numpy as jnp
import numpy as np
from jax import lax
from jax.experimental import pallas as pl
from jax.experimental.pallas import tpu as pltpu
from jax.sharding import PartitionSpec as P

HD = 64
HEADS = 8
WIN = 8
D = 512
F = 80
LEVELS = 8
LATENT = 3
KX = 128
MV = 544
CHUNK = 176
UNROLL = 4
TERMS = 16 * CHUNK
BF = jnp.bfloat16
F32 = jnp.float32
VMEM_LIMIT = 56 * 1024 * 1024


def dot(a, b, ca=1, cb=0):
    return lax.dot_general(a, b, (((ca,), (cb,)), ((), ())), preferred_element_type=F32)


def split(value):
    high = value.astype(BF)
    return high, (value - high.astype(F32)).astype(BF)


def place(lev, tile):
    return {"lev": lev, "tile": tile}


def remote(src, dst, send, recv, device):
    return pltpu.make_async_remote_copy(src_ref=src, dst_ref=dst, send_sem=send, recv_sem=recv, device_id=device, device_id_type=pl.DeviceIdType.MESH)


def query_rows(queries):
    rows = jnp.concatenate([jnp.broadcast_to(queries[q : q + 1], (HEADS, D)) for q in range(LATENT)], axis=0)
    head = lax.broadcasted_iota(jnp.int32, (LATENT * HEADS, D), 0) % HEADS
    lane = lax.broadcasted_iota(jnp.int32, (LATENT * HEADS, D), 1) // HD
    return jnp.where(head == lane, rows, 0.0)


def fold_weights(ids_ref, table_ref, embed_ref, queries_ref, wkv_ref, wout_ref, w2_ref, woutp_ref, we_ref):
    slab = lax.broadcasted_iota(jnp.int32, (16, 1), 0)
    wanted = jnp.full((16, 1), -1, jnp.int32)
    for l in range(LEVELS):
        wanted = jnp.where(slab == l, ids_ref[l], wanted)
    rows = jnp.zeros((16, D), F32)
    for entry in range(table_ref.shape[0]):
        rows = jnp.where(wanted == entry, table_ref[entry : entry + 1, :].astype(F32), rows)
    we_ref[0:F, :] = embed_ref[...]
    we_ref[F : F + 16, :] = rows.astype(BF)
    we_ref[F + 16 :, :] = jnp.zeros((KX - F - 16, D), BF)
    row = lax.broadcasted_iota(jnp.int32, (D, 1), 0)
    lane = lax.broadcasted_iota(jnp.int32, (D, D), 1)
    mix = jnp.where(lane == (row % HEADS) * HD + row // HEADS, 1.0, 0.0).astype(BF)
    we = we_ref[...]
    wv = dot(mix, wkv_ref[:, D:], 1, 1).astype(BF)
    woutp_ref[...] = dot(mix, wout_ref[...]).astype(BF)
    high, low = split(dot(wv, we, 1, 1))
    w2_ref[0:D, 0:KX] = high
    w2_ref[0:D, KX:] = low
    qm = query_rows(queries_ref[...].astype(F32)).astype(BF)
    shigh, slow = split(dot(qm, wkv_ref[:, :D], 1, 1) * (1.0 / math.sqrt(HD)))
    score = dot(shigh, we, 1, 1) + dot(slow, we, 1, 1)
    score = jnp.concatenate([score, jnp.zeros((MV - D - 24, KX), F32)], axis=0)
    high, low = split(score)
    w2_ref[D:MV, 0:KX] = high
    w2_ref[D:MV, KX:] = low


def level_rows(x, level):
    row = lax.broadcasted_iota(jnp.int32, (KX - F, 128), 0)
    ones = jnp.where(row == level, 1.0, 0.0).astype(BF)
    return jnp.concatenate([x, ones], axis=0)


def forward_levels(read, w2_ref, vals_ref):
    scores = []
    pairs = []
    for pair in range(LEVELS // 2):
        pixels = jnp.concatenate([level_rows(read(2 * pair), 2 * pair), level_rows(read(2 * pair + 1), 2 * pair + 1)], axis=1)
        pairs.append(pixels)
        out = dot(w2_ref[...], jnp.concatenate([pixels, pixels], axis=0))
        vals_ref[2 * pair] = out[:D, :128]
        vals_ref[2 * pair + 1] = out[:D, 128:]
        scores.append(out[D : D + 24, :128])
        scores.append(out[D : D + 24, 128:])
    expo = [jnp.exp(s) for s in scores]
    total = expo[0]
    for e in expo[1:]:
        total = total + e
    inverse = 1.0 / total
    return pairs, [(e * inverse).astype(BF).astype(F32) for e in expo]


def select(rows, lanes, want):
    row = lax.broadcasted_iota(jnp.int32, (rows, lanes), 0)
    return jnp.where(row == want, 1.0, 0.0).astype(BF)


def lane_ids(lanes, start=0):
    return lax.broadcasted_iota(jnp.int32, (1, lanes), 1) + start


def inside_row(lon, lat):
    return jnp.where((lat >= 0) & (lat < 128), lon * 128 + lat, -1)


def exchange_stages(x_ref, pixels_ref, xa_ref, xb_ref, own_ref, near_ref, side_ref, mine_ref, rim_ref, send_sem, recv_sem):
    lev, tile = lax.axis_index("lev"), lax.axis_index("tile")
    bands, tiles = lax.axis_size("lev"), lax.axis_size("tile")
    next_tile, last_tile = lax.rem(tile + 1, tiles), lax.rem(tile + tiles - 1, tiles)
    levs = [lax.rem(lev + off, bands) for off in range(bands)]

    def copy(src, dst, slot, device):
        return remote(src, dst, send_sem.at[slot], recv_sem.at[slot], device)

    own, near, east, west = [], [], [], []
    for off in range(1, bands):
        own.append(lambda g, off=off: copy(own_ref.at[g, levs[off]], mine_ref.at[g, lev], 30 + g * 7 + off - 1, place(levs[off], tile)))
        near.append(copy(near_ref.at[levs[off]], rim_ref.at[lev, :, 256:512], off - 1, place(levs[off], tile)))
    for off in range(bands):
        east.append(copy(side_ref.at[0, levs[off]], rim_ref.at[lev, :, 0:128], 7 + off, place(levs[off], next_tile)))
        west.append(copy(side_ref.at[1, levs[off]], rim_ref.at[lev, :, 128:256], 15 + off, place(levs[off], last_tile)))

    def greet():
        barrier = pltpu.get_barrier_semaphore()
        for off in range(1, bands):
            pl.semaphore_signal(barrier, inc=1, device_id=place(levs[off], tile), device_id_type=pl.DeviceIdType.MESH)
        for off in range(bands):
            for side in (next_tile, last_tile):
                pl.semaphore_signal(barrier, inc=1, device_id=place(levs[off], side), device_id_type=pl.DeviceIdType.MESH)

    def send_own():
        pixels_ref[...] = x_ref[...].reshape(F * 32, 128).astype(F32)
        for lon in range(32):
            plane = pixels_ref[pl.ds(lon, F, stride=32), :].astype(BF)
            xa_ref[(lon // 8) * F : (lon // 8 + 1) * F, (lon % 8) * 128 : (lon % 8 + 1) * 128] = plane
            moved = (lon + 4) % 32
            xb_ref[(moved // 8) * F : (moved // 8 + 1) * F, (moved % 8) * 128 : (moved % 8 + 1) * 128] = plane
        rows = xa_ref[...]
        for two in range(bands // 2):
            j = lane_ids(256)
            want = ((j % 128) // 16) * 128 + 16 * (2 * two + j // 128) + j % 16
            out = dot(rows, select(1024, 256, want)).astype(BF)
            for c in range(4):
                for half in range(2):
                    own_ref[c, 2 * two + half] = out[c * F : (c + 1) * F, half * 128 : (half + 1) * 128]
        pl.semaphore_wait(pltpu.get_barrier_semaphore(), 3 * bands - 1)
        for g in range(4):
            for c in own:
                c(g).start()
        for g in range(4):
            mine_ref[g, lev] = own_ref[g, lev]

    def sort_rim():
        rows = xb_ref[...]
        for four in range(2):
            j = lane_ids(256)
            band = 4 * four + j // 64
            lat = 16 * band + j % 4 + jnp.where(j % 64 < 32, -4, 16)
            out = dot(rows, select(1024, 256, inside_row((j % 32) // 4, lat))).astype(BF)
            for b in range(4):
                lanes = slice(64 * b, 64 * b + 64)
                for c in range(2):
                    pair = [out[k * F : (k + 1) * F, lanes] for k in (2 * c, 2 * c + 1)]
                    near_ref[4 * four + b, :, c * 128 : (c + 1) * 128] = jnp.concatenate(pair, axis=1)
        rows = jnp.concatenate([xb_ref[0:F, 0:512], xb_ref[0:F, 512:1024]], axis=0)
        for two in range(bands // 2):
            j = lane_ids(256)
            k = j % 128
            thin = k % 16
            wide = k - 32
            lat = jnp.where(k < 16, 4 + thin % 4, jnp.where(k < 32, thin % 4, jnp.where(k < 64, 8 + wide % 8, jnp.where(k < 80, 16 + thin % 4, 20 + thin % 4))))
            lon = jnp.where((k >= 32) & (k < 64), wide // 8, thin // 4)
            lat = jnp.where(k < 96, 16 * (2 * two + j // 128) - 4 + lat, -1)
            out = dot(rows, select(512, 256, inside_row(lon, lat))).astype(BF)
            for side in range(2):
                for half in range(2):
                    side_ref[side, 2 * two + half] = out[side * F : (side + 1) * F, half * 128 : (half + 1) * 128]
        rim_ref[lev, :, 256:512] = near_ref[lev]

    def take_own(group):
        for c in own:
            c(group).wait_recv()

        @pl.when(group == 1)
        def _():
            for c in near + east + west:
                c.start()

    def take_rim():
        for c in near + east + west:
            c.wait_recv()
        for c in near + east + west + [c(g) for c in own for g in range(4)]:
            c.wait_send()

    return greet, send_own, sort_rim, take_own, take_rim


def pool_kernel(ids_ref, x_ref, d_ref, table_ref, embed_ref, queries_ref, wkv_ref, wout_ref, latent_ref, terms_ref, w2_ref, woutp_ref, far_ref, we_ref, vals_ref, dpool_ref, pooled_ref, dv_ref, tacc_ref, gacc_ref, pixels_ref, xa_ref, xb_ref, own_ref, near_ref, side_ref, mine_ref, rim_ref, send_sem, recv_sem):
    greet, send_own, sort_rim, take_own, take_rim = exchange_stages(x_ref, pixels_ref, xa_ref, xb_ref, own_ref, near_ref, side_ref, mine_ref, rim_ref, send_sem, recv_sem)
    greet()
    send_own()
    sort_rim()
    fold_weights(ids_ref, table_ref, embed_ref, queries_ref, wkv_ref, wout_ref, w2_ref, woutp_ref, we_ref)
    tacc_ref[...] = jnp.zeros_like(tacc_ref)
    gacc_ref[...] = jnp.zeros_like(gacc_ref)

    def group_loop(group, carry):
        take_own(group)
        pool_group(group, mine_ref, d_ref, w2_ref, woutp_ref, latent_ref, vals_ref, dpool_ref, pooled_ref, dv_ref, tacc_ref, gacc_ref)
        return carry

    lax.fori_loop(0, 4, group_loop, 0)
    for h in range(HEADS):
        for j in range(4):
            terms_ref[j * D + h * HD : j * D + (h + 1) * HD, :] = gacc_ref[pl.ds(j * D + h, HD, stride=HEADS), :].astype(BF)
        terms_ref[4 * D + h * HD : 4 * D + (h + 1) * HD, :] = tacc_ref[pl.ds(h, HD, stride=HEADS), :].astype(BF)
    terms_ref[5 * D : 5 * D + MV - D, :] = tacc_ref[D:MV, :].astype(BF)
    terms_ref[5 * D + MV - D :, :] = jnp.zeros((TERMS - 5 * D - MV + D, KX), BF)
    take_rim()
    far_ref[...] = rim_ref[...]


def pool_group(group, x_ref, d_ref, w2_ref, woutp_ref, latent_ref, vals_ref, dpool_ref, pooled_ref, dv_ref, tacc_ref, gacc_ref):
    pairs, probs = forward_levels(lambda l: x_ref[group, l], w2_ref, vals_ref)
    d_rows = jnp.concatenate([d_ref[pl.ds(8 * group, 8), q].reshape(128, D) for q in range(LATENT)], axis=0)
    dpool_ref[...] = dot(woutp_ref[...], d_rows, 1, 1)
    parts = [[probs[l][q * HEADS : (q + 1) * HEADS] for q in range(LATENT)] for l in range(LEVELS)]

    def mix_loop(i, carry):
        base = pl.multiple_of(i * 16, 16)
        pooled = [[], [], []]
        dvals = [[] for _ in range(LEVELS)]
        for e in range(2):
            rows = pl.ds(base + 8 * e, 8)
            dq = [dpool_ref[rows, q * 128 : (q + 1) * 128] for q in range(LATENT)]
            acc = [None] * LATENT
            for l in range(LEVELS):
                v = vals_ref[l, rows, :]
                for q in range(LATENT):
                    term = parts[l][q] * v
                    acc[q] = term if acc[q] is None else acc[q] + term
                dvals[l].append(parts[l][0] * dq[0] + parts[l][1] * dq[1] + parts[l][2] * dq[2])
            for q in range(LATENT):
                pooled[q].append(acc[q])
        for q in range(LATENT):
            pooled_ref[pl.ds(base, 16), q * 128 : (q + 1) * 128] = jnp.concatenate(pooled[q], axis=0).astype(BF)
        for l in range(LEVELS):
            lanes = slice((l % 2) * 128, (l % 2) * 128 + 128)
            dv_ref[l // 2, pl.ds(base, 16), lanes] = jnp.concatenate(dvals[l], axis=0).astype(BF)
        return carry

    lax.fori_loop(0, D // 16, mix_loop, 0, unroll=UNROLL)

    def dprob_loop(i, carry):
        acc = list(carry)
        for e in range(2):
            rows = pl.ds(pl.multiple_of(i * 16 + 8 * e, 8), 8)
            dq = [dpool_ref[rows, q * 128 : (q + 1) * 128] for q in range(LATENT)]
            for l in range(LEVELS):
                v = vals_ref[l, rows, :]
                for q in range(LATENT):
                    acc[l * LATENT + q] = acc[l * LATENT + q] + dq[q] * v
        return tuple(acc)

    zero = jnp.zeros((HEADS, 128), F32)
    dprob = lax.fori_loop(0, D // 16, dprob_loop, (zero,) * (LEVELS * LATENT), unroll=UNROLL)
    scale = 1.0 / math.sqrt(HD)
    delta = []
    for q in range(LATENT):
        total = parts[0][q] * dprob[q]
        for l in range(1, LEVELS):
            total = total + parts[l][q] * dprob[l * LATENT + q]
        delta.append(total)
    for l in range(LEVELS):
        ds = [parts[l][q] * (dprob[l * LATENT + q] - delta[q]) * scale for q in range(LATENT)]
        lanes = slice((l % 2) * 128, (l % 2) * 128 + 128)
        dv_ref[l // 2, D:MV, lanes] = jnp.concatenate(ds + [zero], axis=0).astype(BF)

    terms = dot(dv_ref[0], pairs[0], 1, 1)
    for pair in range(1, LEVELS // 2):
        terms = terms + dot(dv_ref[pair], pairs[pair], 1, 1)
    tacc_ref[...] += terms
    pooled = pooled_ref[...]
    gterm = dot(pooled, d_rows)
    for j in range(4):
        gacc_ref[j * D : (j + 1) * D, :] += gterm[:, j * 128 : (j + 1) * 128]
    latent = dot(pooled, woutp_ref[...], 0, 0).astype(BF)
    for q in range(LATENT):
        latent_ref[pl.ds(8 * group, 8), q] = latent[q * 128 : (q + 1) * 128].reshape(8, 16, D)


def normalise(values, gain):
    mean = jnp.mean(values, axis=-1, keepdims=True)
    centred = values - mean
    var = jnp.mean(centred * centred, axis=-1, keepdims=True)
    return (centred * lax.rsqrt(var + 1e-05) * gain).astype(BF)


def permutation(dim):
    dst = lax.broadcasted_iota(jnp.int32, (384, 1) if dim == 0 else (1, 384), dim)
    src = lax.broadcasted_iota(jnp.int32, (384, 384), 1 - dim)
    mid, high = dst - 96, dst - 288
    low = (dst // 4) * 16 + dst % 4
    mid = (mid // 8) * 16 + 4 + mid % 8
    high = (high // 4) * 16 + 12 + high % 4
    want = jnp.where(dst < 96, low, jnp.where(dst < 288, mid, high))
    return jnp.where(src == want, 1.0, 0.0).astype(BF)


def sum_stages(terms_ref, halves_ref, pair_ref, part_ref, band_ref, full_ref, send_sem, recv_sem):
    lev, tile = lax.axis_index("lev"), lax.axis_index("tile")
    bands, tiles = lax.axis_size("lev"), lax.axis_size("tile")
    groups = tiles // 2
    group, core = tile // 2, lax.rem(tile, 2)

    def copy(src, dst, slot, device):
        return remote(src, dst, send_sem.at[slot], recv_sem.at[slot], device)

    other = place(lev, 2 * group + 1 - core)
    lev_peers = [place(lax.rem(lev + off, bands), tile) for off in range(1, bands)]
    group_ids = [lax.rem(group + off, groups) for off in range(1, groups)]
    group_peers = [place(lev, 2 * g + core) for g in group_ids]
    swap = copy(terms_ref.at[1 - core], halves_ref, 0, other)
    first = [copy(pair_ref.at[g], part_ref.at[i], 1 + i, group_peers[i]) for i, g in enumerate(group_ids)]
    second = [copy(band_ref.at[lev], band_ref.at[lev], 8 + i, peer) for i, peer in enumerate(lev_peers)]
    third = [copy(full_ref.at[core, group], full_ref.at[core, group], 15 + i, peer) for i, peer in enumerate(group_peers)]
    back = copy(full_ref.at[core], full_ref.at[core], 22, other)

    def greet():
        barrier = pltpu.get_barrier_semaphore()
        for peer in group_peers + lev_peers + [other]:
            pl.semaphore_signal(barrier, inc=1, device_id=peer, device_id_type=pl.DeviceIdType.MESH)
        pl.semaphore_wait(barrier, groups + bands - 1)
        swap.start()

    def over_group():
        swap.wait_recv()
        pair_ref[...] = (terms_ref[core].astype(F32) + halves_ref[...].astype(F32)).astype(BF)
        for c in first:
            c.start()

    def over_lev():
        total = pair_ref[group].astype(F32)
        for i, c in enumerate(first):
            c.wait_recv()
            total = total + part_ref[i].astype(F32)
        band_ref[lev] = total.astype(BF)
        for c in second:
            c.start()

    def gather():
        for c in second:
            c.wait_recv()
        total = band_ref[0].astype(F32)
        for b in range(1, bands):
            total = total + band_ref[b].astype(F32)
        full_ref[core, group] = total.astype(BF)
        for c in third:
            c.start()

    def swap_back():
        for c in third:
            c.wait_recv()
        back.start()

    def close(total_ref):
        back.wait_recv()
        total_ref[...] = full_ref[...]
        for c in [swap] + first + second + third + [back]:
            c.wait_send()

    return greet, over_group, over_lev, gather, swap_back, close


def window_kernel(terms_ref, xh_ref, latent_ref, w2_ref, woutp_ref, gain_ref, wqkv_ref, wproj_ref, out_ref, total_ref, vals_ref, pooled_ref, q_ref, kv_ref, att_ref, perm_ref, halves_ref, pair_ref, part_ref, band_ref, full_ref, send_sem, recv_sem):
    gain = gain_ref[...]
    greet, over_group, over_lev, gather, swap_back, close = sum_stages(terms_ref, halves_ref, pair_ref, part_ref, band_ref, full_ref, send_sem, recv_sem)
    greet()
    perm_ref[0] = permutation(0)
    perm_ref[1] = permutation(1)

    def halo(group, carry):
        lane0 = pl.multiple_of(group * 128, 128)
        _, probs = forward_levels(lambda l: xh_ref[l, :, pl.ds(lane0, 128)], w2_ref, vals_ref)
        parts = [[probs[l][q * HEADS : (q + 1) * HEADS] for q in range(LATENT)] for l in range(LEVELS)]

        def mix_loop(i, inner):
            base = pl.multiple_of(i * 16, 16)
            pooled = [[], [], []]
            for e in range(2):
                rows = pl.ds(base + 8 * e, 8)
                acc = [None] * LATENT
                for l in range(LEVELS):
                    v = vals_ref[l, rows, :]
                    for q in range(LATENT):
                        term = parts[l][q] * v
                        acc[q] = term if acc[q] is None else acc[q] + term
                for q in range(LATENT):
                    pooled[q].append(acc[q])
            for q in range(LATENT):
                pooled_ref[pl.ds(base, 16), q * 128 : (q + 1) * 128] = jnp.concatenate(pooled[q], axis=0).astype(BF)
            return inner

        lax.fori_loop(0, D // 16, mix_loop, 0, unroll=UNROLL)
        latent = dot(pooled_ref[...], woutp_ref[...], 0, 0).astype(BF).astype(F32)
        normed = normalise(latent, gain)
        kv = dot(normed, wqkv_ref[:, D:]).astype(BF)

        @pl.when(group < 2)
        def _():
            first = group * 3
            for q in range(LATENT):
                row = q * 128
                kv_ref[first, 48 + 32 * q : 80 + 32 * q, :] = kv[row : row + 32]
                kv_ref[first + 1, 96 + 32 * q : 128 + 32 * q, :] = kv[row + 32 : row + 64]
                kv_ref[first + 2, 48 + 32 * q : 80 + 32 * q, :] = kv[row + 64 : row + 96]

        @pl.when(group == 2)
        def _():
            for q in range(LATENT):
                row = q * 128
                near = slice(144 + 16 * q, 160 + 16 * q)
                kv_ref[3, near, :] = kv[row : row + 16]
                kv_ref[0, near, :] = kv[row + 16 : row + 32]
                kv_ref[5, near, :] = kv[row + 32 : row + 48]
                kv_ref[2, near, :] = kv[row + 48 : row + 64]

        def column_rim(half, column):
            for q in range(LATENT):
                row = q * 128 + half * 64
                near = slice(96 + 32 * q, 128 + 32 * q)
                kv_ref[3 + 3 * column, near, :] = kv[row : row + 32]
                kv_ref[5 + 3 * column, near, :] = kv[row + 32 : row + 64]

        @pl.when(group == 2)
        def _():
            column_rim(1, 1)

        @pl.when(group == 3)
        def _():
            column_rim(0, 2)
            column_rim(1, 3)

        @pl.when(group == 0)
        def _():
            over_group()
        return carry

    lax.fori_loop(0, 4, halo, 0)
    over_lev()

    def project(rows, column):
        normed = normalise(rows.astype(F32), gain)
        normed = dot(perm_ref[0], normed).astype(BF)
        q_ref[column] = (dot(normed, wqkv_ref[:, :D]).astype(BF).astype(F32) * (1.0 / math.sqrt(HD))).astype(BF)
        return dot(normed, wqkv_ref[:, D:]).astype(BF)

    rows = jnp.concatenate([latent_ref[28:32].reshape(192, D), latent_ref[0:4].reshape(192, D)], axis=0)
    kv = project(rows, 0)
    for side in range(2):
        first = 3 * (1 - side)
        kv_ref[first, 0:48, :] = kv[48 * side : 48 * side + 48]
        kv_ref[first + 1, 0:96, :] = kv[96 + 96 * side : 192 + 96 * side]
        kv_ref[first + 2, 0:48, :] = kv[288 + 48 * side : 336 + 48 * side]

    def own(column, carry):
        rows = latent_ref[pl.ds(8 * column - 4, 8)].reshape(384, D)
        kv = project(rows, column)
        first = 3 + 3 * column
        kv_ref[first, 0:96, :] = kv[0:96]
        kv_ref[first + 1, 0:192, :] = kv[96:288]
        kv_ref[first + 2, 0:96, :] = kv[288:384]
        return carry

    lax.fori_loop(1, 4, own, 0)
    gather()

    key = lax.broadcasted_iota(jnp.int32, (1, 192), 1)
    odd_lane = lax.broadcasted_iota(jnp.int32, (1, 128), 1) >= HD

    def attend(column, window, row0, count, valid):
        for pair in range(HEADS // 2):
            lanes = slice(pair * 128, pair * 128 + 128)
            q = q_ref[column, row0 : row0 + count, lanes]
            nil = jnp.zeros_like(q)
            q2 = jnp.concatenate([jnp.where(odd_lane, nil, q), jnp.where(odd_lane, q, nil)], axis=0)
            expo = jnp.exp(dot(q2, kv_ref[window, :, lanes], 1, 1))
            if valid is not None:
                expo = jnp.where(valid, expo, 0.0)
            probs = (expo * (1.0 / jnp.sum(expo, axis=-1, keepdims=True))).astype(BF)
            both = dot(probs, kv_ref[window, :, D + pair * 128 : D + pair * 128 + 128])
            att_ref[row0 : row0 + count, lanes] = jnp.where(odd_lane, both[count:], both[:count]).astype(BF)

    lev = lax.axis_index("lev")
    inside = (lev > 0, lev < lax.axis_size("lev") - 1)
    plain = [(key < 96) | ok for ok in inside]
    corner = [(key < 48) | ((key < 144) & ((key + 16) % 32 < 16)) | ok for ok in inside]

    for side in range(2):
        first = 3 * (1 - side)
        attend(0, first, 48 * side, 48, corner[0])
        attend(0, first + 1, 96 + 96 * side, 96, None)
        attend(0, first + 2, 288 + 48 * side, 48, corner[1])

    def finish(rows):
        natural = dot(perm_ref[1], att_ref[...]).astype(BF)
        return (rows.astype(F32) + dot(natural, wproj_ref[...])).astype(BF)

    done = finish(rows)
    out_ref[28:32] = done[:192].reshape(4, 3, 16, D)
    out_ref[0:4] = done[192:].reshape(4, 3, 16, D)

    def column_loop(column, carry):
        first = 3 + 3 * column
        attend(column, first, 0, 96, plain[0])
        attend(column, first + 1, 96, 192, None)
        attend(column, first + 2, 288, 96, plain[1])
        rows = latent_ref[pl.ds(8 * column - 4, 8)].reshape(384, D)
        out_ref[pl.ds(8 * column - 4, 8)] = finish(rows).reshape(8, 3, 16, D)

        @pl.when(column == 2)
        def _():
            swap_back()

        return carry

    lax.fori_loop(1, 4, column_loop, 0)
    close(total_ref)


def finish_kernel(done_ref, total_ref, we_ref, queries_ref, wkv_ref, out_ref, gembed_ref, gkv_ref, gout_ref, sem, factor):
    copy = pltpu.make_async_copy(done_ref, out_ref, sem)
    copy.start()
    grads(total_ref, we_ref, queries_ref, wkv_ref, gembed_ref, gkv_ref, gout_ref, factor)
    copy.wait()


def grads(total_ref, we_ref, queries_ref, wkv_ref, gembed_ref, gkv_ref, gout_ref, factor):
    qm = query_rows(queries_ref[...].astype(F32)).astype(BF)
    for j in range(4):
        gout_ref[:, j * 128 : (j + 1) * 128] = total_ref[j * D : (j + 1) * D, :].astype(F32) * factor
    values = total_ref[4 * D : 5 * D, :]
    keys = dot(qm, total_ref[5 * D : 5 * D + 32, :][:24], 0, 0)
    khigh, klow = split(keys)
    we = we_ref[...]
    gkv_ref[:, :D] = (dot(we, khigh, 0, 1) + dot(we, klow, 0, 1)) * factor
    gkv_ref[:, D:] = dot(we, values, 0, 1) * factor
    wk, wv = wkv_ref[:, :D], wkv_ref[:, D:]
    grad = dot(khigh, wk, 0, 1) + dot(klow, wk, 0, 1) + dot(values, wv, 0, 1)
    gembed_ref[...] = grad[:F] * factor


def whole(shape, dtype):
    return jax.ShapeDtypeStruct(shape, dtype)


def params(**kw):
    return pltpu.CompilerParams(vmem_limit_bytes=VMEM_LIMIT, **kw)


def per_device(inputs, level_ids, level_table, w_embed, queries, w_kv, w_out, gain, w_qkv, w_proj, d_latent):
    bands = lax.axis_size("lev")
    tiles = lax.axis_size("tile")
    lon_rows, lat_rows = d_latent.shape[:2]
    vmem = pl.BlockSpec(memory_space=pltpu.VMEM)
    d_nat = d_latent.transpose(0, 2, 1, 3)
    latent, terms, w2, woutp, far, we = pl.pallas_call(
        pool_kernel,
        in_specs=[pl.BlockSpec(memory_space=pltpu.SMEM)] + [vmem] * 7,
        out_specs=(vmem,) * 6,
        out_shape=(whole(d_nat.shape, BF), whole((TERMS, KX), BF), whole((MV, 2 * KX), BF), whole((D, D), BF), whole((LEVELS, F, 512), BF), whole((KX, D), BF)),
        scratch_shapes=[
            pltpu.VMEM((LEVELS, D, 128), F32),
            pltpu.VMEM((D, 384), F32),
            pltpu.VMEM((D, 384), BF),
            pltpu.VMEM((LEVELS // 2, MV, 256), BF),
            pltpu.VMEM((MV, KX), F32),
            pltpu.VMEM((4 * D, 128), F32),
            pltpu.VMEM((F * 32, 128), F32),
            pltpu.VMEM((4 * F, 1024), BF),
            pltpu.VMEM((4 * F, 1024), BF),
            pltpu.VMEM((4, LEVELS, F, 128), BF),
            pltpu.VMEM((LEVELS, F, 256), BF),
            pltpu.VMEM((2, LEVELS, F, 128), BF),
            pltpu.VMEM((4, LEVELS, F, 128), BF),
            pltpu.VMEM((LEVELS, F, 512), BF),
            pltpu.SemaphoreType.DMA((58,)),
            pltpu.SemaphoreType.DMA((58,)),
        ],
        compiler_params=params(collective_id=2, has_side_effects=True),
        name="pool",
    )(level_ids, inputs[0], d_nat, level_table, w_embed, queries, w_kv, w_out)

    factor = 1.0 / math.sqrt(lon_rows * lat_rows * bands * tiles)
    done, total = pl.pallas_call(
        window_kernel,
        in_specs=[vmem] * 8,
        out_specs=(vmem, vmem),
        out_shape=(whole(d_nat.shape, BF), whole((2, 8, CHUNK, KX), BF)),
        scratch_shapes=[
            pltpu.VMEM((LEVELS, D, 128), F32),
            pltpu.VMEM((D, 384), BF),
            pltpu.VMEM((4, 384, D), BF),
            pltpu.VMEM((15, 192, 2 * D), BF),
            pltpu.VMEM((384, D), BF),
            pltpu.VMEM((2, 384, 384), BF),
            pltpu.VMEM((8, CHUNK, KX), BF),
            pltpu.VMEM((8, CHUNK, KX), BF),
            pltpu.VMEM((7, CHUNK, KX), BF),
            pltpu.VMEM((8, CHUNK, KX), BF),
            pltpu.VMEM((2, 8, CHUNK, KX), BF),
            pltpu.SemaphoreType.DMA((23,)),
            pltpu.SemaphoreType.DMA((23,)),
        ],
        compiler_params=params(collective_id=1, has_side_effects=True),
        name="windows",
    )(terms.reshape(2, 8, CHUNK, KX), far, latent, w2, woutp, gain.reshape(1, D), w_qkv, w_proj)

    anywhere = pl.BlockSpec(memory_space=pl.ANY)
    out, gembed, gkv, gout = pl.pallas_call(
        functools.partial(finish_kernel, factor=factor),
        in_specs=[vmem] * 5,
        out_specs=(anywhere, vmem, vmem, vmem),
        out_shape=(whole(d_nat.shape, BF), whole((F, D), F32), whole((D, 2 * D), F32), whole((D, D), F32)),
        scratch_shapes=[pltpu.SemaphoreType.DMA],
        compiler_params=params(),
        name="finish",
    )(done, total.reshape(TERMS, KX), we, queries, w_kv)
    return (out.transpose(0, 2, 1, 3), gembed, gkv, gout)


def solution(mesh):
    placed = (P("lev", None, "tile", None),) + (P(),) * 9 + (P("tile", "lev", None, None),)
    return jax.shard_map(
        per_device,
        mesh=mesh,
        in_specs=placed,
        out_specs=(P("tile", "lev", None, None), P(), P(), P()),
        check_vma=False,
    )
```

```python
import functools
import math

import jax
import jax.numpy as jnp
import numpy as np
from jax import lax
from jax.experimental import pallas as pl
from jax.experimental.pallas import tpu as pltpu
from jax.sharding import PartitionSpec as P

HD = 64
HEADS = 8
WIN = 8
D = 512
F = 80
LEVELS = 8
LATENT = 3
KX = 128
MV = 544
CHUNK = 176
UNROLL = 4
TERMS = 16 * CHUNK
BF = jnp.bfloat16
F32 = jnp.float32
VMEM_LIMIT = 56 * 1024 * 1024


def dot(a, b, ca=1, cb=0):
    return lax.dot_general(a, b, (((ca,), (cb,)), ((), ())), preferred_element_type=F32)


def split(value):
    high = value.astype(BF)
    return high, (value - high.astype(F32)).astype(BF)


def place(lev, tile):
    return {"lev": lev, "tile": tile}


def remote(src, dst, send, recv, device):
    return pltpu.make_async_remote_copy(src_ref=src, dst_ref=dst, send_sem=send, recv_sem=recv, device_id=device, device_id_type=pl.DeviceIdType.MESH)


def fetch(pairs, sems):
    loads = [pltpu.make_async_copy(src, dst, sems.at[i]) for i, (src, dst) in enumerate(pairs)]
    for load in loads:
        load.start()
    return loads


def query_rows(queries):
    rows = jnp.concatenate([jnp.broadcast_to(queries[q : q + 1], (HEADS, D)) for q in range(LATENT)], axis=0)
    head = lax.broadcasted_iota(jnp.int32, (LATENT * HEADS, D), 0) % HEADS
    lane = lax.broadcasted_iota(jnp.int32, (LATENT * HEADS, D), 1) // HD
    return jnp.where(head == lane, rows, 0.0)


def fold_weights(ids_ref, table_ref, embed_ref, queries_ref, wkv_ref, wout_ref, w2_ref, woutp_ref, we_ref):
    slab = lax.broadcasted_iota(jnp.int32, (16, 1), 0)
    wanted = jnp.full((16, 1), -1, jnp.int32)
    for l in range(LEVELS):
        wanted = jnp.where(slab == l, ids_ref[l], wanted)
    rows = jnp.zeros((16, D), F32)
    for entry in range(table_ref.shape[0]):
        rows = jnp.where(wanted == entry, table_ref[entry : entry + 1, :].astype(F32), rows)
    we_ref[0:F, :] = embed_ref[...]
    we_ref[F : F + 16, :] = rows.astype(BF)
    we_ref[F + 16 :, :] = jnp.zeros((KX - F - 16, D), BF)
    row = lax.broadcasted_iota(jnp.int32, (D, 1), 0)
    lane = lax.broadcasted_iota(jnp.int32, (D, D), 1)
    mix = jnp.where(lane == (row % HEADS) * HD + row // HEADS, 1.0, 0.0).astype(BF)
    we = we_ref[...]
    wv = dot(mix, wkv_ref[:, D:], 1, 1).astype(BF)
    woutp_ref[...] = dot(mix, wout_ref[...]).astype(BF)
    high, low = split(dot(wv, we, 1, 1))
    w2_ref[0:D, 0:KX] = high
    w2_ref[0:D, KX:] = low
    qm = query_rows(queries_ref[...].astype(F32)).astype(BF)
    shigh, slow = split(dot(qm, wkv_ref[:, :D], 1, 1) * (1.0 / math.sqrt(HD)))
    score = dot(shigh, we, 1, 1) + dot(slow, we, 1, 1)
    score = jnp.concatenate([score, jnp.zeros((MV - D - 24, KX), F32)], axis=0)
    high, low = split(score)
    w2_ref[D:MV, 0:KX] = high
    w2_ref[D:MV, KX:] = low


def level_rows(x, level):
    row = lax.broadcasted_iota(jnp.int32, (KX - F, 128), 0)
    ones = jnp.where(row == level, 1.0, 0.0).astype(BF)
    return jnp.concatenate([x, ones], axis=0)


def forward_levels(read, w2_ref, vals_ref):
    scores = []
    pairs = []
    for pair in range(LEVELS // 2):
        pixels = jnp.concatenate([level_rows(read(2 * pair), 2 * pair), level_rows(read(2 * pair + 1), 2 * pair + 1)], axis=1)
        pairs.append(pixels)
        out = dot(w2_ref[...], jnp.concatenate([pixels, pixels], axis=0))
        vals_ref[2 * pair] = out[:D, :128]
        vals_ref[2 * pair + 1] = out[:D, 128:]
        scores.append(out[D : D + 24, :128])
        scores.append(out[D : D + 24, 128:])
    expo = [jnp.exp(s) for s in scores]
    total = expo[0]
    for e in expo[1:]:
        total = total + e
    inverse = 1.0 / total
    return pairs, [(e * inverse).astype(BF).astype(F32) for e in expo]


def select(rows, lanes, want):
    row = lax.broadcasted_iota(jnp.int32, (rows, lanes), 0)
    return jnp.where(row == want, 1.0, 0.0).astype(BF)


def lane_ids(lanes, start=0):
    return lax.broadcasted_iota(jnp.int32, (1, lanes), 1) + start


def inside_row(lon, lat):
    return jnp.where((lat >= 0) & (lat < 128), lon * 128 + lat, -1)


def exchange_stages(x_ref, pixels_ref, xa_ref, xb_ref, own_ref, near_ref, side_ref, mine_ref, rim_ref, send_sem, recv_sem):
    lev, tile = lax.axis_index("lev"), lax.axis_index("tile")
    bands, tiles = lax.axis_size("lev"), lax.axis_size("tile")
    next_tile, last_tile = lax.rem(tile + 1, tiles), lax.rem(tile + tiles - 1, tiles)
    levs = [lax.rem(lev + off, bands) for off in range(bands)]

    def copy(src, dst, slot, device):
        return remote(src, dst, send_sem.at[slot], recv_sem.at[slot], device)

    own, near, east, west = [], [], [], []
    for off in range(1, bands):
        own.append(lambda g, off=off: copy(own_ref.at[g, levs[off]], mine_ref.at[g, lev], 30 + g * 7 + off - 1, place(levs[off], tile)))
        near.append(copy(near_ref.at[levs[off]], rim_ref.at[lev, :, 256:512], off - 1, place(levs[off], tile)))
    for off in range(bands):
        east.append(copy(side_ref.at[0, levs[off]], rim_ref.at[lev, :, 0:128], 7 + off, place(levs[off], next_tile)))
        west.append(copy(side_ref.at[1, levs[off]], rim_ref.at[lev, :, 128:256], 15 + off, place(levs[off], last_tile)))

    def greet():
        barrier = pltpu.get_barrier_semaphore()
        for off in range(1, bands):
            pl.semaphore_signal(barrier, inc=1, device_id=place(levs[off], tile), device_id_type=pl.DeviceIdType.MESH)
        for off in range(bands):
            for side in (next_tile, last_tile):
                pl.semaphore_signal(barrier, inc=1, device_id=place(levs[off], side), device_id_type=pl.DeviceIdType.MESH)

    def send_own():
        pixels_ref[...] = x_ref[...].reshape(F * 32, 128).astype(F32)
        for lon in range(32):
            plane = pixels_ref[pl.ds(lon, F, stride=32), :].astype(BF)
            xa_ref[(lon // 8) * F : (lon // 8 + 1) * F, (lon % 8) * 128 : (lon % 8 + 1) * 128] = plane
            moved = (lon + 4) % 32
            xb_ref[(moved // 8) * F : (moved // 8 + 1) * F, (moved % 8) * 128 : (moved % 8 + 1) * 128] = plane
        rows = xa_ref[...]
        for two in range(bands // 2):
            j = lane_ids(256)
            want = ((j % 128) // 16) * 128 + 16 * (2 * two + j // 128) + j % 16
            out = dot(rows, select(1024, 256, want)).astype(BF)
            for c in range(4):
                for half in range(2):
                    own_ref[c, 2 * two + half] = out[c * F : (c + 1) * F, half * 128 : (half + 1) * 128]
        pl.semaphore_wait(pltpu.get_barrier_semaphore(), 3 * bands - 1)
        for g in range(4):
            for c in own:
                c(g).start()
        for g in range(4):
            mine_ref[g, lev] = own_ref[g, lev]

    def sort_rim():
        rows = xb_ref[...]
        for four in range(2):
            j = lane_ids(256)
            band = 4 * four + j // 64
            lat = 16 * band + j % 4 + jnp.where(j % 64 < 32, -4, 16)
            out = dot(rows, select(1024, 256, inside_row((j % 32) // 4, lat))).astype(BF)
            for b in range(4):
                lanes = slice(64 * b, 64 * b + 64)
                for c in range(2):
                    pair = [out[k * F : (k + 1) * F, lanes] for k in (2 * c, 2 * c + 1)]
                    near_ref[4 * four + b, :, c * 128 : (c + 1) * 128] = jnp.concatenate(pair, axis=1)
        rows = jnp.concatenate([xb_ref[0:F, 0:512], xb_ref[0:F, 512:1024]], axis=0)
        for two in range(bands // 2):
            j = lane_ids(256)
            k = j % 128
            thin = k % 16
            wide = k - 32
            lat = jnp.where(k < 16, 4 + thin % 4, jnp.where(k < 32, thin % 4, jnp.where(k < 64, 8 + wide % 8, jnp.where(k < 80, 16 + thin % 4, 20 + thin % 4))))
            lon = jnp.where((k >= 32) & (k < 64), wide // 8, thin // 4)
            lat = jnp.where(k < 96, 16 * (2 * two + j // 128) - 4 + lat, -1)
            out = dot(rows, select(512, 256, inside_row(lon, lat))).astype(BF)
            for side in range(2):
                for half in range(2):
                    side_ref[side, 2 * two + half] = out[side * F : (side + 1) * F, half * 128 : (half + 1) * 128]
        rim_ref[lev, :, 256:512] = near_ref[lev]

    def take_own(group):
        for c in own:
            c(group).wait_recv()

        @pl.when(group == 1)
        def _():
            for c in near + east + west:
                c.start()

    def take_rim():
        for c in near + east + west:
            c.wait_recv()
        for c in near + east + west + [c(g) for c in own for g in range(4)]:
            c.wait_send()

    return greet, send_own, sort_rim, take_own, take_rim


def pool_kernel(ids_ref, x_ref, d_ref, table_ref, embed_ref, queries_ref, wkv_ref, wout_ref, latent_ref, terms_ref, w2_ref, woutp_ref, far_ref, we_ref, vals_ref, dpool_ref, pooled_ref, dv_ref, seen_ref, tacc_ref, gacc_ref, pixels_ref, xa_ref, xb_ref, own_ref, near_ref, side_ref, mine_ref, rim_ref, d_vmem, wkv_vmem, wout_vmem, load_sem, send_sem, recv_sem):
    loads = fetch(((wkv_ref, wkv_vmem), (wout_ref, wout_vmem), (d_ref, d_vmem)), load_sem)
    greet, send_own, sort_rim, take_own, take_rim = exchange_stages(x_ref, pixels_ref, xa_ref, xb_ref, own_ref, near_ref, side_ref, mine_ref, rim_ref, send_sem, recv_sem)
    greet()
    send_own()
    sort_rim()
    loads[0].wait()
    loads[1].wait()
    fold_weights(ids_ref, table_ref, embed_ref, queries_ref, wkv_vmem, wout_vmem, w2_ref, woutp_ref, we_ref)
    gacc_ref[...] = jnp.zeros_like(gacc_ref)
    loads[2].wait()

    def group_loop(group, carry):
        take_own(group)
        pool_group(group, mine_ref, d_vmem, w2_ref, woutp_ref, latent_ref, vals_ref, dpool_ref, pooled_ref, dv_ref, seen_ref, gacc_ref)
        return carry

    lax.fori_loop(0, 4, group_loop, 0)
    tacc_ref[...] = dot(dv_ref[...], seen_ref[...], 1, 1)
    for h in range(HEADS):
        for j in range(4):
            terms_ref[j * D + h * HD : j * D + (h + 1) * HD, :] = gacc_ref[pl.ds(j * D + h, HD, stride=HEADS), :].astype(BF)
        terms_ref[4 * D + h * HD : 4 * D + (h + 1) * HD, :] = tacc_ref[pl.ds(h, HD, stride=HEADS), :].astype(BF)
    terms_ref[5 * D : 5 * D + MV - D, :] = tacc_ref[D:MV, :].astype(BF)
    terms_ref[5 * D + MV - D :, :] = jnp.zeros((TERMS - 5 * D - MV + D, KX), BF)
    take_rim()
    far_ref[...] = rim_ref[...]


def pool_group(group, x_ref, d_ref, w2_ref, woutp_ref, latent_ref, vals_ref, dpool_ref, pooled_ref, dv_ref, seen_ref, gacc_ref):
    column = pl.multiple_of(group * (LEVELS * 128), 128)
    pairs, probs = forward_levels(lambda l: x_ref[group, l], w2_ref, vals_ref)
    d_rows = jnp.concatenate([d_ref[pl.ds(8 * group, 8), q].reshape(128, D) for q in range(LATENT)], axis=0)
    dpool_ref[...] = dot(woutp_ref[...], d_rows, 1, 1)
    parts = [[probs[l][q * HEADS : (q + 1) * HEADS] for q in range(LATENT)] for l in range(LEVELS)]

    def mix_loop(i, carry):
        base = pl.multiple_of(i * 16, 16)
        pooled = [[], [], []]
        dvals = [[] for _ in range(LEVELS)]
        for e in range(2):
            rows = pl.ds(base + 8 * e, 8)
            dq = [dpool_ref[rows, q * 128 : (q + 1) * 128] for q in range(LATENT)]
            acc = [None] * LATENT
            for l in range(LEVELS):
                v = vals_ref[l, rows, :]
                for q in range(LATENT):
                    term = parts[l][q] * v
                    acc[q] = term if acc[q] is None else acc[q] + term
                dvals[l].append(parts[l][0] * dq[0] + parts[l][1] * dq[1] + parts[l][2] * dq[2])
            for q in range(LATENT):
                pooled[q].append(acc[q])
        for q in range(LATENT):
            pooled_ref[pl.ds(base, 16), q * 128 : (q + 1) * 128] = jnp.concatenate(pooled[q], axis=0).astype(BF)
        for l in range(LEVELS):
            dv_ref[pl.ds(base, 16), pl.ds(column + l * 128, 128)] = jnp.concatenate(dvals[l], axis=0).astype(BF)
        return carry

    lax.fori_loop(0, D // 16, mix_loop, 0, unroll=UNROLL)

    def dprob_loop(i, carry):
        acc = list(carry)
        for e in range(2):
            rows = pl.ds(pl.multiple_of(i * 16 + 8 * e, 8), 8)
            dq = [dpool_ref[rows, q * 128 : (q + 1) * 128] for q in range(LATENT)]
            for l in range(LEVELS):
                v = vals_ref[l, rows, :]
                for q in range(LATENT):
                    acc[l * LATENT + q] = acc[l * LATENT + q] + dq[q] * v
        return tuple(acc)

    zero = jnp.zeros((HEADS, 128), F32)
    dprob = lax.fori_loop(0, D // 16, dprob_loop, (zero,) * (LEVELS * LATENT), unroll=UNROLL)
    scale = 1.0 / math.sqrt(HD)
    delta = []
    for q in range(LATENT):
        total = parts[0][q] * dprob[q]
        for l in range(1, LEVELS):
            total = total + parts[l][q] * dprob[l * LATENT + q]
        delta.append(total)
    for l in range(LEVELS):
        ds = [parts[l][q] * (dprob[l * LATENT + q] - delta[q]) * scale for q in range(LATENT)]
        dv_ref[D:MV, pl.ds(column + l * 128, 128)] = jnp.concatenate(ds + [zero], axis=0).astype(BF)

    for pair in range(LEVELS // 2):
        seen_ref[:, pl.ds(column + pair * 256, 256)] = pairs[pair]
    pooled = pooled_ref[...]
    gterm = dot(pooled, d_rows)
    for j in range(4):
        gacc_ref[j * D : (j + 1) * D, :] += gterm[:, j * 128 : (j + 1) * 128]
    latent = dot(pooled, woutp_ref[...], 0, 0).astype(BF)
    for q in range(LATENT):
        latent_ref[pl.ds(8 * group, 8), q] = latent[q * 128 : (q + 1) * 128].reshape(8, 16, D)


def normalise(values, gain):
    mean = jnp.mean(values, axis=-1, keepdims=True)
    centred = values - mean
    var = jnp.mean(centred * centred, axis=-1, keepdims=True)
    return (centred * lax.rsqrt(var + 1e-05) * gain).astype(BF)


def permutation(dim):
    dst = lax.broadcasted_iota(jnp.int32, (384, 1) if dim == 0 else (1, 384), dim)
    src = lax.broadcasted_iota(jnp.int32, (384, 384), 1 - dim)
    mid, high = dst - 96, dst - 288
    low = (dst // 4) * 16 + dst % 4
    mid = (mid // 8) * 16 + 4 + mid % 8
    high = (high // 4) * 16 + 12 + high % 4
    want = jnp.where(dst < 96, low, jnp.where(dst < 288, mid, high))
    return jnp.where(src == want, 1.0, 0.0).astype(BF)


def sum_stages(terms_ref, halves_ref, pair_ref, part_ref, band_ref, full_ref, send_sem, recv_sem):
    lev, tile = lax.axis_index("lev"), lax.axis_index("tile")
    bands, tiles = lax.axis_size("lev"), lax.axis_size("tile")
    groups = tiles // 2
    group, core = tile // 2, lax.rem(tile, 2)

    def copy(src, dst, slot, device):
        return remote(src, dst, send_sem.at[slot], recv_sem.at[slot], device)

    other = place(lev, 2 * group + 1 - core)
    lev_peers = [place(lax.rem(lev + off, bands), tile) for off in range(1, bands)]
    group_ids = [lax.rem(group + off, groups) for off in range(1, groups)]
    group_peers = [place(lev, 2 * g + core) for g in group_ids]
    swap = copy(terms_ref.at[1 - core], halves_ref, 0, other)
    first = [copy(pair_ref.at[g], part_ref.at[i], 1 + i, group_peers[i]) for i, g in enumerate(group_ids)]
    second = [copy(band_ref.at[lev], band_ref.at[lev], 8 + i, peer) for i, peer in enumerate(lev_peers)]
    third = [copy(full_ref.at[core, group], full_ref.at[core, group], 15 + i, peer) for i, peer in enumerate(group_peers)]
    back = copy(full_ref.at[core], full_ref.at[core], 22, other)

    def greet():
        barrier = pltpu.get_barrier_semaphore()
        for peer in group_peers + lev_peers + [other]:
            pl.semaphore_signal(barrier, inc=1, device_id=peer, device_id_type=pl.DeviceIdType.MESH)
        pl.semaphore_wait(barrier, groups + bands - 1)
        swap.start()

    def over_group():
        swap.wait_recv()
        pair_ref[...] = (terms_ref[core].astype(F32) + halves_ref[...].astype(F32)).astype(BF)
        for c in first:
            c.start()

    def over_lev():
        total = pair_ref[group].astype(F32)
        for i, c in enumerate(first):
            c.wait_recv()
            total = total + part_ref[i].astype(F32)
        band_ref[lev] = total.astype(BF)
        for c in second:
            c.start()

    def gather():
        for c in second:
            c.wait_recv()
        total = band_ref[0].astype(F32)
        for b in range(1, bands):
            total = total + band_ref[b].astype(F32)
        full_ref[core, group] = total.astype(BF)
        for c in third:
            c.start()

    def swap_back():
        for c in third:
            c.wait_recv()
        back.start()

    def close(total_ref):
        back.wait_recv()
        total_ref[...] = full_ref[...]
        for c in [swap] + first + second + third + [back]:
            c.wait_send()

    return greet, over_group, over_lev, gather, swap_back, close


def window_kernel(terms_ref, xh_ref, latent_hbm, w2_ref, woutp_ref, gain_ref, wqkv_hbm, wproj_hbm, out_ref, total_ref, vals_ref, pooled_ref, q_ref, kv_ref, att_ref, perm_ref, halves_ref, pair_ref, part_ref, band_ref, full_ref, latent_ref, wqkv_ref, wproj_ref, load_sem, send_sem, recv_sem):
    loads = fetch(((wqkv_hbm, wqkv_ref), (latent_hbm, latent_ref), (wproj_hbm, wproj_ref)), load_sem)
    gain = gain_ref[...]
    greet, over_group, over_lev, gather, swap_back, close = sum_stages(terms_ref, halves_ref, pair_ref, part_ref, band_ref, full_ref, send_sem, recv_sem)
    greet()
    perm_ref[0] = permutation(0)
    perm_ref[1] = permutation(1)
    loads[0].wait()

    def halo(group, carry):
        lane0 = pl.multiple_of(group * 128, 128)
        _, probs = forward_levels(lambda l: xh_ref[l, :, pl.ds(lane0, 128)], w2_ref, vals_ref)
        parts = [[probs[l][q * HEADS : (q + 1) * HEADS] for q in range(LATENT)] for l in range(LEVELS)]

        def mix_loop(i, inner):
            base = pl.multiple_of(i * 16, 16)
            pooled = [[], [], []]
            for e in range(2):
                rows = pl.ds(base + 8 * e, 8)
                acc = [None] * LATENT
                for l in range(LEVELS):
                    v = vals_ref[l, rows, :]
                    for q in range(LATENT):
                        term = parts[l][q] * v
                        acc[q] = term if acc[q] is None else acc[q] + term
                for q in range(LATENT):
                    pooled[q].append(acc[q])
            for q in range(LATENT):
                pooled_ref[pl.ds(base, 16), q * 128 : (q + 1) * 128] = jnp.concatenate(pooled[q], axis=0).astype(BF)
            return inner

        lax.fori_loop(0, D // 16, mix_loop, 0, unroll=UNROLL)
        latent = dot(pooled_ref[...], woutp_ref[...], 0, 0).astype(BF).astype(F32)
        normed = normalise(latent, gain)
        kv = dot(normed, wqkv_ref[:, D:]).astype(BF)

        @pl.when(group < 2)
        def _():
            first = group * 3
            for q in range(LATENT):
                row = q * 128
                kv_ref[first, 48 + 32 * q : 80 + 32 * q, :] = kv[row : row + 32]
                kv_ref[first + 1, 96 + 32 * q : 128 + 32 * q, :] = kv[row + 32 : row + 64]
                kv_ref[first + 2, 48 + 32 * q : 80 + 32 * q, :] = kv[row + 64 : row + 96]

        @pl.when(group == 2)
        def _():
            for q in range(LATENT):
                row = q * 128
                near = slice(144 + 16 * q, 160 + 16 * q)
                kv_ref[3, near, :] = kv[row : row + 16]
                kv_ref[0, near, :] = kv[row + 16 : row + 32]
                kv_ref[5, near, :] = kv[row + 32 : row + 48]
                kv_ref[2, near, :] = kv[row + 48 : row + 64]

        def column_rim(half, column):
            for q in range(LATENT):
                row = q * 128 + half * 64
                near = slice(96 + 32 * q, 128 + 32 * q)
                kv_ref[3 + 3 * column, near, :] = kv[row : row + 32]
                kv_ref[5 + 3 * column, near, :] = kv[row + 32 : row + 64]

        @pl.when(group == 2)
        def _():
            column_rim(1, 1)

        @pl.when(group == 3)
        def _():
            column_rim(0, 2)
            column_rim(1, 3)

        @pl.when(group == 0)
        def _():
            over_group()
        return carry

    lax.fori_loop(0, 4, halo, 0)
    over_lev()
    loads[1].wait()
    loads[2].wait()

    def project(rows, column):
        normed = normalise(rows.astype(F32), gain)
        normed = dot(perm_ref[0], normed).astype(BF)
        q_ref[column] = (dot(normed, wqkv_ref[:, :D]).astype(BF).astype(F32) * (1.0 / math.sqrt(HD))).astype(BF)
        return dot(normed, wqkv_ref[:, D:]).astype(BF)

    rows = jnp.concatenate([latent_ref[28:32].reshape(192, D), latent_ref[0:4].reshape(192, D)], axis=0)
    kv = project(rows, 0)
    for side in range(2):
        first = 3 * (1 - side)
        kv_ref[first, 0:48, :] = kv[48 * side : 48 * side + 48]
        kv_ref[first + 1, 0:96, :] = kv[96 + 96 * side : 192 + 96 * side]
        kv_ref[first + 2, 0:48, :] = kv[288 + 48 * side : 336 + 48 * side]

    def own(column, carry):
        rows = latent_ref[pl.ds(8 * column - 4, 8)].reshape(384, D)
        kv = project(rows, column)
        first = 3 + 3 * column
        kv_ref[first, 0:96, :] = kv[0:96]
        kv_ref[first + 1, 0:192, :] = kv[96:288]
        kv_ref[first + 2, 0:96, :] = kv[288:384]
        return carry

    lax.fori_loop(1, 4, own, 0)
    gather()

    key = lax.broadcasted_iota(jnp.int32, (1, 192), 1)
    head_lane = lax.broadcasted_iota(jnp.int32, (1, 256), 1) // HD
    odd_lane = lax.broadcasted_iota(jnp.int32, (1, 128), 1) >= HD

    def attend(column, window, row0, count, valid):
        for quad in range(HEADS // 4):
            lanes = slice(quad * 256, quad * 256 + 256)
            q = q_ref[column, row0 : row0 + count, lanes]
            nil = jnp.zeros_like(q)
            q4 = jnp.concatenate([jnp.where(head_lane == h, q, nil) for h in range(4)], axis=0)
            expo = jnp.exp(dot(q4, kv_ref[window, :, lanes], 1, 1))
            if valid is not None:
                expo = jnp.where(valid, expo, 0.0)
            probs = (expo * (1.0 / jnp.sum(expo, axis=-1, keepdims=True))).astype(BF)
            both = dot(probs, kv_ref[window, :, D + quad * 256 : D + quad * 256 + 256])
            for two in range(2):
                part = both[2 * two * count : 2 * (two + 1) * count, two * 128 : (two + 1) * 128]
                spot = slice(quad * 256 + two * 128, quad * 256 + two * 128 + 128)
                att_ref[row0 : row0 + count, spot] = jnp.where(odd_lane, part[count:], part[:count]).astype(BF)

    lev = lax.axis_index("lev")
    inside = (lev > 0, lev < lax.axis_size("lev") - 1)
    plain = [(key < 96) | ok for ok in inside]
    corner = [(key < 48) | ((key < 144) & ((key + 16) % 32 < 16)) | ok for ok in inside]

    for side in range(2):
        first = 3 * (1 - side)
        attend(0, first, 48 * side, 48, corner[0])
        attend(0, first + 1, 96 + 96 * side, 96, None)
        attend(0, first + 2, 288 + 48 * side, 48, corner[1])

    def finish(rows):
        natural = dot(perm_ref[1], att_ref[...]).astype(BF)
        return (rows.astype(F32) + dot(natural, wproj_ref[...])).astype(BF)

    done = finish(rows)
    out_ref[28:32] = done[:192].reshape(4, 3, 16, D)
    out_ref[0:4] = done[192:].reshape(4, 3, 16, D)

    def column_loop(column, carry):
        first = 3 + 3 * column
        attend(column, first, 0, 96, plain[0])
        attend(column, first + 1, 96, 192, None)
        attend(column, first + 2, 288, 96, plain[1])
        rows = latent_ref[pl.ds(8 * column - 4, 8)].reshape(384, D)
        out_ref[pl.ds(8 * column - 4, 8)] = finish(rows).reshape(8, 3, 16, D)

        @pl.when(column == 2)
        def _():
            swap_back()

        return carry

    lax.fori_loop(1, 4, column_loop, 0)
    close(total_ref)


def finish_kernel(done_hbm, total_ref, we_ref, queries_ref, wkv_hbm, out_ref, gembed_ref, gkv_ref, gout_ref, done_vmem, wkv_ref, gkv_vmem, gout_vmem, load_sem, save_sem, factor):
    loads = fetch(((wkv_hbm, wkv_ref), (done_hbm, done_vmem)), load_sem)
    for j in range(4):
        gout_vmem[:, j * 128 : (j + 1) * 128] = total_ref[j * D : (j + 1) * D, :].astype(F32) * factor
    saves = [pltpu.make_async_copy(gout_vmem, gout_ref, save_sem.at[0])]
    saves[0].start()
    qm = query_rows(queries_ref[...].astype(F32)).astype(BF)
    values = total_ref[4 * D : 5 * D, :]
    keys = dot(qm, total_ref[5 * D : 5 * D + 32, :][:24], 0, 0)
    khigh, klow = split(keys)
    we = we_ref[...]
    gkv_vmem[1] = dot(we, values, 0, 1) * factor
    saves.append(pltpu.make_async_copy(gkv_vmem.at[1], gkv_ref.at[:, D : 2 * D], save_sem.at[1]))
    saves[1].start()
    gkv_vmem[0] = (dot(we, khigh, 0, 1) + dot(we, klow, 0, 1)) * factor
    saves.append(pltpu.make_async_copy(gkv_vmem.at[0], gkv_ref.at[:, 0:D], save_sem.at[2]))
    saves[2].start()
    loads[0].wait()
    loads[1].wait()
    saves.append(pltpu.make_async_copy(done_vmem, out_ref, save_sem.at[3]))
    saves[3].start()
    wk, wv = wkv_ref[:, :D], wkv_ref[:, D:]
    grad = dot(khigh, wk, 0, 1) + dot(klow, wk, 0, 1) + dot(values, wv, 0, 1)
    gembed_ref[...] = grad[:F] * factor
    for save in saves:
        save.wait()


def whole(shape, dtype):
    return jax.ShapeDtypeStruct(shape, dtype)


def params(**kw):
    return pltpu.CompilerParams(vmem_limit_bytes=VMEM_LIMIT, **kw)


def per_device(inputs, level_ids, level_table, w_embed, queries, w_kv, w_out, gain, w_qkv, w_proj, d_latent):
    bands = lax.axis_size("lev")
    tiles = lax.axis_size("tile")
    lon_rows, lat_rows = d_latent.shape[:2]
    vmem = pl.BlockSpec(memory_space=pltpu.VMEM)
    anywhere = pl.BlockSpec(memory_space=pl.ANY)
    d_nat = d_latent.transpose(0, 2, 1, 3)
    latent, terms, w2, woutp, far, we = pl.pallas_call(
        pool_kernel,
        in_specs=[pl.BlockSpec(memory_space=pltpu.SMEM), vmem, anywhere, vmem, vmem, vmem, anywhere, anywhere],
        out_specs=(vmem,) * 6,
        out_shape=(whole(d_nat.shape, BF), whole((TERMS, KX), BF), whole((MV, 2 * KX), BF), whole((D, D), BF), whole((LEVELS, F, 512), BF), whole((KX, D), BF)),
        scratch_shapes=[
            pltpu.VMEM((LEVELS, D, 128), F32),
            pltpu.VMEM((D, 384), F32),
            pltpu.VMEM((D, 384), BF),
            pltpu.VMEM((MV, 4 * LEVELS * 128), BF),
            pltpu.VMEM((KX, 4 * LEVELS * 128), BF),
            pltpu.VMEM((MV, KX), F32),
            pltpu.VMEM((4 * D, 128), F32),
            pltpu.VMEM((F * 32, 128), F32),
            pltpu.VMEM((4 * F, 1024), BF),
            pltpu.VMEM((4 * F, 1024), BF),
            pltpu.VMEM((4, LEVELS, F, 128), BF),
            pltpu.VMEM((LEVELS, F, 256), BF),
            pltpu.VMEM((2, LEVELS, F, 128), BF),
            pltpu.VMEM((4, LEVELS, F, 128), BF),
            pltpu.VMEM((LEVELS, F, 512), BF),
            pltpu.VMEM(d_nat.shape, BF),
            pltpu.VMEM((D, 2 * D), BF),
            pltpu.VMEM((D, D), BF),
            pltpu.SemaphoreType.DMA((3,)),
            pltpu.SemaphoreType.DMA((58,)),
            pltpu.SemaphoreType.DMA((58,)),
        ],
        compiler_params=params(collective_id=2, has_side_effects=True),
        name="pool",
    )(level_ids, inputs[0], d_nat, level_table, w_embed, queries, w_kv, w_out)

    factor = 1.0 / math.sqrt(lon_rows * lat_rows * bands * tiles)
    done, total = pl.pallas_call(
        window_kernel,
        in_specs=[vmem, vmem, anywhere, vmem, vmem, vmem, anywhere, anywhere],
        out_specs=(vmem, vmem),
        out_shape=(whole(d_nat.shape, BF), whole((2, 8, CHUNK, KX), BF)),
        scratch_shapes=[
            pltpu.VMEM((LEVELS, D, 128), F32),
            pltpu.VMEM((D, 384), BF),
            pltpu.VMEM((4, 384, D), BF),
            pltpu.VMEM((15, 192, 2 * D), BF),
            pltpu.VMEM((384, D), BF),
            pltpu.VMEM((2, 384, 384), BF),
            pltpu.VMEM((8, CHUNK, KX), BF),
            pltpu.VMEM((8, CHUNK, KX), BF),
            pltpu.VMEM((7, CHUNK, KX), BF),
            pltpu.VMEM((8, CHUNK, KX), BF),
            pltpu.VMEM((2, 8, CHUNK, KX), BF),
            pltpu.VMEM(d_nat.shape, BF),
            pltpu.VMEM((D, 3 * D), BF),
            pltpu.VMEM((D, D), BF),
            pltpu.SemaphoreType.DMA((3,)),
            pltpu.SemaphoreType.DMA((23,)),
            pltpu.SemaphoreType.DMA((23,)),
        ],
        compiler_params=params(collective_id=1, has_side_effects=True),
        name="windows",
    )(terms.reshape(2, 8, CHUNK, KX), far, latent, w2, woutp, gain.reshape(1, D), w_qkv, w_proj)

    out, gembed, gkv, gout = pl.pallas_call(
        functools.partial(finish_kernel, factor=factor),
        in_specs=[anywhere, vmem, vmem, vmem, anywhere],
        out_specs=(anywhere, vmem, anywhere, anywhere),
        out_shape=(whole(d_nat.shape, BF), whole((F, D), F32), whole((D, 2 * D), F32), whole((D, D), F32)),
        scratch_shapes=[
            pltpu.VMEM(d_nat.shape, BF),
            pltpu.VMEM((D, 2 * D), BF),
            pltpu.VMEM((2, D, D), F32),
            pltpu.VMEM((D, D), F32),
            pltpu.SemaphoreType.DMA((2,)),
            pltpu.SemaphoreType.DMA((4,)),
        ],
        compiler_params=params(),
        name="finish",
    )(done, total.reshape(TERMS, KX), we, queries, w_kv)
    return (out.transpose(0, 2, 1, 3), gembed, gkv, gout)


def solution(mesh):
    placed = (P("lev", None, "tile", None),) + (P(),) * 9 + (P("tile", "lev", None, None),)
    return jax.shard_map(
        per_device,
        mesh=mesh,
        in_specs=placed,
        out_specs=(P("tile", "lev", None, None), P(), P(), P()),
        check_vma=False,
    )
```

```python
import functools
import math

import jax
import jax.numpy as jnp
import numpy as np
from jax import lax
from jax.experimental import pallas as pl
from jax.experimental.pallas import tpu as pltpu
from jax.sharding import PartitionSpec as P

HD = 64
HEADS = 8
WIN = 8
D = 512
F = 80
LEVELS = 8
LATENT = 3
KX = 128
MV = 544
CHUNK = 176
UNROLL = 4
TERMS = 16 * CHUNK
BF = jnp.bfloat16
F32 = jnp.float32
VMEM_LIMIT = 56 * 1024 * 1024


def dot(a, b, ca=1, cb=0):
    return lax.dot_general(a, b, (((ca,), (cb,)), ((), ())), preferred_element_type=F32)


def split(value):
    high = value.astype(BF)
    return high, (value - high.astype(F32)).astype(BF)


def place(lev, tile):
    return {"lev": lev, "tile": tile}


def remote(src, dst, send, recv, device):
    return pltpu.make_async_remote_copy(src_ref=src, dst_ref=dst, send_sem=send, recv_sem=recv, device_id=device, device_id_type=pl.DeviceIdType.MESH)


def fetch(pairs, sems):
    loads = [pltpu.make_async_copy(src, dst, sems.at[i]) for i, (src, dst) in enumerate(pairs)]
    for load in loads:
        load.start()
    return loads


def query_rows(queries):
    rows = jnp.concatenate([jnp.broadcast_to(queries[q : q + 1], (HEADS, D)) for q in range(LATENT)], axis=0)
    head = lax.broadcasted_iota(jnp.int32, (LATENT * HEADS, D), 0) % HEADS
    lane = lax.broadcasted_iota(jnp.int32, (LATENT * HEADS, D), 1) // HD
    return jnp.where(head == lane, rows, 0.0)


def fold_weights(ids_ref, table_ref, embed_ref, queries_ref, wkv_ref, wout_ref, w2_ref, woutp_ref, we_ref):
    slab = lax.broadcasted_iota(jnp.int32, (16, 1), 0)
    wanted = jnp.full((16, 1), -1, jnp.int32)
    for l in range(LEVELS):
        wanted = jnp.where(slab == l, ids_ref[l], wanted)
    rows = jnp.zeros((16, D), F32)
    for entry in range(table_ref.shape[0]):
        rows = jnp.where(wanted == entry, table_ref[entry : entry + 1, :].astype(F32), rows)
    we_ref[0:F, :] = embed_ref[...]
    we_ref[F : F + 16, :] = rows.astype(BF)
    we_ref[F + 16 :, :] = jnp.zeros((KX - F - 16, D), BF)
    row = lax.broadcasted_iota(jnp.int32, (D, 1), 0)
    lane = lax.broadcasted_iota(jnp.int32, (D, D), 1)
    mix = jnp.where(lane == (row % HEADS) * HD + row // HEADS, 1.0, 0.0).astype(BF)
    we = we_ref[...]
    wv = dot(mix, wkv_ref[:, D:], 1, 1).astype(BF)
    woutp_ref[...] = dot(mix, wout_ref[...]).astype(BF)
    high, low = split(dot(wv, we, 1, 1))
    w2_ref[0:D, 0:KX] = high
    w2_ref[0:D, KX:] = low
    qm = query_rows(queries_ref[...].astype(F32)).astype(BF)
    shigh, slow = split(dot(qm, wkv_ref[:, :D], 1, 1) * (1.0 / math.sqrt(HD)))
    score = dot(shigh, we, 1, 1) + dot(slow, we, 1, 1)
    score = jnp.concatenate([score, jnp.zeros((MV - D - 24, KX), F32)], axis=0)
    high, low = split(score)
    w2_ref[D:MV, 0:KX] = high
    w2_ref[D:MV, KX:] = low


def level_rows(x, level):
    row = lax.broadcasted_iota(jnp.int32, (KX - F, 128), 0)
    ones = jnp.where(row == level, 1.0, 0.0).astype(BF)
    return jnp.concatenate([x, ones], axis=0)


def forward_levels(read, w2_ref, vals_ref):
    scores = []
    pairs = []
    for pair in range(LEVELS // 2):
        pixels = jnp.concatenate([level_rows(read(2 * pair), 2 * pair), level_rows(read(2 * pair + 1), 2 * pair + 1)], axis=1)
        pairs.append(pixels)
        out = dot(w2_ref[...], jnp.concatenate([pixels, pixels], axis=0))
        vals_ref[2 * pair] = out[:D, :128]
        vals_ref[2 * pair + 1] = out[:D, 128:]
        scores.append(out[D : D + 24, :128])
        scores.append(out[D : D + 24, 128:])
    expo = [jnp.exp(s) for s in scores]
    total = expo[0]
    for e in expo[1:]:
        total = total + e
    inverse = 1.0 / total
    return pairs, [(e * inverse).astype(BF).astype(F32) for e in expo]


def select(rows, lanes, want):
    row = lax.broadcasted_iota(jnp.int32, (rows, lanes), 0)
    return jnp.where(row == want, 1.0, 0.0).astype(BF)


def lane_ids(lanes, start=0):
    return lax.broadcasted_iota(jnp.int32, (1, lanes), 1) + start


def inside_row(lon, lat):
    return jnp.where((lat >= 0) & (lat < 128), lon * 128 + lat, -1)


def exchange_stages(x_ref, pixels_ref, xa_ref, xb_ref, own_ref, near_ref, side_ref, mine_ref, rim_ref, send_sem, recv_sem):
    lev, tile = lax.axis_index("lev"), lax.axis_index("tile")
    bands, tiles = lax.axis_size("lev"), lax.axis_size("tile")
    next_tile, last_tile = lax.rem(tile + 1, tiles), lax.rem(tile + tiles - 1, tiles)
    levs = [lax.rem(lev + off, bands) for off in range(bands)]

    def copy(src, dst, slot, device):
        return remote(src, dst, send_sem.at[slot], recv_sem.at[slot], device)

    own, near, east, west = [], [], [], []
    for off in range(1, bands):
        own.append(lambda g, off=off: copy(own_ref.at[g, levs[off]], mine_ref.at[g, lev], 30 + g * 7 + off - 1, place(levs[off], tile)))
        near.append(copy(near_ref.at[levs[off]], rim_ref.at[lev, :, 256:512], off - 1, place(levs[off], tile)))
    for off in range(bands):
        east.append(copy(side_ref.at[0, levs[off]], rim_ref.at[lev, :, 0:128], 7 + off, place(levs[off], next_tile)))
        west.append(copy(side_ref.at[1, levs[off]], rim_ref.at[lev, :, 128:256], 15 + off, place(levs[off], last_tile)))

    def greet():
        barrier = pltpu.get_barrier_semaphore()
        for off in range(1, bands):
            pl.semaphore_signal(barrier, inc=1, device_id=place(levs[off], tile), device_id_type=pl.DeviceIdType.MESH)
        for off in range(bands):
            for side in (next_tile, last_tile):
                pl.semaphore_signal(barrier, inc=1, device_id=place(levs[off], side), device_id_type=pl.DeviceIdType.MESH)

    def send_own():
        pixels_ref[...] = x_ref[...].reshape(F * 32, 128).astype(F32)
        for lon in range(32):
            plane = pixels_ref[pl.ds(lon, F, stride=32), :].astype(BF)
            xa_ref[(lon // 8) * F : (lon // 8 + 1) * F, (lon % 8) * 128 : (lon % 8 + 1) * 128] = plane
            moved = (lon + 4) % 32
            xb_ref[(moved // 8) * F : (moved // 8 + 1) * F, (moved % 8) * 128 : (moved % 8 + 1) * 128] = plane
        rows = xa_ref[...]
        for two in range(bands // 2):
            j = lane_ids(256)
            want = ((j % 128) // 16) * 128 + 16 * (2 * two + j // 128) + j % 16
            out = dot(rows, select(1024, 256, want)).astype(BF)
            for c in range(4):
                for half in range(2):
                    own_ref[c, 2 * two + half] = out[c * F : (c + 1) * F, half * 128 : (half + 1) * 128]
        pl.semaphore_wait(pltpu.get_barrier_semaphore(), 3 * bands - 1)
        for g in range(4):
            for c in own:
                c(g).start()
        for g in range(4):
            mine_ref[g, lev] = own_ref[g, lev]

    def sort_rim():
        rows = xb_ref[...]
        for four in range(2):
            j = lane_ids(256)
            band = 4 * four + j // 64
            lat = 16 * band + j % 4 + jnp.where(j % 64 < 32, -4, 16)
            out = dot(rows, select(1024, 256, inside_row((j % 32) // 4, lat))).astype(BF)
            for b in range(4):
                lanes = slice(64 * b, 64 * b + 64)
                for c in range(2):
                    pair = [out[k * F : (k + 1) * F, lanes] for k in (2 * c, 2 * c + 1)]
                    near_ref[4 * four + b, :, c * 128 : (c + 1) * 128] = jnp.concatenate(pair, axis=1)
        rows = jnp.concatenate([xb_ref[0:F, 0:512], xb_ref[0:F, 512:1024]], axis=0)
        for two in range(bands // 2):
            j = lane_ids(256)
            k = j % 128
            thin = k % 16
            wide = k - 32
            lat = jnp.where(k < 16, 4 + thin % 4, jnp.where(k < 32, thin % 4, jnp.where(k < 64, 8 + wide % 8, jnp.where(k < 80, 16 + thin % 4, 20 + thin % 4))))
            lon = jnp.where((k >= 32) & (k < 64), wide // 8, thin // 4)
            lat = jnp.where(k < 96, 16 * (2 * two + j // 128) - 4 + lat, -1)
            out = dot(rows, select(512, 256, inside_row(lon, lat))).astype(BF)
            for side in range(2):
                for half in range(2):
                    side_ref[side, 2 * two + half] = out[side * F : (side + 1) * F, half * 128 : (half + 1) * 128]
        rim_ref[lev, :, 256:512] = near_ref[lev]

    def take_own(group):
        for c in own:
            c(group).wait_recv()

        @pl.when(group == 1)
        def _():
            for c in near + east + west:
                c.start()

    def take_rim():
        for c in near + east + west:
            c.wait_recv()
        for c in near + east + west + [c(g) for c in own for g in range(4)]:
            c.wait_send()

    return greet, send_own, sort_rim, take_own, take_rim


def pool_kernel(ids_ref, x_ref, d_ref, table_ref, embed_ref, queries_ref, wkv_ref, wout_ref, latent_ref, terms_ref, w2_ref, woutp_ref, far_ref, we_ref, vals_ref, dpool_ref, pooled_ref, dv_ref, seen_ref, tacc_ref, gacc_ref, pixels_ref, xa_ref, xb_ref, own_ref, near_ref, side_ref, mine_ref, rim_ref, d_vmem, wkv_vmem, wout_vmem, load_sem, send_sem, recv_sem):
    loads = fetch(((wkv_ref, wkv_vmem), (wout_ref, wout_vmem), (d_ref, d_vmem)), load_sem)
    greet, send_own, sort_rim, take_own, take_rim = exchange_stages(x_ref, pixels_ref, xa_ref, xb_ref, own_ref, near_ref, side_ref, mine_ref, rim_ref, send_sem, recv_sem)
    greet()
    send_own()
    sort_rim()
    loads[0].wait()
    loads[1].wait()
    fold_weights(ids_ref, table_ref, embed_ref, queries_ref, wkv_vmem, wout_vmem, w2_ref, woutp_ref, we_ref)
    gacc_ref[...] = jnp.zeros_like(gacc_ref)
    loads[2].wait()

    def group_loop(group, carry):
        take_own(group)
        pool_group(group, mine_ref, d_vmem, w2_ref, woutp_ref, latent_ref, vals_ref, dpool_ref, pooled_ref, dv_ref, seen_ref, gacc_ref)
        return carry

    lax.fori_loop(0, 4, group_loop, 0)
    tacc_ref[...] = dot(dv_ref[...], seen_ref[...], 1, 1)
    for h in range(HEADS):
        for j in range(4):
            terms_ref[j * D + h * HD : j * D + (h + 1) * HD, :] = gacc_ref[pl.ds(j * D + h, HD, stride=HEADS), :].astype(BF)
        terms_ref[4 * D + h * HD : 4 * D + (h + 1) * HD, :] = tacc_ref[pl.ds(h, HD, stride=HEADS), :].astype(BF)
    terms_ref[5 * D : 5 * D + MV - D, :] = tacc_ref[D:MV, :].astype(BF)
    terms_ref[5 * D + MV - D :, :] = jnp.zeros((TERMS - 5 * D - MV + D, KX), BF)
    take_rim()
    far_ref[...] = rim_ref[...]


def pool_group(group, x_ref, d_ref, w2_ref, woutp_ref, latent_ref, vals_ref, dpool_ref, pooled_ref, dv_ref, seen_ref, gacc_ref):
    column = pl.multiple_of(group * (LEVELS * 128), 128)
    pairs, probs = forward_levels(lambda l: x_ref[group, l], w2_ref, vals_ref)
    d_rows = jnp.concatenate([d_ref[pl.ds(8 * group, 8), q].reshape(128, D) for q in range(LATENT)], axis=0)
    dpool_ref[...] = dot(woutp_ref[...], d_rows, 1, 1)
    parts = [[probs[l][q * HEADS : (q + 1) * HEADS] for q in range(LATENT)] for l in range(LEVELS)]

    def mix_loop(i, carry):
        base = pl.multiple_of(i * 16, 16)
        pooled = [[], [], []]
        dvals = [[] for _ in range(LEVELS)]
        for e in range(2):
            rows = pl.ds(base + 8 * e, 8)
            dq = [dpool_ref[rows, q * 128 : (q + 1) * 128] for q in range(LATENT)]
            acc = [None] * LATENT
            for l in range(LEVELS):
                v = vals_ref[l, rows, :]
                for q in range(LATENT):
                    term = parts[l][q] * v
                    acc[q] = term if acc[q] is None else acc[q] + term
                dvals[l].append(parts[l][0] * dq[0] + parts[l][1] * dq[1] + parts[l][2] * dq[2])
            for q in range(LATENT):
                pooled[q].append(acc[q])
        for q in range(LATENT):
            pooled_ref[pl.ds(base, 16), q * 128 : (q + 1) * 128] = jnp.concatenate(pooled[q], axis=0).astype(BF)
        for l in range(LEVELS):
            dv_ref[pl.ds(base, 16), pl.ds(column + l * 128, 128)] = jnp.concatenate(dvals[l], axis=0).astype(BF)
        return carry

    lax.fori_loop(0, D // 16, mix_loop, 0, unroll=UNROLL)

    def dprob_loop(i, carry):
        acc = list(carry)
        for e in range(2):
            rows = pl.ds(pl.multiple_of(i * 16 + 8 * e, 8), 8)
            dq = [dpool_ref[rows, q * 128 : (q + 1) * 128] for q in range(LATENT)]
            for l in range(LEVELS):
                v = vals_ref[l, rows, :]
                for q in range(LATENT):
                    acc[l * LATENT + q] = acc[l * LATENT + q] + dq[q] * v
        return tuple(acc)

    zero = jnp.zeros((HEADS, 128), F32)
    dprob = lax.fori_loop(0, D // 16, dprob_loop, (zero,) * (LEVELS * LATENT), unroll=UNROLL)
    scale = 1.0 / math.sqrt(HD)
    delta = []
    for q in range(LATENT):
        total = parts[0][q] * dprob[q]
        for l in range(1, LEVELS):
            total = total + parts[l][q] * dprob[l * LATENT + q]
        delta.append(total)
    for l in range(LEVELS):
        ds = [parts[l][q] * (dprob[l * LATENT + q] - delta[q]) * scale for q in range(LATENT)]
        dv_ref[D:MV, pl.ds(column + l * 128, 128)] = jnp.concatenate(ds + [zero], axis=0).astype(BF)

    for pair in range(LEVELS // 2):
        seen_ref[:, pl.ds(column + pair * 256, 256)] = pairs[pair]
    pooled = pooled_ref[...]
    gterm = dot(pooled, d_rows)
    for j in range(4):
        gacc_ref[j * D : (j + 1) * D, :] += gterm[:, j * 128 : (j + 1) * 128]
    latent = dot(pooled, woutp_ref[...], 0, 0).astype(BF)
    for q in range(LATENT):
        latent_ref[pl.ds(8 * group, 8), q] = latent[q * 128 : (q + 1) * 128].reshape(8, 16, D)


def normalise(values, gain):
    mean = jnp.mean(values, axis=-1, keepdims=True)
    centred = values - mean
    var = jnp.mean(centred * centred, axis=-1, keepdims=True)
    return (centred * lax.rsqrt(var + 1e-05) * gain).astype(BF)


def permutation(dim):
    dst = lax.broadcasted_iota(jnp.int32, (384, 1) if dim == 0 else (1, 384), dim)
    src = lax.broadcasted_iota(jnp.int32, (384, 384), 1 - dim)
    mid, high = dst - 96, dst - 288
    low = (dst // 4) * 16 + dst % 4
    mid = (mid // 8) * 16 + 4 + mid % 8
    high = (high // 4) * 16 + 12 + high % 4
    want = jnp.where(dst < 96, low, jnp.where(dst < 288, mid, high))
    return jnp.where(src == want, 1.0, 0.0).astype(BF)


def sum_stages(start, size, slot0, terms_ref, halves_ref, pair_ref, part_ref, band_ref, full_ref, send_sem, recv_sem):
    cut = pl.ds(start, size)
    lev, tile = lax.axis_index("lev"), lax.axis_index("tile")
    bands, tiles = lax.axis_size("lev"), lax.axis_size("tile")
    groups = tiles // 2
    group, core = tile // 2, lax.rem(tile, 2)

    def copy(src, dst, slot, device):
        return remote(src, dst, send_sem.at[slot0 + slot], recv_sem.at[slot0 + slot], device)

    other = place(lev, 2 * group + 1 - core)
    lev_peers = [place(lax.rem(lev + off, bands), tile) for off in range(1, bands)]
    group_ids = [lax.rem(group + off, groups) for off in range(1, groups)]
    group_peers = [place(lev, 2 * g + core) for g in group_ids]
    swap = copy(terms_ref.at[1 - core, :, cut, :], halves_ref.at[:, cut, :], 0, other)
    first = [copy(pair_ref.at[g, cut, :], part_ref.at[i, cut, :], 1 + i, group_peers[i]) for i, g in enumerate(group_ids)]
    second = [copy(band_ref.at[lev, cut, :], band_ref.at[lev, cut, :], 8 + i, peer) for i, peer in enumerate(lev_peers)]
    third = [copy(full_ref.at[core, group, cut, :], full_ref.at[core, group, cut, :], 15 + i, peer) for i, peer in enumerate(group_peers)]
    back = copy(full_ref.at[core, :, cut, :], full_ref.at[core, :, cut, :], 22, other)

    def greet():
        barrier = pltpu.get_barrier_semaphore()
        for peer in group_peers + lev_peers + [other]:
            pl.semaphore_signal(barrier, inc=1, device_id=peer, device_id_type=pl.DeviceIdType.MESH)
        pl.semaphore_wait(barrier, groups + bands - 1)

    def begin():
        swap.start()

    def over_group():
        swap.wait_recv()
        pair_ref[:, cut, :] = (terms_ref[core, :, cut, :].astype(F32) + halves_ref[:, cut, :].astype(F32)).astype(BF)
        for c in first:
            c.start()

    def over_lev():
        total = pair_ref[group, cut, :].astype(F32)
        for i, c in enumerate(first):
            c.wait_recv()
            total = total + part_ref[i, cut, :].astype(F32)
        band_ref[lev, cut, :] = total.astype(BF)
        for c in second:
            c.start()

    def gather():
        for c in second:
            c.wait_recv()
        total = band_ref[0, cut, :].astype(F32)
        for b in range(1, bands):
            total = total + band_ref[b, cut, :].astype(F32)
        full_ref[core, group, cut, :] = total.astype(BF)
        for c in third:
            c.start()

    def swap_back():
        for c in third:
            c.wait_recv()
        back.start()

    def close(total_ref):
        back.wait_recv()
        total_ref[:, :, cut, :] = full_ref[:, :, cut, :]
        for c in [swap] + first + second + third + [back]:
            c.wait_send()

    return greet, begin, over_group, over_lev, gather, swap_back, close


def window_kernel(terms_ref, xh_ref, latent_hbm, w2_ref, woutp_ref, gain_ref, wqkv_hbm, wproj_hbm, out_ref, total_ref, vals_ref, pooled_ref, q_ref, kv_ref, att_ref, perm_ref, halves_ref, pair_ref, part_ref, band_ref, full_ref, latent_ref, wqkv_ref, wproj_ref, load_sem, send_sem, recv_sem):
    loads = fetch(((wqkv_hbm, wqkv_ref), (latent_hbm, latent_ref), (wproj_hbm, wproj_ref)), load_sem)
    gain = gain_ref[...]
    buffers = (terms_ref, halves_ref, pair_ref, part_ref, band_ref, full_ref, send_sem, recv_sem)
    greet, begin_a, over_group_a, over_lev_a, gather_a, swap_back_a, close_a = sum_stages(0, 96, 0, *buffers)
    _, begin_b, over_group_b, over_lev_b, gather_b, swap_back_b, close_b = sum_stages(96, CHUNK - 96, 23, *buffers)
    greet()
    begin_a()
    begin_b()
    perm_ref[0] = permutation(0)
    perm_ref[1] = permutation(1)
    loads[0].wait()

    def halo(group, carry):
        lane0 = pl.multiple_of(group * 128, 128)
        _, probs = forward_levels(lambda l: xh_ref[l, :, pl.ds(lane0, 128)], w2_ref, vals_ref)
        parts = [[probs[l][q * HEADS : (q + 1) * HEADS] for q in range(LATENT)] for l in range(LEVELS)]

        def mix_loop(i, inner):
            base = pl.multiple_of(i * 16, 16)
            pooled = [[], [], []]
            for e in range(2):
                rows = pl.ds(base + 8 * e, 8)
                acc = [None] * LATENT
                for l in range(LEVELS):
                    v = vals_ref[l, rows, :]
                    for q in range(LATENT):
                        term = parts[l][q] * v
                        acc[q] = term if acc[q] is None else acc[q] + term
                for q in range(LATENT):
                    pooled[q].append(acc[q])
            for q in range(LATENT):
                pooled_ref[pl.ds(base, 16), q * 128 : (q + 1) * 128] = jnp.concatenate(pooled[q], axis=0).astype(BF)
            return inner

        lax.fori_loop(0, D // 16, mix_loop, 0, unroll=UNROLL)
        latent = dot(pooled_ref[...], woutp_ref[...], 0, 0).astype(BF).astype(F32)
        normed = normalise(latent, gain)
        kv = dot(normed, wqkv_ref[:, D:]).astype(BF)

        @pl.when(group < 2)
        def _():
            first = group * 3
            for q in range(LATENT):
                row = q * 128
                kv_ref[first, 48 + 32 * q : 80 + 32 * q, :] = kv[row : row + 32]
                kv_ref[first + 1, 96 + 32 * q : 128 + 32 * q, :] = kv[row + 32 : row + 64]
                kv_ref[first + 2, 48 + 32 * q : 80 + 32 * q, :] = kv[row + 64 : row + 96]

        @pl.when(group == 2)
        def _():
            for q in range(LATENT):
                row = q * 128
                near = slice(144 + 16 * q, 160 + 16 * q)
                kv_ref[3, near, :] = kv[row : row + 16]
                kv_ref[0, near, :] = kv[row + 16 : row + 32]
                kv_ref[5, near, :] = kv[row + 32 : row + 48]
                kv_ref[2, near, :] = kv[row + 48 : row + 64]

        def column_rim(half, column):
            for q in range(LATENT):
                row = q * 128 + half * 64
                near = slice(96 + 32 * q, 128 + 32 * q)
                kv_ref[3 + 3 * column, near, :] = kv[row : row + 32]
                kv_ref[5 + 3 * column, near, :] = kv[row + 32 : row + 64]

        @pl.when(group == 2)
        def _():
            column_rim(1, 1)

        @pl.when(group == 3)
        def _():
            column_rim(0, 2)
            column_rim(1, 3)

        @pl.when(group == 0)
        def _():
            over_group_a()
            over_group_b()
        return carry

    lax.fori_loop(0, 4, halo, 0)
    over_lev_a()
    loads[1].wait()
    loads[2].wait()

    def project(rows, column):
        normed = normalise(rows.astype(F32), gain)
        normed = dot(perm_ref[0], normed).astype(BF)
        q_ref[column] = (dot(normed, wqkv_ref[:, :D]).astype(BF).astype(F32) * (1.0 / math.sqrt(HD))).astype(BF)
        return dot(normed, wqkv_ref[:, D:]).astype(BF)

    rows = jnp.concatenate([latent_ref[28:32].reshape(192, D), latent_ref[0:4].reshape(192, D)], axis=0)
    kv = project(rows, 0)
    for side in range(2):
        first = 3 * (1 - side)
        kv_ref[first, 0:48, :] = kv[48 * side : 48 * side + 48]
        kv_ref[first + 1, 0:96, :] = kv[96 + 96 * side : 192 + 96 * side]
        kv_ref[first + 2, 0:48, :] = kv[288 + 48 * side : 336 + 48 * side]

    over_lev_b()

    def own(column, carry):
        rows = latent_ref[pl.ds(8 * column - 4, 8)].reshape(384, D)
        kv = project(rows, column)
        first = 3 + 3 * column
        kv_ref[first, 0:96, :] = kv[0:96]
        kv_ref[first + 1, 0:192, :] = kv[96:288]
        kv_ref[first + 2, 0:96, :] = kv[288:384]

        @pl.when(column == 2)
        def _():
            gather_a()

        return carry

    lax.fori_loop(1, 4, own, 0)
    gather_b()

    key = lax.broadcasted_iota(jnp.int32, (1, 192), 1)
    head_lane = lax.broadcasted_iota(jnp.int32, (1, 256), 1) // HD
    odd_lane = lax.broadcasted_iota(jnp.int32, (1, 128), 1) >= HD

    def attend(column, window, row0, count, valid):
        for quad in range(HEADS // 4):
            lanes = slice(quad * 256, quad * 256 + 256)
            q = q_ref[column, row0 : row0 + count, lanes]
            nil = jnp.zeros_like(q)
            q4 = jnp.concatenate([jnp.where(head_lane == h, q, nil) for h in range(4)], axis=0)
            expo = jnp.exp(dot(q4, kv_ref[window, :, lanes], 1, 1))
            if valid is not None:
                expo = jnp.where(valid, expo, 0.0)
            probs = (expo * (1.0 / jnp.sum(expo, axis=-1, keepdims=True))).astype(BF)
            both = dot(probs, kv_ref[window, :, D + quad * 256 : D + quad * 256 + 256])
            for two in range(2):
                part = both[2 * two * count : 2 * (two + 1) * count, two * 128 : (two + 1) * 128]
                spot = slice(quad * 256 + two * 128, quad * 256 + two * 128 + 128)
                att_ref[row0 : row0 + count, spot] = jnp.where(odd_lane, part[count:], part[:count]).astype(BF)

    lev = lax.axis_index("lev")
    inside = (lev > 0, lev < lax.axis_size("lev") - 1)
    plain = [(key < 96) | ok for ok in inside]
    corner = [(key < 48) | ((key < 144) & ((key + 16) % 32 < 16)) | ok for ok in inside]

    for side in range(2):
        first = 3 * (1 - side)
        attend(0, first, 48 * side, 48, corner[0])
        attend(0, first + 1, 96 + 96 * side, 96, None)
        attend(0, first + 2, 288 + 48 * side, 48, corner[1])

    def finish(rows):
        natural = dot(perm_ref[1], att_ref[...]).astype(BF)
        return (rows.astype(F32) + dot(natural, wproj_ref[...])).astype(BF)

    done = finish(rows)
    out_ref[28:32] = done[:192].reshape(4, 3, 16, D)
    out_ref[0:4] = done[192:].reshape(4, 3, 16, D)
    swap_back_a()

    def column_loop(column, carry):
        first = 3 + 3 * column
        attend(column, first, 0, 96, plain[0])
        attend(column, first + 1, 96, 192, None)
        attend(column, first + 2, 288, 96, plain[1])
        rows = latent_ref[pl.ds(8 * column - 4, 8)].reshape(384, D)
        out_ref[pl.ds(8 * column - 4, 8)] = finish(rows).reshape(8, 3, 16, D)

        @pl.when(column == 2)
        def _():
            swap_back_b()

        return carry

    lax.fori_loop(1, 4, column_loop, 0)
    close_a(total_ref)
    close_b(total_ref)


def finish_kernel(done_hbm, total_ref, we_ref, queries_ref, wkv_hbm, out_ref, gembed_ref, gkv_ref, gout_ref, done_vmem, wkv_ref, gkv_vmem, gout_vmem, load_sem, save_sem, factor):
    blocks = [pl.ds(8 * i, 8) for i in range(4)]
    loads = fetch([(done_hbm.at[block], done_vmem.at[block]) for block in blocks] + [(wkv_hbm, wkv_ref)], load_sem)
    for j in range(4):
        gout_vmem[:, j * 128 : (j + 1) * 128] = total_ref[j * D : (j + 1) * D, :].astype(F32) * factor
    saves = fetch([(gout_vmem, gout_ref)], save_sem.at[pl.ds(5, 1)])
    for load in loads[:4]:
        load.wait()
    saves += fetch([(done_vmem.at[block], out_ref.at[block]) for block in blocks], save_sem)
    qm = query_rows(queries_ref[...].astype(F32)).astype(BF)
    values = total_ref[4 * D : 5 * D, :]
    keys = dot(qm, total_ref[5 * D : 5 * D + 32, :][:24], 0, 0)
    khigh, klow = split(keys)
    we = we_ref[...]
    gkv_vmem[:, D:] = dot(we, values, 0, 1) * factor
    gkv_vmem[:, :D] = (dot(we, khigh, 0, 1) + dot(we, klow, 0, 1)) * factor
    saves += fetch([(gkv_vmem, gkv_ref)], save_sem.at[pl.ds(4, 1)])
    loads[4].wait()
    wk, wv = wkv_ref[:, :D], wkv_ref[:, D:]
    grad = dot(khigh, wk, 0, 1) + dot(klow, wk, 0, 1) + dot(values, wv, 0, 1)
    gembed_ref[...] = grad[:F] * factor
    for save in saves:
        save.wait()


def whole(shape, dtype):
    return jax.ShapeDtypeStruct(shape, dtype)


def params(**kw):
    return pltpu.CompilerParams(vmem_limit_bytes=VMEM_LIMIT, **kw)


def per_device(inputs, level_ids, level_table, w_embed, queries, w_kv, w_out, gain, w_qkv, w_proj, d_latent):
    bands = lax.axis_size("lev")
    tiles = lax.axis_size("tile")
    lon_rows, lat_rows = d_latent.shape[:2]
    vmem = pl.BlockSpec(memory_space=pltpu.VMEM)
    anywhere = pl.BlockSpec(memory_space=pl.ANY)
    d_nat = d_latent.transpose(0, 2, 1, 3)
    latent, terms, w2, woutp, far, we = pl.pallas_call(
        pool_kernel,
        in_specs=[pl.BlockSpec(memory_space=pltpu.SMEM), vmem, anywhere, vmem, vmem, vmem, anywhere, anywhere],
        out_specs=(vmem,) * 6,
        out_shape=(whole(d_nat.shape, BF), whole((TERMS, KX), BF), whole((MV, 2 * KX), BF), whole((D, D), BF), whole((LEVELS, F, 512), BF), whole((KX, D), BF)),
        scratch_shapes=[
            pltpu.VMEM((LEVELS, D, 128), F32),
            pltpu.VMEM((D, 384), F32),
            pltpu.VMEM((D, 384), BF),
            pltpu.VMEM((MV, 4 * LEVELS * 128), BF),
            pltpu.VMEM((KX, 4 * LEVELS * 128), BF),
            pltpu.VMEM((MV, KX), F32),
            pltpu.VMEM((4 * D, 128), F32),
            pltpu.VMEM((F * 32, 128), F32),
            pltpu.VMEM((4 * F, 1024), BF),
            pltpu.VMEM((4 * F, 1024), BF),
            pltpu.VMEM((4, LEVELS, F, 128), BF),
            pltpu.VMEM((LEVELS, F, 256), BF),
            pltpu.VMEM((2, LEVELS, F, 128), BF),
            pltpu.VMEM((4, LEVELS, F, 128), BF),
            pltpu.VMEM((LEVELS, F, 512), BF),
            pltpu.VMEM(d_nat.shape, BF),
            pltpu.VMEM((D, 2 * D), BF),
            pltpu.VMEM((D, D), BF),
            pltpu.SemaphoreType.DMA((3,)),
            pltpu.SemaphoreType.DMA((58,)),
            pltpu.SemaphoreType.DMA((58,)),
        ],
        compiler_params=params(collective_id=2, has_side_effects=True),
        name="pool",
    )(level_ids, inputs[0], d_nat, level_table, w_embed, queries, w_kv, w_out)

    factor = 1.0 / math.sqrt(lon_rows * lat_rows * bands * tiles)
    done, total = pl.pallas_call(
        window_kernel,
        in_specs=[vmem, vmem, anywhere, vmem, vmem, vmem, anywhere, anywhere],
        out_specs=(vmem, vmem),
        out_shape=(whole(d_nat.shape, BF), whole((2, 8, CHUNK, KX), BF)),
        scratch_shapes=[
            pltpu.VMEM((LEVELS, D, 128), F32),
            pltpu.VMEM((D, 384), BF),
            pltpu.VMEM((4, 384, D), BF),
            pltpu.VMEM((15, 192, 2 * D), BF),
            pltpu.VMEM((384, D), BF),
            pltpu.VMEM((2, 384, 384), BF),
            pltpu.VMEM((8, CHUNK, KX), BF),
            pltpu.VMEM((8, CHUNK, KX), BF),
            pltpu.VMEM((7, CHUNK, KX), BF),
            pltpu.VMEM((8, CHUNK, KX), BF),
            pltpu.VMEM((2, 8, CHUNK, KX), BF),
            pltpu.VMEM(d_nat.shape, BF),
            pltpu.VMEM((D, 3 * D), BF),
            pltpu.VMEM((D, D), BF),
            pltpu.SemaphoreType.DMA((3,)),
            pltpu.SemaphoreType.DMA((46,)),
            pltpu.SemaphoreType.DMA((46,)),
        ],
        compiler_params=params(collective_id=1, has_side_effects=True),
        name="windows",
    )(terms.reshape(2, 8, CHUNK, KX), far, latent, w2, woutp, gain.reshape(1, D), w_qkv, w_proj)

    out, gembed, gkv, gout = pl.pallas_call(
        functools.partial(finish_kernel, factor=factor),
        in_specs=[anywhere, vmem, vmem, vmem, anywhere],
        out_specs=(anywhere, vmem, anywhere, anywhere),
        out_shape=(whole(d_nat.shape, BF), whole((F, D), F32), whole((D, 2 * D), F32), whole((D, D), F32)),
        scratch_shapes=[
            pltpu.VMEM(d_nat.shape, BF),
            pltpu.VMEM((D, 2 * D), BF),
            pltpu.VMEM((D, 2 * D), F32),
            pltpu.VMEM((D, D), F32),
            pltpu.SemaphoreType.DMA((5,)),
            pltpu.SemaphoreType.DMA((6,)),
        ],
        compiler_params=params(),
        name="finish",
    )(done, total.reshape(TERMS, KX), we, queries, w_kv)
    return (out.transpose(0, 2, 1, 3), gembed, gkv, gout)


def solution(mesh):
    placed = (P("lev", None, "tile", None),) + (P(),) * 9 + (P("tile", "lev", None, None),)
    return jax.shard_map(
        per_device,
        mesh=mesh,
        in_specs=placed,
        out_specs=(P("tile", "lev", None, None), P(), P(), P()),
        check_vma=False,
    )
```

```python
import functools
import math

import jax
import jax.numpy as jnp
import numpy as np
from jax import lax
from jax.experimental import pallas as pl
from jax.experimental.pallas import tpu as pltpu
from jax.sharding import PartitionSpec as P

HD = 64
HEADS = 8
WIN = 8
D = 512
F = 80
LEVELS = 8
LATENT = 3
KX = 128
MV = 544
CHUNK = 176
UNROLL = 4
TERMS = 16 * CHUNK
BF = jnp.bfloat16
F32 = jnp.float32
VMEM_LIMIT = 56 * 1024 * 1024


def dot(a, b, ca=1, cb=0):
    return lax.dot_general(a, b, (((ca,), (cb,)), ((), ())), preferred_element_type=F32)


def split(value):
    high = value.astype(BF)
    return high, (value - high.astype(F32)).astype(BF)


def place(lev, tile):
    return {"lev": lev, "tile": tile}


def remote(src, dst, send, recv, device):
    return pltpu.make_async_remote_copy(src_ref=src, dst_ref=dst, send_sem=send, recv_sem=recv, device_id=device, device_id_type=pl.DeviceIdType.MESH)


def fetch(pairs, sems):
    loads = [pltpu.make_async_copy(src, dst, sems.at[i]) for i, (src, dst) in enumerate(pairs)]
    for load in loads:
        load.start()
    return loads


def query_rows(queries):
    rows = jnp.concatenate([jnp.broadcast_to(queries[q : q + 1], (HEADS, D)) for q in range(LATENT)], axis=0)
    head = lax.broadcasted_iota(jnp.int32, (LATENT * HEADS, D), 0) % HEADS
    lane = lax.broadcasted_iota(jnp.int32, (LATENT * HEADS, D), 1) // HD
    return jnp.where(head == lane, rows, 0.0)


def fold_weights(ids_ref, table_ref, embed_ref, queries_ref, wkv_ref, wout_ref, w2_ref, woutp_ref, we_ref):
    slab = lax.broadcasted_iota(jnp.int32, (16, 1), 0)
    wanted = jnp.full((16, 1), -1, jnp.int32)
    for l in range(LEVELS):
        wanted = jnp.where(slab == l, ids_ref[l], wanted)
    rows = jnp.zeros((16, D), F32)
    for entry in range(table_ref.shape[0]):
        rows = jnp.where(wanted == entry, table_ref[entry : entry + 1, :].astype(F32), rows)
    we_ref[0:F, :] = embed_ref[...]
    we_ref[F : F + 16, :] = rows.astype(BF)
    we_ref[F + 16 :, :] = jnp.zeros((KX - F - 16, D), BF)
    row = lax.broadcasted_iota(jnp.int32, (D, 1), 0)
    lane = lax.broadcasted_iota(jnp.int32, (D, D), 1)
    mix = jnp.where(lane == (row % HEADS) * HD + row // HEADS, 1.0, 0.0).astype(BF)
    we = we_ref[...]
    wv = dot(mix, wkv_ref[:, D:], 1, 1).astype(BF)
    woutp_ref[...] = dot(mix, wout_ref[...]).astype(BF)
    high, low = split(dot(wv, we, 1, 1))
    w2_ref[0:D, 0:KX] = high
    w2_ref[0:D, KX:] = low
    qm = query_rows(queries_ref[...].astype(F32)).astype(BF)
    shigh, slow = split(dot(qm, wkv_ref[:, :D], 1, 1) * (1.0 / math.sqrt(HD)))
    score = dot(shigh, we, 1, 1) + dot(slow, we, 1, 1)
    score = jnp.concatenate([score, jnp.zeros((MV - D - 24, KX), F32)], axis=0)
    high, low = split(score)
    w2_ref[D:MV, 0:KX] = high
    w2_ref[D:MV, KX:] = low


def level_rows(x, level):
    row = lax.broadcasted_iota(jnp.int32, (KX - F, 128), 0)
    ones = jnp.where(row == level, 1.0, 0.0).astype(BF)
    return jnp.concatenate([x, ones], axis=0)


def forward_levels(read, w2_ref, vals_ref):
    scores = []
    pairs = []
    for pair in range(LEVELS // 2):
        pixels = jnp.concatenate([level_rows(read(2 * pair), 2 * pair), level_rows(read(2 * pair + 1), 2 * pair + 1)], axis=1)
        pairs.append(pixels)
        out = dot(w2_ref[...], jnp.concatenate([pixels, pixels], axis=0))
        vals_ref[2 * pair] = out[:D, :128]
        vals_ref[2 * pair + 1] = out[:D, 128:]
        scores.append(out[D : D + 24, :128])
        scores.append(out[D : D + 24, 128:])
    expo = [jnp.exp(s) for s in scores]
    total = expo[0]
    for e in expo[1:]:
        total = total + e
    inverse = 1.0 / total
    return pairs, [(e * inverse).astype(BF).astype(F32) for e in expo]


def select(rows, lanes, want):
    row = lax.broadcasted_iota(jnp.int32, (rows, lanes), 0)
    return jnp.where(row == want, 1.0, 0.0).astype(BF)


def lane_ids(lanes, start=0):
    return lax.broadcasted_iota(jnp.int32, (1, lanes), 1) + start


def inside_row(lon, lat):
    return jnp.where((lat >= 0) & (lat < 128), lon * 128 + lat, -1)


def exchange_stages(x_ref, pixels_ref, xa_ref, xb_ref, own_ref, near_ref, side_ref, mine_ref, rim_ref, send_sem, recv_sem):
    lev, tile = lax.axis_index("lev"), lax.axis_index("tile")
    bands, tiles = lax.axis_size("lev"), lax.axis_size("tile")
    next_tile, last_tile = lax.rem(tile + 1, tiles), lax.rem(tile + tiles - 1, tiles)
    levs = [lax.rem(lev + off, bands) for off in range(bands)]

    def copy(src, dst, slot, device):
        return remote(src, dst, send_sem.at[slot], recv_sem.at[slot], device)

    own, near, east, west = [], [], [], []
    for off in range(1, bands):
        own.append(lambda g, off=off: copy(own_ref.at[g, levs[off]], mine_ref.at[g, lev], 30 + g * 7 + off - 1, place(levs[off], tile)))
        near.append(copy(near_ref.at[levs[off]], rim_ref.at[lev, :, 256:512], off - 1, place(levs[off], tile)))
    for off in range(bands):
        east.append(copy(side_ref.at[0, levs[off]], rim_ref.at[lev, :, 0:128], 7 + off, place(levs[off], next_tile)))
        west.append(copy(side_ref.at[1, levs[off]], rim_ref.at[lev, :, 128:256], 15 + off, place(levs[off], last_tile)))

    def greet():
        barrier = pltpu.get_barrier_semaphore()
        for off in range(1, bands):
            pl.semaphore_signal(barrier, inc=1, device_id=place(levs[off], tile), device_id_type=pl.DeviceIdType.MESH)
        for off in range(bands):
            for side in (next_tile, last_tile):
                pl.semaphore_signal(barrier, inc=1, device_id=place(levs[off], side), device_id_type=pl.DeviceIdType.MESH)

    def send_own():
        pixels_ref[...] = x_ref[...].reshape(F * 32, 128).astype(F32)
        for lon in range(32):
            plane = pixels_ref[pl.ds(lon, F, stride=32), :].astype(BF)
            xa_ref[(lon // 8) * F : (lon // 8 + 1) * F, (lon % 8) * 128 : (lon % 8 + 1) * 128] = plane
            moved = (lon + 4) % 32
            xb_ref[(moved // 8) * F : (moved // 8 + 1) * F, (moved % 8) * 128 : (moved % 8 + 1) * 128] = plane
        rows = xa_ref[...]
        for two in range(bands // 2):
            j = lane_ids(256)
            want = ((j % 128) // 16) * 128 + 16 * (2 * two + j // 128) + j % 16
            out = dot(rows, select(1024, 256, want)).astype(BF)
            for c in range(4):
                for half in range(2):
                    own_ref[c, 2 * two + half] = out[c * F : (c + 1) * F, half * 128 : (half + 1) * 128]
        pl.semaphore_wait(pltpu.get_barrier_semaphore(), 3 * bands - 1)
        for g in range(4):
            for c in own:
                c(g).start()
        for g in range(4):
            mine_ref[g, lev] = own_ref[g, lev]

    def sort_rim():
        rows = xb_ref[...]
        for four in range(2):
            j = lane_ids(256)
            band = 4 * four + j // 64
            lat = 16 * band + j % 4 + jnp.where(j % 64 < 32, -4, 16)
            out = dot(rows, select(1024, 256, inside_row((j % 32) // 4, lat))).astype(BF)
            for b in range(4):
                lanes = slice(64 * b, 64 * b + 64)
                for c in range(2):
                    pair = [out[k * F : (k + 1) * F, lanes] for k in (2 * c, 2 * c + 1)]
                    near_ref[4 * four + b, :, c * 128 : (c + 1) * 128] = jnp.concatenate(pair, axis=1)
        rows = jnp.concatenate([xb_ref[0:F, 0:512], xb_ref[0:F, 512:1024]], axis=0)
        for two in range(bands // 2):
            j = lane_ids(256)
            k = j % 128
            thin = k % 16
            wide = k - 32
            lat = jnp.where(k < 16, 4 + thin % 4, jnp.where(k < 32, thin % 4, jnp.where(k < 64, 8 + wide % 8, jnp.where(k < 80, 16 + thin % 4, 20 + thin % 4))))
            lon = jnp.where((k >= 32) & (k < 64), wide // 8, thin // 4)
            lat = jnp.where(k < 96, 16 * (2 * two + j // 128) - 4 + lat, -1)
            out = dot(rows, select(512, 256, inside_row(lon, lat))).astype(BF)
            for side in range(2):
                for half in range(2):
                    side_ref[side, 2 * two + half] = out[side * F : (side + 1) * F, half * 128 : (half + 1) * 128]
        rim_ref[lev, :, 256:512] = near_ref[lev]

    def take_own(group):
        for c in own:
            c(group).wait_recv()

        @pl.when(group == 1)
        def _():
            for c in near + east + west:
                c.start()

    def take_rim():
        for c in near + east + west:
            c.wait_recv()
        for c in near + east + west + [c(g) for c in own for g in range(4)]:
            c.wait_send()

    return greet, send_own, sort_rim, take_own, take_rim


def pool_kernel(ids_ref, x_ref, d_ref, table_ref, embed_ref, queries_ref, wkv_ref, wout_ref, latent_ref, terms_ref, w2_ref, woutp_ref, far_ref, we_ref, vals_ref, dpool_ref, pooled_ref, dv_ref, seen_ref, tacc_ref, gacc_ref, pixels_ref, xa_ref, xb_ref, own_ref, near_ref, side_ref, mine_ref, rim_ref, d_vmem, wkv_vmem, wout_vmem, load_sem, send_sem, recv_sem):
    loads = fetch(((wkv_ref, wkv_vmem), (wout_ref, wout_vmem), (d_ref, d_vmem)), load_sem)
    greet, send_own, sort_rim, take_own, take_rim = exchange_stages(x_ref, pixels_ref, xa_ref, xb_ref, own_ref, near_ref, side_ref, mine_ref, rim_ref, send_sem, recv_sem)
    greet()
    send_own()
    sort_rim()
    loads[0].wait()
    loads[1].wait()
    fold_weights(ids_ref, table_ref, embed_ref, queries_ref, wkv_vmem, wout_vmem, w2_ref, woutp_ref, we_ref)
    gacc_ref[...] = jnp.zeros_like(gacc_ref)
    loads[2].wait()

    def group_loop(group, carry):
        take_own(group)
        pool_group(group, mine_ref, d_vmem, w2_ref, woutp_ref, latent_ref, vals_ref, dpool_ref, pooled_ref, dv_ref, seen_ref, gacc_ref)
        return carry

    lax.fori_loop(0, 4, group_loop, 0)
    tacc_ref[...] = dot(dv_ref[...], seen_ref[...], 1, 1)
    for h in range(HEADS):
        for j in range(4):
            terms_ref[j * D + h * HD : j * D + (h + 1) * HD, :] = gacc_ref[pl.ds(j * D + h, HD, stride=HEADS), :].astype(BF)
        terms_ref[4 * D + h * HD : 4 * D + (h + 1) * HD, :] = tacc_ref[pl.ds(h, HD, stride=HEADS), :].astype(BF)
    terms_ref[5 * D : 5 * D + MV - D, :] = tacc_ref[D:MV, :].astype(BF)
    terms_ref[5 * D + MV - D :, :] = jnp.zeros((TERMS - 5 * D - MV + D, KX), BF)
    take_rim()
    far_ref[...] = rim_ref[...]


def pool_group(group, x_ref, d_ref, w2_ref, woutp_ref, latent_ref, vals_ref, dpool_ref, pooled_ref, dv_ref, seen_ref, gacc_ref):
    column = pl.multiple_of(group * (LEVELS * 128), 128)
    pairs, probs = forward_levels(lambda l: x_ref[group, l], w2_ref, vals_ref)
    d_rows = jnp.concatenate([d_ref[pl.ds(8 * group, 8), q].reshape(128, D) for q in range(LATENT)], axis=0)
    dpool_ref[...] = dot(woutp_ref[...], d_rows, 1, 1)
    parts = [[probs[l][q * HEADS : (q + 1) * HEADS] for q in range(LATENT)] for l in range(LEVELS)]

    def mix_loop(i, carry):
        base = pl.multiple_of(i * 16, 16)
        pooled = [[], [], []]
        dvals = [[] for _ in range(LEVELS)]
        for e in range(2):
            rows = pl.ds(base + 8 * e, 8)
            dq = [dpool_ref[rows, q * 128 : (q + 1) * 128] for q in range(LATENT)]
            acc = [None] * LATENT
            for l in range(LEVELS):
                v = vals_ref[l, rows, :]
                for q in range(LATENT):
                    term = parts[l][q] * v
                    acc[q] = term if acc[q] is None else acc[q] + term
                dvals[l].append(parts[l][0] * dq[0] + parts[l][1] * dq[1] + parts[l][2] * dq[2])
            for q in range(LATENT):
                pooled[q].append(acc[q])
        for q in range(LATENT):
            pooled_ref[pl.ds(base, 16), q * 128 : (q + 1) * 128] = jnp.concatenate(pooled[q], axis=0).astype(BF)
        for l in range(LEVELS):
            dv_ref[pl.ds(base, 16), pl.ds(column + l * 128, 128)] = jnp.concatenate(dvals[l], axis=0).astype(BF)
        return carry

    lax.fori_loop(0, D // 16, mix_loop, 0, unroll=UNROLL)

    def dprob_loop(i, carry):
        acc = list(carry)
        for e in range(2):
            rows = pl.ds(pl.multiple_of(i * 16 + 8 * e, 8), 8)
            dq = [dpool_ref[rows, q * 128 : (q + 1) * 128] for q in range(LATENT)]
            for l in range(LEVELS):
                v = vals_ref[l, rows, :]
                for q in range(LATENT):
                    acc[l * LATENT + q] = acc[l * LATENT + q] + dq[q] * v
        return tuple(acc)

    zero = jnp.zeros((HEADS, 128), F32)
    dprob = lax.fori_loop(0, D // 16, dprob_loop, (zero,) * (LEVELS * LATENT), unroll=UNROLL)
    scale = 1.0 / math.sqrt(HD)
    delta = []
    for q in range(LATENT):
        total = parts[0][q] * dprob[q]
        for l in range(1, LEVELS):
            total = total + parts[l][q] * dprob[l * LATENT + q]
        delta.append(total)
    for l in range(LEVELS):
        ds = [parts[l][q] * (dprob[l * LATENT + q] - delta[q]) * scale for q in range(LATENT)]
        dv_ref[D:MV, pl.ds(column + l * 128, 128)] = jnp.concatenate(ds + [zero], axis=0).astype(BF)

    for pair in range(LEVELS // 2):
        seen_ref[:, pl.ds(column + pair * 256, 256)] = pairs[pair]
    pooled = pooled_ref[...]
    gterm = dot(pooled, d_rows)
    for j in range(4):
        gacc_ref[j * D : (j + 1) * D, :] += gterm[:, j * 128 : (j + 1) * 128]
    latent = dot(pooled, woutp_ref[...], 0, 0).astype(BF)
    for q in range(LATENT):
        latent_ref[pl.ds(8 * group, 8), q] = latent[q * 128 : (q + 1) * 128].reshape(8, 16, D)


def normalise(values, gain):
    mean = jnp.mean(values, axis=-1, keepdims=True)
    centred = values - mean
    var = jnp.mean(centred * centred, axis=-1, keepdims=True)
    return (centred * lax.rsqrt(var + 1e-05) * gain).astype(BF)


def permutation(dim):
    dst = lax.broadcasted_iota(jnp.int32, (384, 1) if dim == 0 else (1, 384), dim)
    src = lax.broadcasted_iota(jnp.int32, (384, 384), 1 - dim)
    mid, high = dst - 96, dst - 288
    low = (dst // 4) * 16 + dst % 4
    mid = (mid // 8) * 16 + 4 + mid % 8
    high = (high // 4) * 16 + 12 + high % 4
    want = jnp.where(dst < 96, low, jnp.where(dst < 288, mid, high))
    return jnp.where(src == want, 1.0, 0.0).astype(BF)


def sum_stages(start, size, slot0, terms_ref, halves_ref, pair_ref, part_ref, band_ref, full_ref, send_sem, recv_sem):
    cut = pl.ds(start, size)
    lev, tile = lax.axis_index("lev"), lax.axis_index("tile")
    bands, tiles = lax.axis_size("lev"), lax.axis_size("tile")
    groups = tiles // 2
    group, core = tile // 2, lax.rem(tile, 2)

    def copy(src, dst, slot, device):
        return remote(src, dst, send_sem.at[slot0 + slot], recv_sem.at[slot0 + slot], device)

    other = place(lev, 2 * group + 1 - core)
    lev_peers = [place(lax.rem(lev + off, bands), tile) for off in range(1, bands)]
    group_ids = [lax.rem(group + off, groups) for off in range(1, groups)]
    group_peers = [place(lev, 2 * g + core) for g in group_ids]
    swap = copy(terms_ref.at[1 - core, :, cut, :], halves_ref.at[:, cut, :], 0, other)
    first = [copy(pair_ref.at[g, cut, :], part_ref.at[i, cut, :], 1 + i, group_peers[i]) for i, g in enumerate(group_ids)]
    second = [copy(band_ref.at[lev, cut, :], band_ref.at[lev, cut, :], 8 + i, peer) for i, peer in enumerate(lev_peers)]
    third = [copy(full_ref.at[core, group, cut, :], full_ref.at[core, group, cut, :], 15 + i, peer) for i, peer in enumerate(group_peers)]
    back = copy(full_ref.at[core, :, cut, :], full_ref.at[core, :, cut, :], 22, other)

    def greet():
        barrier = pltpu.get_barrier_semaphore()
        for peer in group_peers + lev_peers + [other]:
            pl.semaphore_signal(barrier, inc=1, device_id=peer, device_id_type=pl.DeviceIdType.MESH)
        pl.semaphore_wait(barrier, groups + bands - 1)

    def begin():
        swap.start()

    def over_group():
        swap.wait_recv()
        pair_ref[:, cut, :] = (terms_ref[core, :, cut, :].astype(F32) + halves_ref[:, cut, :].astype(F32)).astype(BF)
        for c in first:
            c.start()

    def over_lev():
        total = pair_ref[group, cut, :].astype(F32)
        for i, c in enumerate(first):
            c.wait_recv()
            total = total + part_ref[i, cut, :].astype(F32)
        band_ref[lev, cut, :] = total.astype(BF)
        for c in second:
            c.start()

    def gather():
        for c in second:
            c.wait_recv()
        total = band_ref[0, cut, :].astype(F32)
        for b in range(1, bands):
            total = total + band_ref[b, cut, :].astype(F32)
        full_ref[core, group, cut, :] = total.astype(BF)
        for c in third:
            c.start()

    def swap_back():
        for c in third:
            c.wait_recv()
        back.start()

    def close(total_ref):
        back.wait_recv()
        total_ref[:, :, cut, :] = full_ref[:, :, cut, :]
        for c in [swap] + first + second + third + [back]:
            c.wait_send()

    return greet, begin, over_group, over_lev, gather, swap_back, close


def window_kernel(terms_ref, xh_ref, latent_hbm, w2_ref, woutp_ref, gain_ref, wqkv_hbm, wproj_hbm, out_ref, total_ref, vals_ref, pooled_ref, q_ref, kv_ref, att_ref, perm_ref, halves_ref, pair_ref, part_ref, band_ref, full_ref, latent_ref, wqkv_ref, wproj_ref, load_sem, send_sem, recv_sem):
    loads = fetch(((wqkv_hbm, wqkv_ref), (latent_hbm, latent_ref), (wproj_hbm, wproj_ref)), load_sem)
    gain = gain_ref[...]
    buffers = (terms_ref, halves_ref, pair_ref, part_ref, band_ref, full_ref, send_sem, recv_sem)
    greet, begin_a, over_group_a, over_lev_a, gather_a, swap_back_a, close_a = sum_stages(0, 96, 0, *buffers)
    _, begin_b, over_group_b, over_lev_b, gather_b, swap_back_b, close_b = sum_stages(96, CHUNK - 96, 23, *buffers)
    greet()
    begin_a()
    begin_b()
    perm_ref[0] = permutation(0)
    perm_ref[1] = permutation(1)
    loads[0].wait()

    def halo(group, carry):
        lane0 = pl.multiple_of(group * 128, 128)
        _, probs = forward_levels(lambda l: xh_ref[l, :, pl.ds(lane0, 128)], w2_ref, vals_ref)
        parts = [[probs[l][q * HEADS : (q + 1) * HEADS] for q in range(LATENT)] for l in range(LEVELS)]

        def mix_loop(i, inner):
            base = pl.multiple_of(i * 16, 16)
            pooled = [[], [], []]
            for e in range(2):
                rows = pl.ds(base + 8 * e, 8)
                acc = [None] * LATENT
                for l in range(LEVELS):
                    v = vals_ref[l, rows, :]
                    for q in range(LATENT):
                        term = parts[l][q] * v
                        acc[q] = term if acc[q] is None else acc[q] + term
                for q in range(LATENT):
                    pooled[q].append(acc[q])
            for q in range(LATENT):
                pooled_ref[pl.ds(base, 16), q * 128 : (q + 1) * 128] = jnp.concatenate(pooled[q], axis=0).astype(BF)
            return inner

        lax.fori_loop(0, D // 16, mix_loop, 0, unroll=UNROLL)
        latent = dot(pooled_ref[...], woutp_ref[...], 0, 0).astype(BF).astype(F32)
        normed = normalise(latent, gain)
        kv = dot(normed, wqkv_ref[:, D:]).astype(BF)

        @pl.when(group < 2)
        def _():
            first = group * 3
            for q in range(LATENT):
                row = q * 128
                kv_ref[first, 48 + 32 * q : 80 + 32 * q, :] = kv[row : row + 32]
                kv_ref[first + 1, 96 + 32 * q : 128 + 32 * q, :] = kv[row + 32 : row + 64]
                kv_ref[first + 2, 48 + 32 * q : 80 + 32 * q, :] = kv[row + 64 : row + 96]

        @pl.when(group == 2)
        def _():
            for q in range(LATENT):
                row = q * 128
                near = slice(144 + 16 * q, 160 + 16 * q)
                kv_ref[3, near, :] = kv[row : row + 16]
                kv_ref[0, near, :] = kv[row + 16 : row + 32]
                kv_ref[5, near, :] = kv[row + 32 : row + 48]
                kv_ref[2, near, :] = kv[row + 48 : row + 64]

        def column_rim(half, column):
            for q in range(LATENT):
                row = q * 128 + half * 64
                near = slice(96 + 32 * q, 128 + 32 * q)
                kv_ref[3 + 3 * column, near, :] = kv[row : row + 32]
                kv_ref[5 + 3 * column, near, :] = kv[row + 32 : row + 64]

        @pl.when(group == 2)
        def _():
            column_rim(1, 1)

        @pl.when(group == 3)
        def _():
            column_rim(0, 2)
            column_rim(1, 3)

        @pl.when(group == 0)
        def _():
            over_group_a()

        @pl.when(group == 2)
        def _():
            over_lev_a()
            over_group_b()
        return carry

    lax.fori_loop(0, 4, halo, 0)
    loads[1].wait()
    loads[2].wait()

    def project(rows, column):
        normed = normalise(rows.astype(F32), gain)
        normed = dot(perm_ref[0], normed).astype(BF)
        q_ref[column] = (dot(normed, wqkv_ref[:, :D]).astype(BF).astype(F32) * (1.0 / math.sqrt(HD))).astype(BF)
        return dot(normed, wqkv_ref[:, D:]).astype(BF)

    rows = jnp.concatenate([latent_ref[28:32].reshape(192, D), latent_ref[0:4].reshape(192, D)], axis=0)
    kv = project(rows, 0)
    for side in range(2):
        first = 3 * (1 - side)
        kv_ref[first, 0:48, :] = kv[48 * side : 48 * side + 48]
        kv_ref[first + 1, 0:96, :] = kv[96 + 96 * side : 192 + 96 * side]
        kv_ref[first + 2, 0:48, :] = kv[288 + 48 * side : 336 + 48 * side]

    gather_a()
    over_lev_b()

    def own(column, carry):
        rows = latent_ref[pl.ds(8 * column - 4, 8)].reshape(384, D)
        kv = project(rows, column)
        first = 3 + 3 * column
        kv_ref[first, 0:96, :] = kv[0:96]
        kv_ref[first + 1, 0:192, :] = kv[96:288]
        kv_ref[first + 2, 0:96, :] = kv[288:384]
        return carry

    lax.fori_loop(1, 4, own, 0)
    swap_back_a()
    gather_b()

    key = lax.broadcasted_iota(jnp.int32, (1, 192), 1)
    head_lane = lax.broadcasted_iota(jnp.int32, (1, 256), 1) // HD
    odd_lane = lax.broadcasted_iota(jnp.int32, (1, 128), 1) >= HD

    def attend(column, window, row0, count, valid):
        for quad in range(HEADS // 4):
            lanes = slice(quad * 256, quad * 256 + 256)
            q = q_ref[column, row0 : row0 + count, lanes]
            nil = jnp.zeros_like(q)
            q4 = jnp.concatenate([jnp.where(head_lane == h, q, nil) for h in range(4)], axis=0)
            expo = jnp.exp(dot(q4, kv_ref[window, :, lanes], 1, 1))
            if valid is not None:
                expo = jnp.where(valid, expo, 0.0)
            probs = (expo * (1.0 / jnp.sum(expo, axis=-1, keepdims=True))).astype(BF)
            both = dot(probs, kv_ref[window, :, D + quad * 256 : D + quad * 256 + 256])
            for two in range(2):
                part = both[2 * two * count : 2 * (two + 1) * count, two * 128 : (two + 1) * 128]
                spot = slice(quad * 256 + two * 128, quad * 256 + two * 128 + 128)
                att_ref[row0 : row0 + count, spot] = jnp.where(odd_lane, part[count:], part[:count]).astype(BF)

    lev = lax.axis_index("lev")
    inside = (lev > 0, lev < lax.axis_size("lev") - 1)
    plain = [(key < 96) | ok for ok in inside]
    corner = [(key < 48) | ((key < 144) & ((key + 16) % 32 < 16)) | ok for ok in inside]

    for side in range(2):
        first = 3 * (1 - side)
        attend(0, first, 48 * side, 48, corner[0])
        attend(0, first + 1, 96 + 96 * side, 96, None)
        attend(0, first + 2, 288 + 48 * side, 48, corner[1])

    def finish(rows):
        natural = dot(perm_ref[1], att_ref[...]).astype(BF)
        return (rows.astype(F32) + dot(natural, wproj_ref[...])).astype(BF)

    done = finish(rows)
    out_ref[28:32] = done[:192].reshape(4, 3, 16, D)
    out_ref[0:4] = done[192:].reshape(4, 3, 16, D)

    def column_loop(column, carry):
        first = 3 + 3 * column
        attend(column, first, 0, 96, plain[0])
        attend(column, first + 1, 96, 192, None)
        attend(column, first + 2, 288, 96, plain[1])
        rows = latent_ref[pl.ds(8 * column - 4, 8)].reshape(384, D)
        out_ref[pl.ds(8 * column - 4, 8)] = finish(rows).reshape(8, 3, 16, D)

        @pl.when(column == 1)
        def _():
            swap_back_b()

        return carry

    lax.fori_loop(1, 4, column_loop, 0)
    close_a(total_ref)
    close_b(total_ref)


def finish_kernel(done_ref, total_ref, we_ref, queries_ref, wkv_ref, out_ref, gembed_ref, gkv_ref, gout_ref, save_sem, factor):
    saves = fetch([(done_ref, out_ref)], save_sem)
    for j in range(4):
        gout_ref[:, j * 128 : (j + 1) * 128] = total_ref[j * D : (j + 1) * D, :].astype(F32) * factor
    qm = query_rows(queries_ref[...].astype(F32)).astype(BF)
    values = total_ref[4 * D : 5 * D, :]
    keys = dot(qm, total_ref[5 * D : 5 * D + 32, :][:24], 0, 0)
    khigh, klow = split(keys)
    we = we_ref[...]
    gkv_ref[:, D:] = dot(we, values, 0, 1) * factor
    gkv_ref[:, :D] = (dot(we, khigh, 0, 1) + dot(we, klow, 0, 1)) * factor
    wk, wv = wkv_ref[:, :D], wkv_ref[:, D:]
    grad = dot(khigh, wk, 0, 1) + dot(klow, wk, 0, 1) + dot(values, wv, 0, 1)
    gembed_ref[...] = grad[:F] * factor
    saves[0].wait()


def whole(shape, dtype):
    return jax.ShapeDtypeStruct(shape, dtype)


def params(**kw):
    return pltpu.CompilerParams(vmem_limit_bytes=VMEM_LIMIT, **kw)


def per_device(inputs, level_ids, level_table, w_embed, queries, w_kv, w_out, gain, w_qkv, w_proj, d_latent):
    bands = lax.axis_size("lev")
    tiles = lax.axis_size("tile")
    lon_rows, lat_rows = d_latent.shape[:2]
    vmem = pl.BlockSpec(memory_space=pltpu.VMEM)
    anywhere = pl.BlockSpec(memory_space=pl.ANY)
    d_nat = d_latent.transpose(0, 2, 1, 3)
    latent, terms, w2, woutp, far, we = pl.pallas_call(
        pool_kernel,
        in_specs=[pl.BlockSpec(memory_space=pltpu.SMEM), vmem, anywhere, vmem, vmem, vmem, anywhere, anywhere],
        out_specs=(vmem,) * 6,
        out_shape=(whole(d_nat.shape, BF), whole((TERMS, KX), BF), whole((MV, 2 * KX), BF), whole((D, D), BF), whole((LEVELS, F, 512), BF), whole((KX, D), BF)),
        scratch_shapes=[
            pltpu.VMEM((LEVELS, D, 128), F32),
            pltpu.VMEM((D, 384), F32),
            pltpu.VMEM((D, 384), BF),
            pltpu.VMEM((MV, 4 * LEVELS * 128), BF),
            pltpu.VMEM((KX, 4 * LEVELS * 128), BF),
            pltpu.VMEM((MV, KX), F32),
            pltpu.VMEM((4 * D, 128), F32),
            pltpu.VMEM((F * 32, 128), F32),
            pltpu.VMEM((4 * F, 1024), BF),
            pltpu.VMEM((4 * F, 1024), BF),
            pltpu.VMEM((4, LEVELS, F, 128), BF),
            pltpu.VMEM((LEVELS, F, 256), BF),
            pltpu.VMEM((2, LEVELS, F, 128), BF),
            pltpu.VMEM((4, LEVELS, F, 128), BF),
            pltpu.VMEM((LEVELS, F, 512), BF),
            pltpu.VMEM(d_nat.shape, BF),
            pltpu.VMEM((D, 2 * D), BF),
            pltpu.VMEM((D, D), BF),
            pltpu.SemaphoreType.DMA((3,)),
            pltpu.SemaphoreType.DMA((58,)),
            pltpu.SemaphoreType.DMA((58,)),
        ],
        compiler_params=params(collective_id=2, has_side_effects=True),
        name="pool",
    )(level_ids, inputs[0], d_nat, level_table, w_embed, queries, w_kv, w_out)

    factor = 1.0 / math.sqrt(lon_rows * lat_rows * bands * tiles)
    done, total = pl.pallas_call(
        window_kernel,
        in_specs=[vmem, vmem, anywhere, vmem, vmem, vmem, anywhere, anywhere],
        out_specs=(vmem, vmem),
        out_shape=(whole(d_nat.shape, BF), whole((2, 8, CHUNK, KX), BF)),
        scratch_shapes=[
            pltpu.VMEM((LEVELS, D, 128), F32),
            pltpu.VMEM((D, 384), BF),
            pltpu.VMEM((4, 384, D), BF),
            pltpu.VMEM((15, 192, 2 * D), BF),
            pltpu.VMEM((384, D), BF),
            pltpu.VMEM((2, 384, 384), BF),
            pltpu.VMEM((8, CHUNK, KX), BF),
            pltpu.VMEM((8, CHUNK, KX), BF),
            pltpu.VMEM((7, CHUNK, KX), BF),
            pltpu.VMEM((8, CHUNK, KX), BF),
            pltpu.VMEM((2, 8, CHUNK, KX), BF),
            pltpu.VMEM(d_nat.shape, BF),
            pltpu.VMEM((D, 3 * D), BF),
            pltpu.VMEM((D, D), BF),
            pltpu.SemaphoreType.DMA((3,)),
            pltpu.SemaphoreType.DMA((46,)),
            pltpu.SemaphoreType.DMA((46,)),
        ],
        compiler_params=params(collective_id=1, has_side_effects=True),
        name="windows",
    )(terms.reshape(2, 8, CHUNK, KX), far, latent, w2, woutp, gain.reshape(1, D), w_qkv, w_proj)

    out, gembed, gkv, gout = pl.pallas_call(
        functools.partial(finish_kernel, factor=factor),
        in_specs=[vmem] * 5,
        out_specs=(anywhere, vmem, vmem, vmem),
        out_shape=(whole(d_nat.shape, BF), whole((F, D), F32), whole((D, 2 * D), F32), whole((D, D), F32)),
        scratch_shapes=[pltpu.SemaphoreType.DMA((1,))],
        compiler_params=params(),
        name="finish",
    )(done, total.reshape(TERMS, KX), we, queries, w_kv)
    return (out.transpose(0, 2, 1, 3), gembed, gkv, gout)


def solution(mesh):
    placed = (P("lev", None, "tile", None),) + (P(),) * 9 + (P("tile", "lev", None, None),)
    return jax.shard_map(
        per_device,
        mesh=mesh,
        in_specs=placed,
        out_specs=(P("tile", "lev", None, None), P(), P(), P()),
        check_vma=False,
    )
```

```python
import functools
import math

import jax
import jax.numpy as jnp
import numpy as np
from jax import lax
from jax.experimental import pallas as pl
from jax.experimental.pallas import tpu as pltpu
from jax.sharding import PartitionSpec as P

HD = 64
HEADS = 8
WIN = 8
D = 512
F = 80
LEVELS = 8
LATENT = 3
KX = 128
MV = 544
CHUNK = 176
UNROLL = 4
TERMS = 16 * CHUNK
BF = jnp.bfloat16
F32 = jnp.float32
VMEM_LIMIT = 56 * 1024 * 1024


def dot(a, b, ca=1, cb=0):
    return lax.dot_general(a, b, (((ca,), (cb,)), ((), ())), preferred_element_type=F32)


def split(value):
    high = value.astype(BF)
    return high, (value - high.astype(F32)).astype(BF)


def place(lev, tile):
    return {"lev": lev, "tile": tile}


def remote(src, dst, send, recv, device):
    return pltpu.make_async_remote_copy(src_ref=src, dst_ref=dst, send_sem=send, recv_sem=recv, device_id=device, device_id_type=pl.DeviceIdType.MESH)


def fetch(pairs, sems):
    loads = [pltpu.make_async_copy(src, dst, sems.at[i]) for i, (src, dst) in enumerate(pairs)]
    for load in loads:
        load.start()
    return loads


def query_rows(queries):
    rows = jnp.concatenate([jnp.broadcast_to(queries[q : q + 1], (HEADS, D)) for q in range(LATENT)], axis=0)
    head = lax.broadcasted_iota(jnp.int32, (LATENT * HEADS, D), 0) % HEADS
    lane = lax.broadcasted_iota(jnp.int32, (LATENT * HEADS, D), 1) // HD
    return jnp.where(head == lane, rows, 0.0)


def fold_weights(ids_ref, table_ref, embed_ref, queries_ref, wkv_ref, wout_ref, w2_ref, woutp_ref, we_ref):
    slab = lax.broadcasted_iota(jnp.int32, (16, 1), 0)
    wanted = jnp.full((16, 1), -1, jnp.int32)
    for l in range(LEVELS):
        wanted = jnp.where(slab == l, ids_ref[l], wanted)
    rows = jnp.zeros((16, D), F32)
    for entry in range(table_ref.shape[0]):
        rows = jnp.where(wanted == entry, table_ref[entry : entry + 1, :].astype(F32), rows)
    we_ref[0:F, :] = embed_ref[...]
    we_ref[F : F + 16, :] = rows.astype(BF)
    we_ref[F + 16 :, :] = jnp.zeros((KX - F - 16, D), BF)
    row = lax.broadcasted_iota(jnp.int32, (D, 1), 0)
    lane = lax.broadcasted_iota(jnp.int32, (D, D), 1)
    mix = jnp.where(lane == (row % HEADS) * HD + row // HEADS, 1.0, 0.0).astype(BF)
    we = we_ref[...]
    wv = dot(mix, wkv_ref[:, D:], 1, 1).astype(BF)
    woutp_ref[...] = dot(mix, wout_ref[...]).astype(BF)
    high, low = split(dot(wv, we, 1, 1))
    w2_ref[0:D, 0:KX] = high
    w2_ref[0:D, KX:] = low
    qm = query_rows(queries_ref[...].astype(F32)).astype(BF)
    shigh, slow = split(dot(qm, wkv_ref[:, :D], 1, 1) * (1.0 / math.sqrt(HD)))
    score = dot(shigh, we, 1, 1) + dot(slow, we, 1, 1)
    score = jnp.concatenate([score, jnp.zeros((MV - D - 24, KX), F32)], axis=0)
    high, low = split(score)
    w2_ref[D:MV, 0:KX] = high
    w2_ref[D:MV, KX:] = low


def level_rows(x, level):
    row = lax.broadcasted_iota(jnp.int32, (KX - F, 128), 0)
    ones = jnp.where(row == level, 1.0, 0.0).astype(BF)
    return jnp.concatenate([x, ones], axis=0)


def forward_levels(read, w2_ref, vals_ref):
    scores = []
    pairs = []
    for pair in range(LEVELS // 2):
        pixels = jnp.concatenate([level_rows(read(2 * pair), 2 * pair), level_rows(read(2 * pair + 1), 2 * pair + 1)], axis=1)
        pairs.append(pixels)
        out = dot(w2_ref[...], jnp.concatenate([pixels, pixels], axis=0))
        vals_ref[2 * pair] = out[:D, :128]
        vals_ref[2 * pair + 1] = out[:D, 128:]
        scores.append(out[D : D + 24, :128])
        scores.append(out[D : D + 24, 128:])
    expo = [jnp.exp(s) for s in scores]
    total = expo[0]
    for e in expo[1:]:
        total = total + e
    inverse = 1.0 / total
    return pairs, [(e * inverse).astype(BF).astype(F32) for e in expo]


def select(rows, lanes, want):
    row = lax.broadcasted_iota(jnp.int32, (rows, lanes), 0)
    return jnp.where(row == want, 1.0, 0.0).astype(BF)


def lane_ids(lanes, start=0):
    return lax.broadcasted_iota(jnp.int32, (1, lanes), 1) + start


def inside_row(lon, lat):
    return jnp.where((lat >= 0) & (lat < 128), lon * 128 + lat, -1)


def exchange_stages(x_ref, pixels_ref, xa_ref, xb_ref, own_ref, near_ref, side_ref, mine_ref, rim_ref, send_sem, recv_sem):
    lev, tile = lax.axis_index("lev"), lax.axis_index("tile")
    bands, tiles = lax.axis_size("lev"), lax.axis_size("tile")
    next_tile, last_tile = lax.rem(tile + 1, tiles), lax.rem(tile + tiles - 1, tiles)
    levs = [lax.rem(lev + off, bands) for off in range(bands)]

    def copy(src, dst, slot, device):
        return remote(src, dst, send_sem.at[slot], recv_sem.at[slot], device)

    own, near, east, west = [], [], [], []
    for off in range(1, bands):
        own.append(lambda g, off=off: copy(own_ref.at[g, levs[off]], mine_ref.at[g, lev], 30 + g * 7 + off - 1, place(levs[off], tile)))
        near.append(copy(near_ref.at[levs[off]], rim_ref.at[lev, :, 256:512], off - 1, place(levs[off], tile)))
    for off in range(bands):
        east.append(copy(side_ref.at[0, levs[off]], rim_ref.at[lev, :, 0:128], 7 + off, place(levs[off], next_tile)))
        west.append(copy(side_ref.at[1, levs[off]], rim_ref.at[lev, :, 128:256], 15 + off, place(levs[off], last_tile)))

    def greet():
        barrier = pltpu.get_barrier_semaphore()
        for off in range(1, bands):
            pl.semaphore_signal(barrier, inc=1, device_id=place(levs[off], tile), device_id_type=pl.DeviceIdType.MESH)
        for off in range(bands):
            for side in (next_tile, last_tile):
                pl.semaphore_signal(barrier, inc=1, device_id=place(levs[off], side), device_id_type=pl.DeviceIdType.MESH)

    def send_own():
        pixels_ref[...] = x_ref[...].reshape(F * 32, 128).astype(F32)
        for lon in range(32):
            plane = pixels_ref[pl.ds(lon, F, stride=32), :].astype(BF)
            xa_ref[(lon // 8) * F : (lon // 8 + 1) * F, (lon % 8) * 128 : (lon % 8 + 1) * 128] = plane
            moved = (lon + 4) % 32
            xb_ref[(moved // 8) * F : (moved // 8 + 1) * F, (moved % 8) * 128 : (moved % 8 + 1) * 128] = plane
        rows = xa_ref[...]
        for two in range(bands // 2):
            j = lane_ids(256)
            want = ((j % 128) // 16) * 128 + 16 * (2 * two + j // 128) + j % 16
            out = dot(rows, select(1024, 256, want)).astype(BF)
            for c in range(4):
                for half in range(2):
                    own_ref[c, 2 * two + half] = out[c * F : (c + 1) * F, half * 128 : (half + 1) * 128]
        pl.semaphore_wait(pltpu.get_barrier_semaphore(), 3 * bands - 1)
        for g in range(4):
            for c in own:
                c(g).start()
        for g in range(4):
            mine_ref[g, lev] = own_ref[g, lev]

    def sort_rim():
        rows = xb_ref[...]
        for four in range(2):
            j = lane_ids(256)
            band = 4 * four + j // 64
            lat = 16 * band + j % 4 + jnp.where(j % 64 < 32, -4, 16)
            out = dot(rows, select(1024, 256, inside_row((j % 32) // 4, lat))).astype(BF)
            for b in range(4):
                lanes = slice(64 * b, 64 * b + 64)
                for c in range(2):
                    pair = [out[k * F : (k + 1) * F, lanes] for k in (2 * c, 2 * c + 1)]
                    near_ref[4 * four + b, :, c * 128 : (c + 1) * 128] = jnp.concatenate(pair, axis=1)
        rows = jnp.concatenate([xb_ref[0:F, 0:512], xb_ref[0:F, 512:1024]], axis=0)
        for two in range(bands // 2):
            j = lane_ids(256)
            k = j % 128
            thin = k % 16
            wide = k - 32
            lat = jnp.where(k < 16, 4 + thin % 4, jnp.where(k < 32, thin % 4, jnp.where(k < 64, 8 + wide % 8, jnp.where(k < 80, 16 + thin % 4, 20 + thin % 4))))
            lon = jnp.where((k >= 32) & (k < 64), wide // 8, thin // 4)
            lat = jnp.where(k < 96, 16 * (2 * two + j // 128) - 4 + lat, -1)
            out = dot(rows, select(512, 256, inside_row(lon, lat))).astype(BF)
            for side in range(2):
                for half in range(2):
                    side_ref[side, 2 * two + half] = out[side * F : (side + 1) * F, half * 128 : (half + 1) * 128]
        rim_ref[lev, :, 256:512] = near_ref[lev]

    def take_own(group):
        for c in own:
            c(group).wait_recv()

        @pl.when(group == 1)
        def _():
            for c in near + east + west:
                c.start()

    def take_rim():
        for c in near + east + west:
            c.wait_recv()
        for c in near + east + west + [c(g) for c in own for g in range(4)]:
            c.wait_send()

    return greet, send_own, sort_rim, take_own, take_rim


def pool_kernel(ids_ref, x_ref, d_ref, table_ref, embed_ref, queries_ref, wkv_ref, wout_ref, latent_ref, terms_ref, w2_ref, woutp_ref, far_ref, we_ref, vals_ref, dpool_ref, pooled_ref, dv_ref, seen_ref, tacc_ref, gacc_ref, pixels_ref, xa_ref, xb_ref, own_ref, near_ref, side_ref, mine_ref, rim_ref, d_vmem, wkv_vmem, wout_vmem, load_sem, send_sem, recv_sem):
    loads = fetch(((wkv_ref, wkv_vmem), (wout_ref, wout_vmem), (d_ref, d_vmem)), load_sem)
    greet, send_own, sort_rim, take_own, take_rim = exchange_stages(x_ref, pixels_ref, xa_ref, xb_ref, own_ref, near_ref, side_ref, mine_ref, rim_ref, send_sem, recv_sem)
    greet()
    send_own()
    sort_rim()
    loads[0].wait()
    loads[1].wait()
    fold_weights(ids_ref, table_ref, embed_ref, queries_ref, wkv_vmem, wout_vmem, w2_ref, woutp_ref, we_ref)
    gacc_ref[...] = jnp.zeros_like(gacc_ref)
    loads[2].wait()

    def group_loop(group, carry):
        take_own(group)
        pool_group(group, mine_ref, d_vmem, w2_ref, woutp_ref, latent_ref, vals_ref, dpool_ref, pooled_ref, dv_ref, seen_ref, gacc_ref)
        return carry

    lax.fori_loop(0, 4, group_loop, 0)
    tacc_ref[...] = dot(dv_ref[...], seen_ref[...], 1, 1)
    for h in range(HEADS):
        for j in range(4):
            terms_ref[j * D + h * HD : j * D + (h + 1) * HD, :] = gacc_ref[pl.ds(j * D + h, HD, stride=HEADS), :].astype(BF)
        terms_ref[4 * D + h * HD : 4 * D + (h + 1) * HD, :] = tacc_ref[pl.ds(h, HD, stride=HEADS), :].astype(BF)
    terms_ref[5 * D : 5 * D + MV - D, :] = tacc_ref[D:MV, :].astype(BF)
    terms_ref[5 * D + MV - D :, :] = jnp.zeros((TERMS - 5 * D - MV + D, KX), BF)
    take_rim()
    far_ref[...] = rim_ref[...]


def pool_group(group, x_ref, d_ref, w2_ref, woutp_ref, latent_ref, vals_ref, dpool_ref, pooled_ref, dv_ref, seen_ref, gacc_ref):
    column = pl.multiple_of(group * (LEVELS * 128), 128)
    pairs, probs = forward_levels(lambda l: x_ref[group, l], w2_ref, vals_ref)
    d_rows = jnp.concatenate([d_ref[pl.ds(8 * group, 8), q].reshape(128, D) for q in range(LATENT)], axis=0)
    dpool_ref[...] = dot(woutp_ref[...], d_rows, 1, 1)
    parts = [[probs[l][q * HEADS : (q + 1) * HEADS] for q in range(LATENT)] for l in range(LEVELS)]

    def mix_loop(i, carry):
        base = pl.multiple_of(i * 16, 16)
        pooled = [[], [], []]
        dvals = [[] for _ in range(LEVELS)]
        for e in range(2):
            rows = pl.ds(base + 8 * e, 8)
            dq = [dpool_ref[rows, q * 128 : (q + 1) * 128] for q in range(LATENT)]
            acc = [None] * LATENT
            for l in range(LEVELS):
                v = vals_ref[l, rows, :]
                for q in range(LATENT):
                    term = parts[l][q] * v
                    acc[q] = term if acc[q] is None else acc[q] + term
                dvals[l].append(parts[l][0] * dq[0] + parts[l][1] * dq[1] + parts[l][2] * dq[2])
            for q in range(LATENT):
                pooled[q].append(acc[q])
        for q in range(LATENT):
            pooled_ref[pl.ds(base, 16), q * 128 : (q + 1) * 128] = jnp.concatenate(pooled[q], axis=0).astype(BF)
        for l in range(LEVELS):
            dv_ref[pl.ds(base, 16), pl.ds(column + l * 128, 128)] = jnp.concatenate(dvals[l], axis=0).astype(BF)
        return carry

    lax.fori_loop(0, D // 16, mix_loop, 0, unroll=UNROLL)

    def dprob_loop(i, carry):
        acc = list(carry)
        for e in range(2):
            rows = pl.ds(pl.multiple_of(i * 16 + 8 * e, 8), 8)
            dq = [dpool_ref[rows, q * 128 : (q + 1) * 128] for q in range(LATENT)]
            for l in range(LEVELS):
                v = vals_ref[l, rows, :]
                for q in range(LATENT):
                    acc[l * LATENT + q] = acc[l * LATENT + q] + dq[q] * v
        return tuple(acc)

    zero = jnp.zeros((HEADS, 128), F32)
    dprob = lax.fori_loop(0, D // 16, dprob_loop, (zero,) * (LEVELS * LATENT), unroll=UNROLL)
    scale = 1.0 / math.sqrt(HD)
    delta = []
    for q in range(LATENT):
        total = parts[0][q] * dprob[q]
        for l in range(1, LEVELS):
            total = total + parts[l][q] * dprob[l * LATENT + q]
        delta.append(total)
    for l in range(LEVELS):
        ds = [parts[l][q] * (dprob[l * LATENT + q] - delta[q]) * scale for q in range(LATENT)]
        dv_ref[D:MV, pl.ds(column + l * 128, 128)] = jnp.concatenate(ds + [zero], axis=0).astype(BF)

    for pair in range(LEVELS // 2):
        seen_ref[:, pl.ds(column + pair * 256, 256)] = pairs[pair]
    pooled = pooled_ref[...]
    gterm = dot(pooled, d_rows)
    for j in range(4):
        gacc_ref[j * D : (j + 1) * D, :] += gterm[:, j * 128 : (j + 1) * 128]
    latent = dot(pooled, woutp_ref[...], 0, 0).astype(BF)
    for q in range(LATENT):
        latent_ref[pl.ds(8 * group, 8), q] = latent[q * 128 : (q + 1) * 128].reshape(8, 16, D)


def normalise(values, gain):
    mean = jnp.mean(values, axis=-1, keepdims=True)
    centred = values - mean
    var = jnp.mean(centred * centred, axis=-1, keepdims=True)
    return (centred * lax.rsqrt(var + 1e-05) * gain).astype(BF)


def permutation(dim):
    dst = lax.broadcasted_iota(jnp.int32, (384, 1) if dim == 0 else (1, 384), dim)
    src = lax.broadcasted_iota(jnp.int32, (384, 384), 1 - dim)
    mid, high = dst - 96, dst - 288
    low = (dst // 4) * 16 + dst % 4
    mid = (mid // 8) * 16 + 4 + mid % 8
    high = (high // 4) * 16 + 12 + high % 4
    want = jnp.where(dst < 96, low, jnp.where(dst < 288, mid, high))
    return jnp.where(src == want, 1.0, 0.0).astype(BF)


def sum_stages(terms_ref, halves_ref, pair_ref, part_ref, band_ref, full_ref, send_sem, recv_sem):
    lev, tile = lax.axis_index("lev"), lax.axis_index("tile")
    bands, tiles = lax.axis_size("lev"), lax.axis_size("tile")
    groups = tiles // 2
    group, core = tile // 2, lax.rem(tile, 2)

    def copy(src, dst, slot, device):
        return remote(src, dst, send_sem.at[slot], recv_sem.at[slot], device)

    other = place(lev, 2 * group + 1 - core)
    lev_peers = [place(lax.rem(lev + off, bands), tile) for off in range(1, bands)]
    group_ids = [lax.rem(group + off, groups) for off in range(1, groups)]
    group_peers = [place(lev, 2 * g + core) for g in group_ids]
    swap = copy(terms_ref.at[1 - core], halves_ref, 0, other)
    first = [copy(pair_ref.at[g], part_ref.at[i], 1 + i, group_peers[i]) for i, g in enumerate(group_ids)]
    second = [copy(band_ref.at[lev], band_ref.at[lev], 8 + i, peer) for i, peer in enumerate(lev_peers)]
    third = [copy(full_ref.at[core, group], full_ref.at[core, group], 15 + i, peer) for i, peer in enumerate(group_peers)]
    back = copy(full_ref.at[core], full_ref.at[core], 22, other)

    def greet():
        barrier = pltpu.get_barrier_semaphore()
        for peer in group_peers + lev_peers + [other]:
            pl.semaphore_signal(barrier, inc=1, device_id=peer, device_id_type=pl.DeviceIdType.MESH)
        pl.semaphore_wait(barrier, groups + bands - 1)
        swap.start()

    def over_group():
        swap.wait_recv()
        pair_ref[...] = (terms_ref[core].astype(F32) + halves_ref[...].astype(F32)).astype(BF)
        for c in first:
            c.start()

    def over_lev():
        total = pair_ref[group].astype(F32)
        for i, c in enumerate(first):
            c.wait_recv()
            total = total + part_ref[i].astype(F32)
        band_ref[lev] = total.astype(BF)
        for c in second:
            c.start()

    def gather():
        for c in second:
            c.wait_recv()
        total = band_ref[0].astype(F32)
        for b in range(1, bands):
            total = total + band_ref[b].astype(F32)
        full_ref[core, group] = total.astype(BF)
        for c in third:
            c.start()

    def swap_back():
        for c in third:
            c.wait_recv()
        back.start()

    def close(total_ref):
        back.wait_recv()
        total_ref[...] = full_ref[...]
        for c in [swap] + first + second + third + [back]:
            c.wait_send()

    return greet, over_group, over_lev, gather, swap_back, close


def window_kernel(terms_ref, xh_ref, latent_hbm, w2_ref, woutp_ref, gain_ref, wqkv_hbm, wproj_hbm, out_ref, total_ref, vals_ref, pooled_ref, q_ref, kv_ref, att_ref, perm_ref, halves_ref, pair_ref, part_ref, band_ref, full_ref, latent_ref, wqkv_ref, wproj_ref, load_sem, send_sem, recv_sem):
    loads = fetch(((wqkv_hbm, wqkv_ref), (latent_hbm, latent_ref), (wproj_hbm, wproj_ref)), load_sem)
    gain = gain_ref[...]
    greet, over_group, over_lev, gather, swap_back, close = sum_stages(terms_ref, halves_ref, pair_ref, part_ref, band_ref, full_ref, send_sem, recv_sem)
    greet()
    perm_ref[0] = permutation(0)
    perm_ref[1] = permutation(1)
    loads[0].wait()

    def halo(group, carry):
        lane0 = pl.multiple_of(group * 128, 128)
        _, probs = forward_levels(lambda l: xh_ref[l, :, pl.ds(lane0, 128)], w2_ref, vals_ref)
        parts = [[probs[l][q * HEADS : (q + 1) * HEADS] for q in range(LATENT)] for l in range(LEVELS)]

        def mix_loop(i, inner):
            base = pl.multiple_of(i * 16, 16)
            pooled = [[], [], []]
            for e in range(2):
                rows = pl.ds(base + 8 * e, 8)
                acc = [None] * LATENT
                for l in range(LEVELS):
                    v = vals_ref[l, rows, :]
                    for q in range(LATENT):
                        term = parts[l][q] * v
                        acc[q] = term if acc[q] is None else acc[q] + term
                for q in range(LATENT):
                    pooled[q].append(acc[q])
            for q in range(LATENT):
                pooled_ref[pl.ds(base, 16), q * 128 : (q + 1) * 128] = jnp.concatenate(pooled[q], axis=0).astype(BF)
            return inner

        lax.fori_loop(0, D // 16, mix_loop, 0, unroll=UNROLL)
        latent = dot(pooled_ref[...], woutp_ref[...], 0, 0).astype(BF).astype(F32)
        normed = normalise(latent, gain)
        kv = dot(normed, wqkv_ref[:, D:]).astype(BF)

        @pl.when(group < 2)
        def _():
            first = group * 3
            for q in range(LATENT):
                row = q * 128
                kv_ref[first, 48 + 32 * q : 80 + 32 * q, :] = kv[row : row + 32]
                kv_ref[first + 1, 96 + 32 * q : 128 + 32 * q, :] = kv[row + 32 : row + 64]
                kv_ref[first + 2, 48 + 32 * q : 80 + 32 * q, :] = kv[row + 64 : row + 96]

        @pl.when(group == 2)
        def _():
            for q in range(LATENT):
                row = q * 128
                near = slice(144 + 16 * q, 160 + 16 * q)
                kv_ref[3, near, :] = kv[row : row + 16]
                kv_ref[0, near, :] = kv[row + 16 : row + 32]
                kv_ref[5, near, :] = kv[row + 32 : row + 48]
                kv_ref[2, near, :] = kv[row + 48 : row + 64]

        def column_rim(half, column):
            for q in range(LATENT):
                row = q * 128 + half * 64
                near = slice(96 + 32 * q, 128 + 32 * q)
                kv_ref[3 + 3 * column, near, :] = kv[row : row + 32]
                kv_ref[5 + 3 * column, near, :] = kv[row + 32 : row + 64]

        @pl.when(group == 2)
        def _():
            column_rim(1, 1)

        @pl.when(group == 3)
        def _():
            column_rim(0, 2)
            column_rim(1, 3)

        @pl.when(group == 0)
        def _():
            over_group()
        return carry

    lax.fori_loop(0, 4, halo, 0)
    over_lev()
    loads[1].wait()
    loads[2].wait()

    def project(rows, column):
        normed = normalise(rows.astype(F32), gain)
        normed = dot(perm_ref[0], normed).astype(BF)
        q_ref[column] = (dot(normed, wqkv_ref[:, :D]).astype(BF).astype(F32) * (1.0 / math.sqrt(HD))).astype(BF)
        return dot(normed, wqkv_ref[:, D:]).astype(BF)

    rows = jnp.concatenate([latent_ref[28:32].reshape(192, D), latent_ref[0:4].reshape(192, D)], axis=0)
    kv = project(rows, 0)
    for side in range(2):
        first = 3 * (1 - side)
        kv_ref[first, 0:48, :] = kv[48 * side : 48 * side + 48]
        kv_ref[first + 1, 0:96, :] = kv[96 + 96 * side : 192 + 96 * side]
        kv_ref[first + 2, 0:48, :] = kv[288 + 48 * side : 336 + 48 * side]

    def own(column, carry):
        rows = latent_ref[pl.ds(8 * column - 4, 8)].reshape(384, D)
        kv = project(rows, column)
        first = 3 + 3 * column
        kv_ref[first, 0:96, :] = kv[0:96]
        kv_ref[first + 1, 0:192, :] = kv[96:288]
        kv_ref[first + 2, 0:96, :] = kv[288:384]
        return carry

    lax.fori_loop(1, 4, own, 0)
    gather()

    key = lax.broadcasted_iota(jnp.int32, (1, 192), 1)
    head_lane = lax.broadcasted_iota(jnp.int32, (1, 256), 1) // HD
    odd_lane = lax.broadcasted_iota(jnp.int32, (1, 128), 1) >= HD

    def attend(column, window, row0, count, valid):
        for quad in range(HEADS // 4):
            lanes = slice(quad * 256, quad * 256 + 256)
            q = q_ref[column, row0 : row0 + count, lanes]
            nil = jnp.zeros_like(q)
            q4 = jnp.concatenate([jnp.where(head_lane == h, q, nil) for h in range(4)], axis=0)
            expo = jnp.exp(dot(q4, kv_ref[window, :, lanes], 1, 1))
            if valid is not None:
                expo = jnp.where(valid, expo, 0.0)
            probs = (expo * (1.0 / jnp.sum(expo, axis=-1, keepdims=True))).astype(BF)
            both = dot(probs, kv_ref[window, :, D + quad * 256 : D + quad * 256 + 256])
            for two in range(2):
                part = both[2 * two * count : 2 * (two + 1) * count, two * 128 : (two + 1) * 128]
                spot = slice(quad * 256 + two * 128, quad * 256 + two * 128 + 128)
                att_ref[row0 : row0 + count, spot] = jnp.where(odd_lane, part[count:], part[:count]).astype(BF)

    lev = lax.axis_index("lev")
    inside = (lev > 0, lev < lax.axis_size("lev") - 1)
    plain = [(key < 96) | ok for ok in inside]
    corner = [(key < 48) | ((key < 144) & ((key + 16) % 32 < 16)) | ok for ok in inside]

    for side in range(2):
        first = 3 * (1 - side)
        attend(0, first, 48 * side, 48, corner[0])
        attend(0, first + 1, 96 + 96 * side, 96, None)
        attend(0, first + 2, 288 + 48 * side, 48, corner[1])

    def finish(rows):
        natural = dot(perm_ref[1], att_ref[...]).astype(BF)
        return (rows.astype(F32) + dot(natural, wproj_ref[...])).astype(BF)

    done = finish(rows)
    out_ref[28:32] = done[:192].reshape(4, 3, 16, D)
    out_ref[0:4] = done[192:].reshape(4, 3, 16, D)

    def column_loop(column, carry):
        first = 3 + 3 * column
        attend(column, first, 0, 96, plain[0])
        attend(column, first + 1, 96, 192, None)
        attend(column, first + 2, 288, 96, plain[1])
        rows = latent_ref[pl.ds(8 * column - 4, 8)].reshape(384, D)
        out_ref[pl.ds(8 * column - 4, 8)] = finish(rows).reshape(8, 3, 16, D)

        @pl.when(column == 2)
        def _():
            swap_back()

        return carry

    lax.fori_loop(1, 4, column_loop, 0)
    close(total_ref)


def finish_kernel(done_ref, total_ref, we_ref, queries_ref, wkv_ref, out_ref, gembed_ref, gkv_ref, gout_ref, save_sem, factor):
    saves = fetch([(done_ref, out_ref)], save_sem)
    for j in range(4):
        gout_ref[:, j * 128 : (j + 1) * 128] = total_ref[j * D : (j + 1) * D, :].astype(F32) * factor
    qm = query_rows(queries_ref[...].astype(F32)).astype(BF)
    values = total_ref[4 * D : 5 * D, :]
    keys = dot(qm, total_ref[5 * D : 5 * D + 32, :][:24], 0, 0)
    khigh, klow = split(keys)
    we = we_ref[...]
    gkv_ref[:, D:] = dot(we, values, 0, 1) * factor
    gkv_ref[:, :D] = (dot(we, khigh, 0, 1) + dot(we, klow, 0, 1)) * factor
    wk, wv = wkv_ref[:, :D], wkv_ref[:, D:]
    grad = dot(khigh, wk, 0, 1) + dot(klow, wk, 0, 1) + dot(values, wv, 0, 1)
    gembed_ref[...] = grad[:F] * factor
    saves[0].wait()


def whole(shape, dtype):
    return jax.ShapeDtypeStruct(shape, dtype)


def params(**kw):
    return pltpu.CompilerParams(vmem_limit_bytes=VMEM_LIMIT, **kw)


def per_device(inputs, level_ids, level_table, w_embed, queries, w_kv, w_out, gain, w_qkv, w_proj, d_latent):
    bands = lax.axis_size("lev")
    tiles = lax.axis_size("tile")
    lon_rows, lat_rows = d_latent.shape[:2]
    vmem = pl.BlockSpec(memory_space=pltpu.VMEM)
    anywhere = pl.BlockSpec(memory_space=pl.ANY)
    d_nat = d_latent.transpose(0, 2, 1, 3)
    latent, terms, w2, woutp, far, we = pl.pallas_call(
        pool_kernel,
        in_specs=[pl.BlockSpec(memory_space=pltpu.SMEM), vmem, anywhere, vmem, vmem, vmem, anywhere, anywhere],
        out_specs=(vmem,) * 6,
        out_shape=(whole(d_nat.shape, BF), whole((TERMS, KX), BF), whole((MV, 2 * KX), BF), whole((D, D), BF), whole((LEVELS, F, 512), BF), whole((KX, D), BF)),
        scratch_shapes=[
            pltpu.VMEM((LEVELS, D, 128), F32),
            pltpu.VMEM((D, 384), F32),
            pltpu.VMEM((D, 384), BF),
            pltpu.VMEM((MV, 4 * LEVELS * 128), BF),
            pltpu.VMEM((KX, 4 * LEVELS * 128), BF),
            pltpu.VMEM((MV, KX), F32),
            pltpu.VMEM((4 * D, 128), F32),
            pltpu.VMEM((F * 32, 128), F32),
            pltpu.VMEM((4 * F, 1024), BF),
            pltpu.VMEM((4 * F, 1024), BF),
            pltpu.VMEM((4, LEVELS, F, 128), BF),
            pltpu.VMEM((LEVELS, F, 256), BF),
            pltpu.VMEM((2, LEVELS, F, 128), BF),
            pltpu.VMEM((4, LEVELS, F, 128), BF),
            pltpu.VMEM((LEVELS, F, 512), BF),
            pltpu.VMEM(d_nat.shape, BF),
            pltpu.VMEM((D, 2 * D), BF),
            pltpu.VMEM((D, D), BF),
            pltpu.SemaphoreType.DMA((3,)),
            pltpu.SemaphoreType.DMA((58,)),
            pltpu.SemaphoreType.DMA((58,)),
        ],
        compiler_params=params(collective_id=2, has_side_effects=True),
        name="pool",
    )(level_ids, inputs[0], d_nat, level_table, w_embed, queries, w_kv, w_out)

    factor = 1.0 / math.sqrt(lon_rows * lat_rows * bands * tiles)
    done, total = pl.pallas_call(
        window_kernel,
        in_specs=[vmem, vmem, anywhere, vmem, vmem, vmem, anywhere, anywhere],
        out_specs=(vmem, vmem),
        out_shape=(whole(d_nat.shape, BF), whole((2, 8, CHUNK, KX), BF)),
        scratch_shapes=[
            pltpu.VMEM((LEVELS, D, 128), F32),
            pltpu.VMEM((D, 384), BF),
            pltpu.VMEM((4, 384, D), BF),
            pltpu.VMEM((15, 192, 2 * D), BF),
            pltpu.VMEM((384, D), BF),
            pltpu.VMEM((2, 384, 384), BF),
            pltpu.VMEM((8, CHUNK, KX), BF),
            pltpu.VMEM((8, CHUNK, KX), BF),
            pltpu.VMEM((7, CHUNK, KX), BF),
            pltpu.VMEM((8, CHUNK, KX), BF),
            pltpu.VMEM((2, 8, CHUNK, KX), BF),
            pltpu.VMEM(d_nat.shape, BF),
            pltpu.VMEM((D, 3 * D), BF),
            pltpu.VMEM((D, D), BF),
            pltpu.SemaphoreType.DMA((3,)),
            pltpu.SemaphoreType.DMA((23,)),
            pltpu.SemaphoreType.DMA((23,)),
        ],
        compiler_params=params(collective_id=1, has_side_effects=True),
        name="windows",
    )(terms.reshape(2, 8, CHUNK, KX), far, latent, w2, woutp, gain.reshape(1, D), w_qkv, w_proj)

    out, gembed, gkv, gout = pl.pallas_call(
        functools.partial(finish_kernel, factor=factor),
        in_specs=[vmem] * 5,
        out_specs=(anywhere, vmem, vmem, vmem),
        out_shape=(whole(d_nat.shape, BF), whole((F, D), F32), whole((D, 2 * D), F32), whole((D, D), F32)),
        scratch_shapes=[pltpu.SemaphoreType.DMA((1,))],
        compiler_params=params(),
        name="finish",
    )(done, total.reshape(TERMS, KX), we, queries, w_kv)
    return (out.transpose(0, 2, 1, 3), gembed, gkv, gout)


def solution(mesh):
    placed = (P("lev", None, "tile", None),) + (P(),) * 9 + (P("tile", "lev", None, None),)
    return jax.shard_map(
        per_device,
        mesh=mesh,
        in_specs=placed,
        out_specs=(P("tile", "lev", None, None), P(), P(), P()),
        check_vma=False,
    )
```
